32 devices in a mesh: dp: 4 (over x, core), blk: 8 (over z, y).
Axes of the slice: x: 2, y: 2, z: 4, core: 2. Of those that a mesh axis runs over, the one named last changes fastest.
Arguments:
- patches: bfloat16 [8192, 768], P(('dp', 'blk')), may hold values from -6 to 6
- segment_ids: int32 [8192], P('dp'), may hold values from 0 to 11, as said below
- sensor_tags: int32 [8192], P('dp'), may hold values from 0 to 3
- seq_starts: int32 [8192], P(('dp', 'blk')), may hold values from 0 to 8191, as said below
- ln1_gain: float32 [768], replicated, may hold values from 0.5 to 1.5
- ln1_bias: float32 [768], replicated, may hold values from -4 to 4
- w_qkv: bfloat16 [768, 2304], replicated, may hold values from -0.21875 to 0.21875
- w_out: bfloat16 [768, 768], replicated, may hold values from -0.875 to 0.875
- b_out: float32 [768], replicated, may hold values from -4 to 4
- ln2_gain: float32 [768], replicated, may hold values from 0.5 to 1.5
- ln2_bias: float32 [768], replicated, may hold values from -4 to 4
- w_up: bfloat16 [768, 3072], replicated, may hold values from -0.21875 to 0.21875
- b_up: float32 [3072], replicated, may hold values from -6 to 6
- w_down: bfloat16 [3072, 768], replicated, may hold values from -0.109375 to 0.109375
- b_down: float32 [768], replicated, may hold values from -4 to 4
- cotangent: bfloat16 [8192, 768], P(('dp', 'blk')), may hold values from -6 to 6
Outputs:
- mixed_out: bfloat16 [8192, 768], P(('dp', 'blk'))
- grad_patches: float32 [8192, 768], P(('dp', 'blk'))
- grad_ln1_gain: float32 [768], P('blk')
- grad_ln1_bias: float32 [768], P('blk')
- grad_w_qkv: float32 [768, 2304], P('blk')
- grad_w_out: float32 [768, 768], P('blk')
- grad_b_out: float32 [768], P('blk')
- grad_ln2_gain: float32 [768], P('blk')
- grad_ln2_bias: float32 [768], P('blk')
- grad_w_up: float32 [768, 3072], P('blk')
- grad_b_up: float32 [3072], P('blk')
- grad_w_down: float32 [3072, 768], P('blk')
- grad_b_down: float32 [768], P('blk')
The draws below stay inside these ranges and needn't reach their ends.
Inputs may be any that keep to these rules, and one draw needn't show every extreme that they name: `segment_ids`: Non-decreasing within each group of 2048 tokens; no two groups share a number; each group holds three sequences, and one of them begins among the group's first 256 tokens and ends among its last 256. `seq_starts`: A global token index inside the token's own sequence, at or before the token itself; the last token of each group starts at itself.
All inputs are finite; a program needn't handle non-finite values.
Results may differ from the reference program's by a relative error of at most 0.02.
Values may be sent and summed in bfloat16 or wider, within the bound.
No kernel may reach another device: no remote copies, remote signals or barrier semaphores. Data moves between devices by JAX's collectives and lax.ppermute only.
A program may use at most 192 MiB of HBM per device.

```python
import jax
import jax.numpy as jnp
from jax import lax

D = 768
HEADS = 12
HEAD_DIM = 64
FF = 3072
TOK_DEV = 256
GROUP_TOK = 2048
TOKENS = 8192
N_DP = 4
N_BLK = 8


def group_bounds(key):
    first_key, last_key = jax.random.split(key)
    seq_first = jax.random.randint(first_key, (N_DP, 1), 1, TOK_DEV)
    seq_last = jax.random.randint(last_key, (N_DP, 1), GROUP_TOK - TOK_DEV + 1, GROUP_TOK)
    positions = jnp.arange(GROUP_TOK, dtype=jnp.int32)[None, :]
    return (seq_first.astype(jnp.int32), seq_last.astype(jnp.int32), positions)


def draw_segment_ids(key, part):
    seq_first, seq_last, positions = group_bounds(key)
    inside = (positions >= seq_first).astype(jnp.int32) + (positions >= seq_last).astype(jnp.int32)
    group_base = 3 * jnp.arange(N_DP, dtype=jnp.int32)[:, None]
    return (inside + group_base).reshape(-1)


def draw_seq_starts(key, part):
    seq_first, seq_last, positions = group_bounds(key)
    key = jax.random.fold_in(key, 23)
    seq_begin = jnp.where(positions >= seq_last, seq_last, jnp.where(positions >= seq_first, seq_first, 0))
    inside_pos = positions - seq_begin
    shape_full = (N_DP, GROUP_TOK)
    offsets = jax.random.randint(key, shape_full, 0, jnp.broadcast_to(inside_pos // 4 + 1, shape_full))
    offsets = jnp.where(jnp.broadcast_to(positions == GROUP_TOK - 1, shape_full), jnp.broadcast_to(inside_pos, shape_full), offsets)
    group_base = GROUP_TOK * jnp.arange(N_DP, dtype=jnp.int32)[:, None]
    return (seq_begin + offsets + group_base).astype(jnp.int32).reshape(-1)


def set_ends(values, own_key, smallest, top_value):
    dims = values.shape
    place = [jax.random.randint(jax.random.fold_in(own_key, axis), (), 0, dims[axis]) for axis in range(len(dims))]
    values = values.at[tuple(place)].set(smallest)
    longest = dims.index(max(dims))
    place[longest] = (place[longest] + 1) % dims[longest]
    return values.at[tuple(place)].set(top_value)


def level_of(stream_key, dims, shards, low, high):
    level = 1.0
    for position, parts in shards:
        draws = jax.random.uniform(jax.random.fold_in(jax.random.fold_in(stream_key, 6), position), (parts,), jnp.float32, low / len(shards), high / len(shards))
        level = level * jnp.repeat(jnp.exp(draws), dims[position] // parts).reshape((-1,) + (1,) * (len(dims) - 1 - position))
    return level


def centred(rng, extent, deviation, most, cuts=(), held_as=jnp.bfloat16):
    level = level_of(rng, extent, cuts, -0.22, 0.18) if cuts else 1.0
    array = jax.random.normal(rng, extent, jnp.float32) * deviation * level
    return jnp.minimum(jnp.maximum(array, -most), most).astype(held_as)


def setup_inputs(seed: int = 0) -> dict:
    arg_keys = jax.random.split(jax.random.key(seed), 17)
    return {
        "patches": centred(arg_keys[0], (TOKENS, D), 1.0, 6.0, ((0, 32),)),
        "segment_ids": draw_segment_ids(jax.random.fold_in(arg_keys[16], 71), 0),
        "sensor_tags": set_ends(jax.random.randint(arg_keys[2], (TOKENS,), 0, 4), jax.random.fold_in(arg_keys[2], 1), 0, 3).astype(jnp.int32),
        "seq_starts": draw_seq_starts(jax.random.fold_in(arg_keys[16], 71), 0),
        "ln1_gain": jnp.clip(1.0 + 0.1 * jax.random.normal(arg_keys[4], (D,), jnp.float32), 0.5, 1.5),
        "ln1_bias": centred(arg_keys[5], (D,), 0.3, 4.0, (), jnp.float32),
        "w_qkv": centred(arg_keys[6], (D, 3 * D), D ** -0.5, 0.21875),
        "w_out": centred(arg_keys[7], (D, D), (D // 16) ** -0.5, 0.875),
        "b_out": centred(arg_keys[8], (D,), 0.3, 4.0, (), jnp.float32),
        "ln2_gain": jnp.clip(1.0 + 0.1 * jax.random.normal(arg_keys[9], (D,), jnp.float32), 0.5, 1.5),
        "ln2_bias": centred(arg_keys[10], (D,), 0.3, 4.0, (), jnp.float32),
        "w_up": centred(arg_keys[11], (D, FF), D ** -0.5, 0.21875),
        "b_up": centred(arg_keys[12], (FF,), 0.5, 6.0, (), jnp.float32),
        "w_down": centred(arg_keys[13], (FF, D), FF ** -0.5, 0.109375),
        "b_down": centred(arg_keys[14], (D,), 0.3, 4.0, (), jnp.float32),
        "cotangent": centred(arg_keys[15], (TOKENS, D), 1.0, 6.0, ((0, 32),)),
    }


@jax.custom_vjp
def low(v):
    return lax.optimization_barrier(v.astype(jnp.bfloat16)).astype(jnp.float32)

@jax.custom_vjp
def low_back(v):
    return v

def low_keep(v):
    return (low(v), None)

def low_pass(kept, grad):
    return (grad,)

def back_keep(v):
    return (v, None)

def back_low(kept, grad):
    return (low(grad),)
low.defvjp(low_keep, low_pass)
low_back.defvjp(back_keep, back_low)
EPSILON = 1e-06
MASKED = -1e+30

def layer_norm(values, gain, bias_vec):
    center_vals = values - lax.optimization_barrier(jnp.mean(values, axis=-1, keepdims=True))
    variance = lax.optimization_barrier(jnp.mean(center_vals * center_vals, axis=-1, keepdims=True))
    return center_vals * lax.rsqrt(variance + EPSILON) * gain + bias_vec

def block_attention(queries, key_rows, value_rows, query_seg, query_tag, query_from, key_seg, key_tag, key_pos):
    q_heads = queries.reshape(TOK_DEV, HEADS, HEAD_DIM)
    k_heads = key_rows.reshape(GROUP_TOK, HEADS, HEAD_DIM)
    v_heads = value_rows.reshape(GROUP_TOK, HEADS, HEAD_DIM)
    scores = jnp.einsum('qhd,khd->hqk', q_heads, k_heads, precision=lax.Precision.HIGHEST) * HEAD_DIM ** (-0.5)
    scores = low_back(scores)
    same_seq = query_seg[:, None] == key_seg[None, :]
    after_start = key_pos[None, :] >= query_from[:, None]
    tag_match = (query_tag[:, None] == key_tag[None, :]) | (query_tag[:, None] == 0) | (key_tag[None, :] == 0)
    visible = same_seq & after_start & tag_match
    scores = jnp.where(visible[None], scores, MASKED)
    probs = low(jax.nn.softmax(scores, axis=-1))
    attended = jnp.einsum('hqk,khd->qhd', probs, v_heads, precision=lax.Precision.HIGHEST)
    return attended.reshape(TOK_DEV, D)

def attention(proj, segment_ids, sensor_tags, seq_starts):
    queries = proj[:, :D]
    key_rows = proj[:, D:2 * D]
    value_rows = proj[:, 2 * D:]
    block_fn = jax.checkpoint(block_attention)

    def one_block(block_num):
        group_num = block_num // N_BLK
        q_first = block_num * TOK_DEV
        k_first = group_num * GROUP_TOK
        q_blk = lax.dynamic_slice_in_dim(queries, q_first, TOK_DEV)
        k_blk = lax.dynamic_slice_in_dim(key_rows, k_first, GROUP_TOK)
        v_blk = lax.dynamic_slice_in_dim(value_rows, k_first, GROUP_TOK)
        q_seg = lax.dynamic_slice_in_dim(segment_ids, q_first, TOK_DEV)
        q_tag = lax.dynamic_slice_in_dim(sensor_tags, q_first, TOK_DEV)
        q_from = lax.dynamic_slice_in_dim(seq_starts, q_first, TOK_DEV)
        k_seg = lax.dynamic_slice_in_dim(segment_ids, k_first, GROUP_TOK)
        k_tag = lax.dynamic_slice_in_dim(sensor_tags, k_first, GROUP_TOK)
        k_pos = k_first + jnp.arange(GROUP_TOK, dtype=jnp.int32)
        return block_fn(q_blk, k_blk, v_blk, q_seg, q_tag, q_from, k_seg, k_tag, k_pos)
    outputs = lax.map(one_block, jnp.arange(TOKENS // TOK_DEV, dtype=jnp.int32))
    return outputs.reshape(TOKENS, D)

def reference(patches, segment_ids, sensor_tags, seq_starts, ln1_gain, ln1_bias, w_qkv, w_out, b_out, ln2_gain, ln2_bias, w_up, b_up, w_down, b_down, cotangent):

    def forward(x_in, gain_one, bias_one, weight_qkv, weight_out, bias_out, gain_two, bias_two, weight_up, bias_up, weight_down, bias_down):
        normed_one = low(layer_norm(x_in, gain_one, bias_one))
        proj = low(low_back(jnp.dot(normed_one, weight_qkv, precision=lax.Precision.HIGHEST)))
        attended = low(low_back(attention(proj, segment_ids, sensor_tags, seq_starts)))
        branch = low_back(jnp.dot(attended, weight_out, precision=lax.Precision.HIGHEST) + bias_out)
        x_mid = x_in + branch
        normed_two = low(layer_norm(x_mid, gain_two, bias_two))
        pre_up = low_back(jnp.dot(normed_two, weight_up, precision=lax.Precision.HIGHEST) + bias_up)
        act = low(jax.nn.gelu(pre_up, approximate=False))
        return x_mid + jnp.dot(act, weight_down, precision=lax.Precision.HIGHEST) + bias_down
    primals = (patches.astype(jnp.float32), ln1_gain, ln1_bias, w_qkv.astype(jnp.float32), w_out.astype(jnp.float32), b_out, ln2_gain, ln2_bias, w_up.astype(jnp.float32), b_up, w_down.astype(jnp.float32), b_down)
    result, vjp_fn = jax.vjp(forward, *primals)
    grads = vjp_fn(cotangent.astype(jnp.float32))
    return (result.astype(jnp.bfloat16), grads[0], grads[1], grads[2], grads[3], grads[4], grads[5], grads[6], grads[7], grads[8], grads[9], grads[10], grads[11])
```

```python
import functools
from functools import partial

import jax
import jax.numpy as jnp
from jax import lax
from jax.experimental import pallas as pl
from jax.experimental.pallas import tpu as pltpu
from jax.sharding import PartitionSpec as P

HEADS = 12
EPSILON = 1e-06
MASKED = -1e30
AXES = ("dp", "blk")
NT = (((1,), (1,)), ((), ()))
TN = (((0,), (0,)), ((), ()))
NN = (((1,), (0,)), ((), ()))
VM = pl.BlockSpec(memory_space=pltpu.VMEM)
LOW = jnp.bfloat16
F32 = jnp.float32
MIB = 1 << 20


def dotf(a, b, dims=NN):
    return lax.dot_general(a, b, dims, preferred_element_type=F32)


def struct(shape, dtype):
    return jax.ShapeDtypeStruct(shape, dtype)


def norm_hat(x):
    center = x - jnp.mean(x, axis=-1, keepdims=True)
    inv = lax.rsqrt(jnp.mean(center * center, axis=-1, keepdims=True) + EPSILON)
    return center * inv, inv


def norm_back(hat, inv, gain, grad):
    g = grad * gain
    return inv * (g - jnp.mean(g, axis=-1, keepdims=True) - hat * jnp.mean(g * hat, axis=-1, keepdims=True))


def call(kernel, name, outs, args, flops, aliases=None, scratch=(), exps=0, vmem=32):
    moved = sum(a.size * a.dtype.itemsize for a in args) + sum(o.size * o.dtype.itemsize for o in outs)
    return pl.pallas_call(
        kernel,
        out_shape=outs,
        in_specs=[VM] * len(args),
        out_specs=tuple(VM for _ in outs),
        input_output_aliases=aliases or {},
        scratch_shapes=scratch,
        compiler_params=pltpu.CompilerParams(vmem_limit_bytes=vmem * MIB),
        cost_estimate=pl.CostEstimate(flops=int(flops), bytes_accessed=int(moved), transcendentals=int(exps)),
        name=name,
    )(*args)


def key_bias(chunk, seg_ref, tag_ref, from_ref):
    keys = seg_ref.shape[1]
    me = lax.axis_index("blk")
    base = lax.axis_index("dp") * (seg_ref.shape[0] * keys)

    def column(ref):
        return jnp.broadcast_to(ref[pl.ds(chunk, 1), :], (8, keys)).T[:, 0:1]

    kseg, ktag = column(seg_ref), column(tag_ref)
    qseg, qtag = seg_ref[pl.ds(me, 1), :], tag_ref[pl.ds(me, 1), :]
    pos = base + chunk * keys + lax.broadcasted_iota(jnp.int32, (keys, keys), 0)
    seen = (kseg == qseg) & (pos >= from_ref[...])
    tags = (ktag == qtag) | (qtag == 0) | (ktag == 0)
    return jnp.where(seen & tags, 0.0, MASKED)


def head_lanes(block, odd):
    lane = lax.broadcasted_iota(jnp.int32, block.shape, 1)
    return jnp.where((lane >= 64) if odd else (lane < 64), block, jnp.zeros_like(block))


def over_pairs(heads, loop, body):
    if loop:
        lax.fori_loop(0, heads // 2, lambda i, c: (body(i), c)[1], 0)
    else:
        for i in range(heads // 2):
            body(i)


def fwd_kernel(places, first, last, loop, *refs):
    n = len(places)
    seg_ref, tag_ref, from_ref, gain_ref, shift_ref, w_ref = refs[:6]
    tokens = refs[6 : 6 + n]
    refs = refs[6 + n :]
    if first:
        top_out, sum_out, acc_out, normed_out, kv_out, q_ref, bias = refs
    else:
        q_ref, top_in, sum_in, acc_in = refs[:4]
        top_out, sum_out, acc_out, normed_out, kv_out, bias = refs[4:]
    keys, width = tokens[0].shape
    for i in range(n):
        at = pl.ds(i * keys, keys)
        hat = norm_hat(tokens[i][...].astype(F32))[0]
        normed = (hat * gain_ref[...] + shift_ref[...]).astype(LOW)
        normed_out[at, :] = normed
        bias[i] = key_bias(places[i](), seg_ref, tag_ref, from_ref)
    normed = normed_out[...]
    if first:
        q_ref[...] = (dotf(normed, w_ref[:, :width]).astype(LOW) * jnp.asarray(0.125, LOW)).astype(LOW)
    for j in range(2):
        cols = pl.ds(j * width, width)
        kv_out[:, cols] = dotf(normed, w_ref[:, pl.ds((j + 1) * width, width)]).astype(LOW)

    def pair_body(pair):
        lanes = pl.multiple_of(pair * 128, 128)
        at, vat = pl.ds(lanes, 128), pl.ds(width + lanes, 128)
        q_pair = q_ref[:, at]
        v_t = [kv_out[pl.ds(i * keys, keys), vat].T for i in range(n)]
        for odd in range(2):
            h = pair * 2 + odd
            row = pl.ds(h, 1)
            rows = pl.ds(pl.multiple_of(h * 64, 64), 64)
            q_h = head_lanes(q_pair, odd)
            scores = [dotf(kv_out[pl.ds(i * keys, keys), at], q_h, NT) + bias[i] for i in range(n)]
            top = jnp.max(scores[0], axis=0, keepdims=True)
            for s in scores[1:]:
                top = jnp.maximum(top, jnp.max(s, axis=0, keepdims=True))
            if not first:
                old = top_in[row, :]
                top = jnp.maximum(top, old)
                fade = jnp.exp(old - top)
            total = None
            out = None
            for i in range(n):
                p = jnp.exp(scores[i] - top)
                t = jnp.sum(p, axis=0, keepdims=True)
                o = dotf(v_t[i][odd * 64 : odd * 64 + 64], p.astype(LOW))
                total = t if total is None else total + t
                out = o if out is None else out + o
            if not first:
                total = total + sum_in[row, :] * fade
                out = out + acc_in[rows, :] * fade
            if last:
                out = out / total
                top = top + jnp.log(total)
            acc_out[rows, :] = out
            top_out[row, :] = top
            sum_out[row, :] = total

    over_pairs(HEADS, loop, pair_body)


def fwd_call(places, first, last, loop, where_, norm, w_qkv, tokens, queries, state):
    keys, width = tokens[0].shape
    n = len(tokens)
    outs = [
        struct((HEADS, keys), F32),
        struct((HEADS, keys), F32),
        struct((width, keys), F32),
        struct((n * keys, width), LOW),
        struct((n * keys, 2 * width), LOW),
    ]
    args = [*where_, *norm, w_qkv, *tokens]
    if first:
        outs.append(struct((keys, width), LOW))
    else:
        args += [queries, *state]
    return call(
        partial(fwd_kernel, places, first, last, loop),
        "attend",
        outs,
        args,
        n * (HEADS * keys * keys * 256 * 8 + keys * width * width * 4),
        aliases={} if first else {len(args) - 3 + i: i for i in range(3)},
        scratch=[pltpu.VMEM((n, keys, keys), F32)],
        exps=n * HEADS * keys * keys,
    )


def bwd_kernel(places, ys, first, last, loop, *refs):
    n = len(places)
    seg_ref, tag_ref, from_ref, w_ref, q_ref, do_ref, lse_ref, delta_ref, kv = refs[:9]
    tokens = refs[9 : 9 + n]
    refs = refs[9 + n :]
    if not first:
        dq_in, sums_in = refs[:2]
        refs = refs[2:]
    dq_out, sums_out, dkv = refs[:3]
    dn = refs[3 : 3 + n]
    if last:
        gq_out = refs[3 + n]
    bias = refs[-1]
    keys, width = tokens[0].shape
    for i in range(n):
        bias[i] = key_bias(places[i](), seg_ref, tag_ref, from_ref)

    def pair_body(pair):
        lanes = pl.multiple_of(pair * 128, 128)
        at, vat = pl.ds(lanes, 128), pl.ds(width + lanes, 128)
        q_pair = q_ref[:, at]
        do_pair = do_ref[:, at]
        chunk = [pl.ds(i * keys, keys) for i in range(n)]
        k_t = [kv[chunk[i], at].T for i in range(n)]
        dk = [None] * n
        dv = [None] * n
        for odd in range(2):
            h = pair * 2 + odd
            row = pl.ds(h, 1)
            rows = pl.ds(pl.multiple_of(h * 64, 64), 64)
            q_h = head_lanes(q_pair, odd)
            do_h = head_lanes(do_pair, odd)
            lse = lse_ref[row, :]
            delta = delta_ref[row, :]
            dq = None
            for i in range(n):
                p = jnp.exp(dotf(kv[chunk[i], at], q_h, NT) + bias[i] - lse)
                dp = dotf(kv[chunk[i], vat], do_h, NT)
                ds = (p * (dp - delta)).astype(LOW)
                v_part = dotf(p.astype(LOW), do_h)
                k_part = dotf(ds, q_h)
                q_part = dotf(k_t[i][odd * 64 : odd * 64 + 64], ds)
                dv[i] = v_part if odd == 0 else dv[i] + v_part
                dk[i] = k_part if odd == 0 else dk[i] + k_part
                dq = q_part if dq is None else dq + q_part
            if not first:
                dq = dq + dq_in[rows, :]
            dq_out[rows, :] = dq
        for i in range(n):
            dkv[chunk[i], at] = dk[i].astype(LOW)
            dkv[chunk[i], vat] = dv[i].astype(LOW)

    over_pairs(HEADS, loop, pair_body)
    gain_sum = bias_sum = 0.0
    if last:
        grad_query = (dq_out[...].T * 0.125).astype(LOW)
        gq_out[...] = grad_query
    for i in range(n):
        part = dotf(dkv[pl.ds(i * keys, keys), :], w_ref[:, width:], NT)
        if last and i == n - 1:
            part = part + dotf(grad_query, w_ref[:, :width], NT)
        dn[i][...] = part.astype(dn[i].dtype)
        hat = norm_hat(tokens[i][...].astype(F32))[0]
        gain_sum = gain_sum + jnp.sum(part * hat, axis=0, keepdims=True)
        bias_sum = bias_sum + jnp.sum(part, axis=0, keepdims=True)
    if first:
        sums_out[...] = jnp.zeros_like(sums_out)
    else:
        sums_out[...] = sums_in[...]
    sums_out[0:1, :] += gain_sum
    sums_out[1:2, :] += bias_sum


def bwd_call(places, kinds, first, last, loop, where_, w_qkv, queries, grad_attn, log_total, delta, kv, tokens, carried):
    keys, width = tokens[0].shape
    n = len(tokens)
    outs = [
        struct((width, keys), F32),
        struct((8, width), F32),
        struct((n * keys, 2 * width), LOW),
        *(struct((keys, width), kind) for kind in kinds),
    ]
    if last:
        outs.append(struct((keys, width), LOW))
    args = [*where_, w_qkv, queries, grad_attn, log_total, delta, kv, *tokens, *carried]
    return call(
        partial(bwd_kernel, places, None, first, last, loop),
        "attend_back",
        outs,
        args,
        n * (HEADS * keys * keys * 256 * 14 + keys * width * width * 4),
        aliases={} if first else {len(args) - 2: 0, len(args) - 1: 1},
        scratch=[pltpu.VMEM((n, keys, keys), F32)],
        exps=n * HEADS * keys * keys,
    )


def mid_kernel(
    attn_ref, x_ref, dy_ref, wo_ref, bo_ref, g2_ref, s2_ref, wu_ref, bu_ref, wd_ref, bd_ref,
    mixed_ref, attn_low_ref, normed_ref, act_ref, pre_ref, branch_ref, mid_ref, do_ref, delta_ref, sums_ref,
):
    rows, width = x_ref.shape
    hidden = wu_ref.shape[1]
    attn_low = attn_ref[...].T.astype(LOW)
    attn_low_ref[...] = attn_low
    x_mid = x_ref[...].astype(F32) + dotf(attn_low, wo_ref[...]) + bo_ref[...]
    hat, inv = norm_hat(x_mid)
    gain = g2_ref[...]
    normed = (hat * gain + s2_ref[...]).astype(LOW)
    normed_ref[...] = normed
    dy = dy_ref[...]
    dy_full = dy.astype(F32)
    down = None
    grad_normed = None
    for j in range(hidden // width):
        cols = pl.ds(j * width, width)
        pre = dotf(normed, wu_ref[:, cols]) + bu_ref[:, cols]
        cdf = 0.5 + 0.5 * lax.erf(pre * (0.5**0.5))
        slope = cdf + pre * (jnp.exp(-0.5 * pre * pre) * 0.3989422804014327)
        act = (pre * cdf).astype(LOW)
        act_ref[:, cols] = act
        part = dotf(act, wd_ref[cols, :])
        down = part if down is None else down + part
        grad_pre = (dotf(dy, wd_ref[cols, :], NT) * slope).astype(LOW)
        pre_ref[:, cols] = grad_pre
        part = dotf(grad_pre, wu_ref[:, cols], NT)
        grad_normed = part if grad_normed is None else grad_normed + part
        sums_ref[4 + j : 5 + j, :] = jnp.sum(grad_pre.astype(F32), axis=0, keepdims=True)
    mixed_ref[...] = (x_mid + down + bd_ref[...]).astype(LOW)
    grad_mid = dy_full + norm_back(hat, inv, gain, grad_normed)
    mid_ref[...] = grad_mid
    branch = grad_mid.astype(LOW)
    branch_ref[...] = branch
    grad_attn = dotf(branch, wo_ref[...], NT).astype(LOW)
    do_ref[...] = grad_attn
    product = grad_attn.astype(F32).T * attn_ref[...]
    size = width // HEADS
    for h in range(HEADS):
        delta_ref[h : h + 1, :] = jnp.sum(product[h * size : (h + 1) * size, :], axis=0, keepdims=True)
    sums_ref[0:1, :] = jnp.sum(branch.astype(F32), axis=0, keepdims=True)
    sums_ref[1:2, :] = jnp.sum(grad_normed * hat, axis=0, keepdims=True)
    sums_ref[2:3, :] = jnp.sum(grad_normed, axis=0, keepdims=True)
    sums_ref[3:4, :] = jnp.sum(dy_full, axis=0, keepdims=True)


def mid_call(attn_t, patches, cotangent, w_out, b_out, g2, s2, w_up, b_up, w_down, b_down):
    rows, width = patches.shape
    hidden = w_up.shape[1]
    outs = [
        struct((rows, width), LOW),
        struct((rows, width), LOW),
        struct((rows, width), LOW),
        struct((rows, hidden), LOW),
        struct((rows, hidden), LOW),
        struct((rows, width), LOW),
        struct((rows, width), F32),
        struct((rows, width), LOW),
        struct((HEADS, rows), F32),
        struct((4 + hidden // width, width), F32),
    ]
    args = [attn_t, patches, cotangent, w_out, b_out, g2, s2, w_up, b_up, w_down, b_down]
    return call(mid_kernel, "middle", outs, args, rows * width * (hidden * 8 + width * 4), exps=rows * hidden * 4, vmem=48)


def weight_kernel(spec, kept, *refs):
    c = lax.axis_index("dp") % 2
    if not kept:
        c = 1 - c
    at = 0
    ins = []
    for lefts, parts in spec:
        ins.append((refs[at : at + lefts], refs[at + lefts : at + 2 * lefts], parts))
        at += 2 * lefts
    got = refs[at : at + len(spec)] if kept else None
    outs = refs[at + len(spec) :] if kept else refs[at:]
    for number, (lefts, rights, parts) in enumerate(ins):
        out = outs[number]
        total = out.shape[0]
        share = rights[0].shape[1] // parts
        half = share // 2
        step = min(total, 768)
        for part in range(parts):
            cols = pl.ds(pl.multiple_of(part * share + c * half, 128), half)
            to = pl.ds(part * half, half)
            for begin in range(0, total, step):
                rows = pl.ds(begin, step)
                acc = None
                for left, right in zip(lefts, rights):
                    term = dotf(left[:, rows], right[:, cols], TN)
                    acc = term if acc is None else acc + term
                if kept:
                    acc = acc + got[number][rows, to].astype(F32)
                out[rows, to] = acc.astype(LOW)


def weight_call(jobs, got=None):
    spec, args, outs, flops = [], [], [], 0
    for lefts, rights, parts in jobs:
        spec.append((len(lefts), parts))
        args += [*lefts, *rights]
        outs.append(struct((lefts[0].shape[1], rights[0].shape[1] // 2), LOW))
        flops += sum(a.shape[0] for a in lefts) * lefts[0].shape[1] * rights[0].shape[1]
    return call(
        partial(weight_kernel, tuple(spec), got is not None),
        "weights",
        outs,
        args + list(got or ()),
        flops,
        vmem=40,
    )


def end_kernel(x_ref, gain_ref, mid_ref, *refs):
    out = refs[-1]
    grad = refs[0][...].astype(F32)
    for ref in refs[1:-1]:
        grad = grad + ref[...].astype(F32)
    hat, inv = norm_hat(x_ref[...].astype(F32))
    out[...] = mid_ref[...] + norm_back(hat, inv, gain_ref[...], grad)


class Grid:
    def __init__(self, mesh):
        ndp, nblk = mesh.shape["dp"], mesh.shape["blk"]
        self.n = {"c": 2, "x": ndp // 2, "y": 2, "z": nblk // 2}
        self.nblk, self.ndp = nblk, ndp

    def locate(self):
        dp, blk = lax.axis_index("dp"), lax.axis_index("blk")
        self.at = {"x": dp // 2, "c": dp % 2, "z": blk // 2, "y": blk % 2}

    def send(self, value, axis, target):
        pairs = []
        n = self.n
        for x in range(n["x"]):
            for c in range(2):
                for z in range(n["z"]):
                    for y in range(2):
                        here = {"x": x, "c": c, "z": z, "y": y}
                        to = target(here[axis])
                        if to is None:
                            continue
                        there = dict(here)
                        there[axis] = to
                        flat = [((p["x"] * 2 + p["c"]) * n["z"] + p["z"]) * 2 + p["y"] for p in (here, there)]
                        pairs.append(tuple(flat))
        return lax.ppermute(value, AXES, pairs)

    def swap(self, value, axis):
        return self.send(value, axis, lambda i: 1 - i)

    def up(self, value, axis, low, high):
        return self.send(value, axis, lambda i: i + 1 if low <= i < high else None)

    def down(self, value, axis, low, high):
        return self.send(value, axis, lambda i: i - 1 if low <= i < high else None)

    def all_sum(self, value, axis):
        step = 1
        while step < self.n[axis]:
            value = value + self.send(value, axis, lambda i: i ^ step)
            step *= 2
        return value

    def number(self, axis, table):
        out = jnp.int32(table[0])
        for i in range(1, len(table)):
            out = jnp.where(self.at[axis] == i, jnp.int32(table[i]), out)
        return out

    def pick(self, axis, choices):
        groups = {}
        for i, value in enumerate(choices):
            groups.setdefault(id(value), (value, []))[1].append(i)
        groups = list(groups.values())
        out = groups[0][0]
        for value, members in groups[1:]:
            here = functools.reduce(jnp.logical_or, [self.at[axis] == i for i in members])
            out = jnp.where(here, value, out)
        return out

    def arrivals(self, axis):
        n = self.n[axis]
        table = []
        for i in range(n):
            row = []
            for s in range(n - 1):
                if i - 1 - s >= 0:
                    row.append((i - 1 - s, "up", s))
                if i + 1 + s < n:
                    row.append((i + 1 + s, "down", s))
            table.append(row)
        return table

    def line_gather(self, value, axis):
        n = self.n[axis]
        table = self.arrivals(axis)
        moved = {}
        up = down = value
        for s in range(n - 1):
            up = self.up(up, axis, s, n - 1)
            down = self.down(down, axis, 1, n - s)
            moved["up", s], moved["down", s] = up, down
        slots = [value]
        for k in range(n - 1):
            slots.append(self.pick(axis, [moved[table[i][k][1:]] for i in range(n)]))
        return slots

    def line_scatter(self, piece, axis, own=None):
        n = self.n[axis]
        if n == 1:
            return [piece([0])]
        if n == 2:
            got = self.swap(piece([1, 0]).astype(LOW), axis)
            return [piece([0, 1]), got]
        up = down = None
        for s in range(n - 1):
            going_up = [n - 1 - s + i if s >= i and i < n - 1 else None for i in range(n)]
            going_down = [s - (n - 1 - i) if s >= n - 1 - i and i > 0 else None for i in range(n)]
            a, b = piece(going_up).astype(F32), piece(going_down).astype(F32)
            if up is not None:
                a, b = a + up.astype(F32), b + down.astype(F32)
            up = self.up(a.astype(LOW), axis, 0, min(s + 1, n - 1))
            down = self.down(b.astype(LOW), axis, max(n - 1 - s, 1), n)
        return [piece(list(range(n))), up, down]

    def of_array(self, array, axis, dim):
        def piece(numbers):
            table = [0 if p is None else p for p in numbers]
            return lax.dynamic_index_in_dim(array, self.number(axis, table), dim, keepdims=False)

        return piece

    def of_slots(self, slots, axis):
        n = self.n[axis]
        table = self.arrivals(axis)

        def piece(numbers):
            chosen = []
            for i, p in enumerate(numbers):
                if p is None:
                    chosen.append(None)
                elif p == i:
                    chosen.append(slots[0])
                else:
                    chosen.append(slots[1 + [row[0] for row in table[i]].index(p)])
            some = next(v for v in chosen if v is not None)
            return self.pick(axis, [some if v is None else v for v in chosen])

        return piece

    def gather_line(self, value, axis):
        n = self.n[axis]
        if n == 1:
            return [value]
        if n == 2:
            got = self.swap(value, axis)
            first = self.at[axis] == 0
            return [jnp.where(first, value, got), jnp.where(first, got, value)]
        slots = self.line_gather(value, axis)
        table = [[i] + [row[0] for row in self.arrivals(axis)[i]] for i in range(n)]
        return [self.pick(axis, [slots[table[i].index(p)] for i in range(n)]) for p in range(n)]


def total_of(terms):
    return functools.reduce(lambda a, b: a + b, [t.astype(F32) for t in terms])


def local(
    grid,
    patches,
    segment_ids,
    sensor_tags,
    seq_starts,
    ln1_gain,
    ln1_bias,
    w_qkv,
    w_out,
    b_out,
    ln2_gain,
    ln2_bias,
    w_up,
    b_up,
    w_down,
    b_down,
    cotangent,
):
    grid.locate()
    nblk, nz, nx = grid.nblk, grid.n["z"], grid.n["x"]
    loop = nz > 4
    rows, width = patches.shape
    me = lax.axis_index("blk")
    row = lambda v: v.reshape(1, -1)
    where_ = (segment_ids.reshape(nblk, rows), sensor_tags.reshape(nblk, rows), row(seq_starts))
    norm_one = (row(ln1_gain), row(ln1_bias))

    arrivals = grid.arrivals("z")

    def place(k, other):
        def chunk():
            blk = lax.axis_index("blk")
            z, y = blk // 2, blk % 2
            at = z
            if k > 0:
                at = jnp.int32(arrivals[0][k - 1][0])
                for i in range(1, nz):
                    at = jnp.where(z == i, jnp.int32(arrivals[i][k - 1][0]), at)
            return at * 2 + (1 - y if other else y)

        return chunk

    units = []
    for u in range(nz + 1):
        parts = ([(u - 1, 1)] if u > 0 else []) + ([(u, 0)] if u < nz else [])
        units.append(parts)
    places = [[place(*p) for p in parts] for parts in units]

    state, queries = None, None
    normed, kv, tokens = [], [], []
    held = {(0, 0): patches}
    moved = {}
    up = down = patches
    for u in range(nz + 1):
        if u < nz - 1:
            up = grid.up(up, "z", u, nz - 1)
            down = grid.down(down, "z", 1, nz - u)
        got = grid.swap(held[u, 0], "y") if u < nz else None
        tokens.append([held[p] for p in units[u]])
        outs = fwd_call(places[u], u == 0, u == nz, loop, where_, norm_one, w_qkv, tokens[u], queries, state)
        if u < nz:
            up, down, got, outs = lax.optimization_barrier((up, down, got, outs))
            moved["up", u], moved["down", u] = up, down
            held[u, 1] = got
        if u < nz - 1:
            held[u + 1, 0] = grid.pick("z", [moved[arrivals[i][u][1:]] for i in range(nz)])
        state = outs[:3]
        normed.append(outs[3])
        kv.append(outs[4])
        if u == 0:
            queries = outs[5]
    log_total, _, attn_t = state

    mixed_out, attn_low, normed_two, act_low, grad_pre, grad_branch, grad_mid, grad_attn, delta, sums = mid_call(
        attn_t, patches, cotangent, w_out, row(b_out), row(ln2_gain), row(ln2_bias), w_up, row(b_up), w_down, row(b_down)
    )

    def reduce_rows(part, order):
        half = part.shape[1]
        part = part.reshape(nz, 2, nx, -1, half)
        dims = {"z": 0, "y": 1, "x": 2}
        for axis in order:
            part = total_of(grid.line_scatter(grid.of_array(part, axis, dims[axis]), axis)).astype(LOW)
            dims = {k: d - (d > dims[axis]) for k, d in dims.items()}
        return grid.gather_line(jnp.concatenate(grid.gather_line(part, "x"), axis=0), "c")

    jobs = [([act_low], [cotangent], 1), ([normed_two], [grad_pre], 1), ([attn_low], [grad_branch], 1)]
    given = weight_call(jobs)
    given, grad_attn = lax.optimization_barrier((given, grad_attn))
    kept = weight_call(jobs, [grid.swap(v, "c") for v in given])
    kept, grad_attn = lax.optimization_barrier((kept, grad_attn))
    total_down, total_up, total_out = (
        jnp.concatenate(reduce_rows(v, order), axis=1).astype(F32) for v, order in zip(kept, ("xyz", "yxz", "xyz"))
    )

    def reduce_small(part):
        for axis in "cxyz":
            part = grid.all_sum(part, axis)
        return part

    def own_part(v):
        size = v.size // nblk
        return lax.dynamic_slice_in_dim(v.reshape(-1), me * size, size)

    sums = reduce_small(sums)

    carried = ()
    dkv = [None] * (nz + 1)
    dn = {}
    slots = [None] * nz
    for u in reversed(range(nz + 1)):
        kinds = [LOW] * len(units[u])
        outs = bwd_call(
            places[u], kinds, u == nz, u == 0, loop, where_, w_qkv, queries, grad_attn, log_total, delta, kv[u], tokens[u],
            carried,
        )
        carried = outs[:2]
        dkv[u] = outs[2]
        for i, part in enumerate(units[u]):
            dn[part] = outs[3 + i]
        if u == 0:
            grad_query = outs[-1]
    for k in range(nz):
        got = grid.swap(dn[k, 1], "y")
        slots[k] = (dn[k, 0].astype(F32) + got.astype(F32)).astype(LOW) if k else None
        if k == 0:
            last_got = got
    slots[0] = dn[0, 0]
    terms = grid.line_scatter(grid.of_slots(slots, "z"), "z")
    (grad_patches,) = call(
        end_kernel, "finish", [struct((rows, width), F32)], [patches, norm_one[0], grad_mid, *terms, last_got], rows * width
    )

    jobs = [(normed[:1], [grad_query], 1), (normed, dkv, 2)]
    given = weight_call(jobs)
    kept = weight_call(jobs, [grid.swap(v, "c") for v in given])
    kept_qkv = jnp.concatenate(kept, axis=1)
    halves = reduce_rows(kept_qkv, "xyz")
    half = width // 2
    total_qkv = jnp.concatenate(
        [h[:, i * half : (i + 1) * half] for i in range(3) for h in halves], axis=1
    ).astype(F32)
    late = reduce_small(carried[1])
    return (
        mixed_out,
        grad_patches,
        own_part(late[0]),
        own_part(late[1]),
        total_qkv,
        total_out,
        own_part(sums[0]),
        own_part(sums[1]),
        own_part(sums[2]),
        total_up,
        own_part(sums[4:]),
        total_down,
        own_part(sums[3]),
    )


def solution(mesh):
    in_specs = (
        P(("dp", "blk"), None),
        P("dp"),
        P("dp"),
        P(("dp", "blk")),
        *(P(),) * 11,
        P(("dp", "blk"), None),
    )
    out_specs = (
        P(("dp", "blk"), None),
        P(("dp", "blk"), None),
        P("blk"),
        P("blk"),
        P("blk", None),
        P("blk", None),
        P("blk"),
        P("blk"),
        P("blk"),
        P("blk", None),
        P("blk"),
        P("blk", None),
        P("blk"),
    )
    return jax.shard_map(
        partial(local, Grid(mesh)), mesh=mesh, in_specs=in_specs, out_specs=out_specs, check_vma=False
    )
```

```python
import functools
from functools import partial

import jax
import jax.numpy as jnp
from jax import lax
from jax.experimental import pallas as pl
from jax.experimental.pallas import tpu as pltpu
from jax.sharding import PartitionSpec as P

HEADS = 12
EPSILON = 1e-06
MASKED = -1e30
AXES = ("dp", "blk")
NT = (((1,), (1,)), ((), ()))
TN = (((0,), (0,)), ((), ()))
NN = (((1,), (0,)), ((), ()))
VM = pl.BlockSpec(memory_space=pltpu.VMEM)
FAR = pl.BlockSpec(memory_space=pltpu.HBM)
LOW = jnp.bfloat16
F32 = jnp.float32
MIB = 1 << 20


def dotf(a, b, dims=NN):
    return lax.dot_general(a, b, dims, preferred_element_type=F32)


def struct(shape, dtype):
    return jax.ShapeDtypeStruct(shape, dtype)


def norm_hat(x):
    center = x - jnp.mean(x, axis=-1, keepdims=True)
    inv = lax.rsqrt(jnp.mean(center * center, axis=-1, keepdims=True) + EPSILON)
    return center * inv, inv


def norm_back(hat, inv, gain, grad):
    g = grad * gain
    return inv * (g - jnp.mean(g, axis=-1, keepdims=True) - hat * jnp.mean(g * hat, axis=-1, keepdims=True))


def call(kernel, name, outs, args, flops, aliases=None, scratch=(), exps=0, vmem=8, far=(), far_outs=()):
    moved = sum(a.size * a.dtype.itemsize for a in args) + sum(o.size * o.dtype.itemsize for o in outs)
    return pl.pallas_call(
        kernel,
        out_shape=outs,
        in_specs=[FAR if i in far else VM for i in range(len(args))],
        out_specs=tuple(FAR if i in far_outs else VM for i in range(len(outs))),
        input_output_aliases=aliases or {},
        scratch_shapes=scratch,
        compiler_params=pltpu.CompilerParams(vmem_limit_bytes=vmem * MIB),
        cost_estimate=pl.CostEstimate(flops=int(flops) // 4, bytes_accessed=int(moved) // 4, transcendentals=0),
        name=name,
    )(*args)


def line(ref):
    return ref[...].reshape(1, -1)


def key_bias(chunk, seg_ref, tag_ref, from_ref):
    keys = seg_ref.shape[1]
    me = lax.axis_index("blk")
    base = lax.axis_index("dp") * (seg_ref.shape[0] * keys)

    def column(ref):
        return jnp.broadcast_to(ref[pl.ds(chunk, 1), :], (8, keys)).T[:, 0:1]

    kseg, ktag = column(seg_ref), column(tag_ref)
    qseg, qtag = seg_ref[pl.ds(me, 1), :], tag_ref[pl.ds(me, 1), :]
    pos = base + chunk * keys + lax.broadcasted_iota(jnp.int32, (keys, keys), 0)
    seen = (kseg == qseg) & (pos >= line(from_ref))
    tags = (ktag == qtag) | (qtag == 0) | (ktag == 0)
    return jnp.where(seen & tags, 0.0, MASKED)


def head_lanes(block, odd):
    lane = lax.broadcasted_iota(jnp.int32, block.shape, 1)
    return jnp.where((lane >= 64) if odd else (lane < 64), block, jnp.zeros_like(block))


def over_pairs(heads, loop, body):
    if loop:
        lax.fori_loop(0, heads // 2, lambda i, c: (body(i), c)[1], 0)
    else:
        for i in range(heads // 2):
            body(i)


def fwd_kernel(places, first, last, loop, *refs):
    n = len(places)
    seg_ref, tag_ref, from_ref, gain_ref, shift_ref, w_ref = refs[:6]
    tokens = refs[6 : 6 + n]
    refs = refs[6 + n :]
    if first:
        top_out, sum_out, acc_out, normed_far, kv_far, q_ref = refs[:6]
    else:
        q_ref, top_in, sum_in, acc_in, top_out, sum_out, acc_out, normed_far, kv_far = refs[:9]
    bias, normed_out, kv_out, sems = refs[-4:]
    keys, width = tokens[0].shape
    for i in range(n):
        at = pl.ds(i * keys, keys)
        hat = norm_hat(tokens[i][...].astype(F32))[0]
        normed = (hat * line(gain_ref) + line(shift_ref)).astype(LOW)
        normed_out[at, :] = normed
        bias[i] = key_bias(places[i](), seg_ref, tag_ref, from_ref)
    keep_normed = pltpu.make_async_copy(normed_out, normed_far, sems.at[0])
    keep_normed.start()
    normed = normed_out[...]
    if first:
        q_ref[...] = (dotf(normed, w_ref[:, :width]).astype(LOW) * jnp.asarray(0.125, LOW)).astype(LOW)
    for j in range(2):
        cols = pl.ds(j * width, width)
        kv_out[:, cols] = dotf(normed, w_ref[:, pl.ds((j + 1) * width, width)]).astype(LOW)
    keep_kv = pltpu.make_async_copy(kv_out, kv_far, sems.at[1])
    keep_kv.start()

    def pair_body(pair):
        lanes = pl.multiple_of(pair * 128, 128)
        at, vat = pl.ds(lanes, 128), pl.ds(width + lanes, 128)
        q_pair = q_ref[:, at]
        v_t = [kv_out[pl.ds(i * keys, keys), vat].T for i in range(n)]
        for odd in range(2):
            h = pair * 2 + odd
            row = pl.ds(h, 1)
            rows = pl.ds(pl.multiple_of(h * 64, 64), 64)
            q_h = head_lanes(q_pair, odd)
            scores = [dotf(kv_out[pl.ds(i * keys, keys), at], q_h, NT) + bias[i] for i in range(n)]
            top = jnp.max(scores[0], axis=0, keepdims=True)
            for s in scores[1:]:
                top = jnp.maximum(top, jnp.max(s, axis=0, keepdims=True))
            if not first:
                old = top_in[row, :]
                top = jnp.maximum(top, old)
                fade = jnp.exp(old - top)
            total = None
            out = None
            for i in range(n):
                p = jnp.exp(scores[i] - top)
                t = jnp.sum(p, axis=0, keepdims=True)
                o = dotf(v_t[i][odd * 64 : odd * 64 + 64], p.astype(LOW))
                total = t if total is None else total + t
                out = o if out is None else out + o
            if not first:
                total = total + sum_in[row, :] * fade
                out = out + acc_in[rows, :] * fade
            if last:
                out = out / total
                top = top + jnp.log(total)
            acc_out[rows, :] = out
            top_out[row, :] = top
            sum_out[row, :] = total

    over_pairs(HEADS, loop, pair_body)
    keep_normed.wait()
    keep_kv.wait()


def fwd_call(places, first, last, loop, where_, norm, w_qkv, tokens, queries, state):
    keys, width = tokens[0].shape
    n = len(tokens)
    outs = [
        struct((HEADS, keys), F32),
        struct((HEADS, keys), F32),
        struct((width, keys), F32),
        struct((n * keys, width), LOW),
        struct((n * keys, 2 * width), LOW),
    ]
    args = [*where_, *norm, w_qkv, *tokens]
    if first:
        outs.append(struct((keys, width), LOW))
    else:
        args += [queries, *state]
    return call(
        partial(fwd_kernel, places, first, last, loop),
        "attend",
        outs,
        args,
        n * (HEADS * keys * keys * 256 * 8 + keys * width * width * 4),
        aliases={} if first else {len(args) - 3 + i: i for i in range(3)},
        scratch=[
            pltpu.VMEM((n, keys, keys), F32),
            pltpu.VMEM((n * keys, width), LOW),
            pltpu.VMEM((n * keys, 2 * width), LOW),
            pltpu.SemaphoreType.DMA((2,)),
        ],
        far_outs=(3, 4),
        exps=n * HEADS * keys * keys,
    )


def bwd_kernel(places, first, last, loop, *refs):
    n = len(places)
    seg_ref, tag_ref, from_ref, w_ref, q_ref, do_ref, lse_ref, delta_ref, kv_far = refs[:9]
    tokens_far = refs[9 : 9 + n]
    refs = refs[9 + n :]
    if not first:
        dq_in, sums_in = refs[:2]
        refs = refs[2:]
    dq_out, sums_out, dkv_far = refs[:3]
    dn = refs[3 : 3 + n]
    if last:
        gq_out = refs[3 + n]
    bias, kv, dkv, tokens, kv_sems, token_sems, out_sem = refs[-7:]
    keys, width = tokens.shape[1:]
    part_rows = keys // 2
    fetches = []
    for i in range(2 * n):
        some = pl.ds(i * part_rows, part_rows)
        fetches.append(pltpu.make_async_copy(kv_far.at[some, :], kv.at[some, :], kv_sems.at[i]))
    fetch_tokens = [pltpu.make_async_copy(tokens_far[i], tokens.at[i], token_sems.at[i]) for i in range(n)]
    for copy in fetches + fetch_tokens:
        copy.start()
    for i in range(n):
        bias[i] = key_bias(places[i](), seg_ref, tag_ref, from_ref)
    for copy in fetches:
        copy.wait()

    def pair_body(pair):
        lanes = pl.multiple_of(pair * 128, 128)
        at, vat = pl.ds(lanes, 128), pl.ds(width + lanes, 128)
        q_pair = q_ref[:, at]
        do_pair = do_ref[:, at]
        chunk = [pl.ds(i * keys, keys) for i in range(n)]
        k_t = [kv[chunk[i], at].T for i in range(n)]
        dk = [None] * n
        dv = [None] * n
        for odd in range(2):
            h = pair * 2 + odd
            row = pl.ds(h, 1)
            rows = pl.ds(pl.multiple_of(h * 64, 64), 64)
            q_h = head_lanes(q_pair, odd)
            do_h = head_lanes(do_pair, odd)
            lse = lse_ref[row, :]
            delta = delta_ref[row, :]
            dq = None
            for i in range(n):
                p = jnp.exp(dotf(kv[chunk[i], at], q_h, NT) + bias[i] - lse)
                dp = dotf(kv[chunk[i], vat], do_h, NT)
                ds = (p * (dp - delta)).astype(LOW)
                v_part = dotf(p.astype(LOW), do_h)
                k_part = dotf(ds, q_h)
                q_part = dotf(k_t[i][odd * 64 : odd * 64 + 64], ds)
                dv[i] = v_part if odd == 0 else dv[i] + v_part
                dk[i] = k_part if odd == 0 else dk[i] + k_part
                dq = q_part if dq is None else dq + q_part
            if not first:
                dq = dq + dq_in[rows, :]
            dq_out[rows, :] = dq
        for i in range(n):
            dkv[chunk[i], at] = dk[i].astype(LOW)
            dkv[chunk[i], vat] = dv[i].astype(LOW)

    over_pairs(HEADS, loop, pair_body)
    keep = pltpu.make_async_copy(dkv, dkv_far, out_sem)
    keep.start()
    gain_sum = bias_sum = 0.0
    if last:
        grad_query = (dq_out[...].T * 0.125).astype(LOW)
        gq_out[...] = grad_query
    for i in range(n):
        part = dotf(dkv[pl.ds(i * keys, keys), :], w_ref[:, width:], NT)
        if last and i == n - 1:
            part = part + dotf(grad_query, w_ref[:, :width], NT)
        dn[i][...] = part.astype(dn[i].dtype)
        fetch_tokens[i].wait()
        hat = norm_hat(tokens[i].astype(F32))[0]
        gain_sum = gain_sum + jnp.sum(part * hat, axis=0, keepdims=True)
        bias_sum = bias_sum + jnp.sum(part, axis=0, keepdims=True)
    if first:
        sums_out[...] = jnp.zeros_like(sums_out)
    else:
        sums_out[...] = sums_in[...]
    sums_out[0:1, :] += gain_sum
    sums_out[1:2, :] += bias_sum
    keep.wait()


def bwd_call(places, kinds, first, last, loop, where_, w_qkv, queries, grad_attn, log_total, delta, kv, tokens, carried):
    keys, width = tokens[0].shape
    n = len(tokens)
    outs = [
        struct((width, keys), F32),
        struct((8, width), F32),
        struct((n * keys, 2 * width), LOW),
        *(struct((keys, width), kind) for kind in kinds),
    ]
    if last:
        outs.append(struct((keys, width), LOW))
    args = [*where_, w_qkv, queries, grad_attn, log_total, delta, kv, *tokens, *carried]
    return call(
        partial(bwd_kernel, places, first, last, loop),
        "attend_back",
        outs,
        args,
        n * (HEADS * keys * keys * 256 * 14 + keys * width * width * 4),
        aliases={} if first else {len(args) - 2: 0, len(args) - 1: 1},
        scratch=[
            pltpu.VMEM((n, keys, keys), F32),
            pltpu.VMEM((n * keys, 2 * width), LOW),
            pltpu.VMEM((n * keys, 2 * width), LOW),
            pltpu.VMEM((n, keys, width), LOW),
            pltpu.SemaphoreType.DMA((2 * n,)),
            pltpu.SemaphoreType.DMA((n,)),
            pltpu.SemaphoreType.DMA,
        ],
        exps=n * HEADS * keys * keys,
        far=tuple(range(8, 9 + n)),
        far_outs=(2,),
    )


def mid_kernel(
    attn_ref, x_ref, dy_ref, wo_ref, bo_ref, g2_ref, s2_ref, wu_ref, bu_ref, wd_ref, bd_ref, *refs
):
    mixed_ref, left_ref, right_ref, given_ref, mid_ref, do_ref, delta_ref, sums_ref = refs[-8:]
    rows, width = x_ref.shape
    hidden = wu_ref.shape[1]
    half, blocks = width // 2, hidden // width
    attn_low = attn_ref[...].T.astype(LOW)
    left_ref[:, pl.ds(hidden + width, width)] = attn_low
    x_mid = x_ref[...].astype(F32) + dotf(attn_low, wo_ref[...]) + line(bo_ref)
    hat, inv = norm_hat(x_mid)
    gain = line(g2_ref)
    normed = (hat * gain + line(s2_ref)).astype(LOW)
    left_ref[:, pl.ds(hidden, width)] = normed
    dy = dy_ref[...]
    dy_full = dy.astype(F32)
    down = None
    grad_normed = None
    for j in range(blocks):
        cols = pl.ds(j * width, width)
        pre = dotf(normed, wu_ref[:, cols]) + bu_ref[cols].reshape(1, -1)
        cdf = 0.5 + 0.5 * lax.erf(pre * (0.5**0.5))
        slope = cdf + pre * (jnp.exp(-0.5 * pre * pre) * 0.3989422804014327)
        act = (pre * cdf).astype(LOW)
        left_ref[:, cols] = act
        part = dotf(act, wd_ref[cols, :])
        down = part if down is None else down + part
        grad_pre = (dotf(dy, wd_ref[cols, :], NT) * slope).astype(LOW)
        right_ref[j * 2 // blocks, :, pl.ds(j % (blocks // 2) * width, width)] = grad_pre
        part = dotf(grad_pre, wu_ref[:, cols], NT)
        grad_normed = part if grad_normed is None else grad_normed + part
        sums_ref[4 + j : 5 + j, :] = jnp.sum(grad_pre.astype(F32), axis=0, keepdims=True)
    mixed_ref[...] = (x_mid + down + line(bd_ref)).astype(LOW)
    grad_mid = dy_full + norm_back(hat, inv, gain, grad_normed)
    mid_ref[...] = grad_mid
    branch = grad_mid.astype(LOW)
    for c in range(2):
        right_ref[c, :, pl.ds(hidden // 2, half)] = branch[:, c * half : (c + 1) * half]
        right_ref[c, :, pl.ds(hidden // 2 + half, half)] = dy[:, c * half : (c + 1) * half]
    given_ref[...] = right_ref[1 - lax.axis_index("dp") % 2]
    grad_attn = dotf(branch, wo_ref[...], NT).astype(LOW)
    do_ref[...] = grad_attn
    product = grad_attn.astype(F32).T * attn_ref[...]
    size = width // HEADS
    for h in range(HEADS):
        delta_ref[h : h + 1, :] = jnp.sum(product[h * size : (h + 1) * size, :], axis=0, keepdims=True)
    sums_ref[0:1, :] = jnp.sum(branch.astype(F32), axis=0, keepdims=True)
    sums_ref[1:2, :] = jnp.sum(grad_normed * hat, axis=0, keepdims=True)
    sums_ref[2:3, :] = jnp.sum(grad_normed, axis=0, keepdims=True)
    sums_ref[3:4, :] = jnp.sum(dy_full, axis=0, keepdims=True)


def mid_call(near, attn_t, patches, cotangent, w_out, b_out, g2, s2, w_up, b_up, w_down, b_down):
    rows, width = patches.shape
    hidden = w_up.shape[1]
    outs = [
        struct((rows, width), LOW),
        struct((rows, hidden + 2 * width), LOW),
        struct((2, rows, hidden // 2 + width), LOW),
        struct((rows, hidden // 2 + width), LOW),
        struct((rows, width), F32),
        struct((rows, width), LOW),
        struct((HEADS, rows), F32),
        struct((4 + hidden // width, width), F32),
    ]
    args = [attn_t, patches, cotangent, w_out, b_out, g2, s2, w_up, b_up, w_down, b_down, *near]
    return call(mid_kernel, "middle", outs, args, rows * width * (hidden * 8 + width * 4), exps=rows * hidden * 4, vmem=16)


def halves_of_x(acc, pieces, half):
    acc = acc.reshape(pieces // 2, 2, -1, half)
    first = lax.axis_index("dp") // 2 == 0
    own = jnp.where(first, acc[:, 0], acc[:, 1]).astype(LOW)
    other = jnp.where(first, acc[:, 1], acc[:, 0]).astype(LOW)
    return other, own


def first_kernel(jobs, sums_to, pieces, left_ref, right_ref, left_got, right_got, sums_ref, sums_got, *refs):
    c = lax.axis_index("dp") % 2
    outs = refs[-2 * (1 + max(job[-1][-1][0] for job in jobs)) :]
    parts = len(outs) // 2
    half = outs[0].shape[2]
    width = 2 * half
    for left, total, right, targets in jobs:
        cols = pl.ds(right, half)
        each = total * 2 // (2 * pieces)
        for begin in range(0, total, width):
            rows = pl.ds(left + begin, width)
            acc = dotf(left_ref[:, rows], right_ref[c, :, cols], TN) + dotf(left_got[:, rows], right_got[:, cols], TN)
            pair = halves_of_x(acc, width // each, half)
            blks = width // each // 2
            at = pl.ds(begin // each // 2, blks)
            for part, low, high, row in targets:
                for side in range(2):
                    outs[part + side * parts][at, pl.ds(row, high - low), :] = pair[side][:, low:high, :]
    mine = sums_ref[:, pl.ds(pl.multiple_of(c * half, 128), half)] + sums_got[:, pl.ds(pl.multiple_of(c * half, 128), half)]
    mine = jnp.concatenate([mine, jnp.zeros_like(mine)], axis=0).astype(LOW)
    part, row = sums_to
    for side in range(2):
        out = outs[part + side * parts]
        out[:, pl.ds(row, 16), :] = jnp.broadcast_to(mine[None], (out.shape[0],) + mine.shape)


def first_call(near, jobs, sums_to, heights, pieces, half, left, right, left_got, right_got, sums, sums_got):
    outs = [struct((pieces // 2, h, half), LOW) for h in heights] * 2
    args = [left, right, left_got, right_got, sums, sums_got, *near]
    return call(
        partial(first_kernel, jobs, sums_to, pieces), "weights", outs, args, sum(h for h in heights) * pieces * half * 1024, vmem=12
    )


def second_kernel(pieces, units, *refs):
    me = lax.axis_index("dp") % 2
    gq_ref, sums_ref = refs[:2]
    normed_far, dkv_far = refs[2 : 2 + units], refs[2 + units : 2 + 2 * units]
    give, keep = refs[2 + 2 * units : 4 + 2 * units]
    normed, dkv = refs[4 + 2 * units : 4 + 3 * units], refs[4 + 3 * units : 4 + 4 * units]
    sems = refs[-1]
    copies = [pltpu.make_async_copy(normed_far[i], normed[i], sems.at[0, i]) for i in range(units)]
    copies += [pltpu.make_async_copy(dkv_far[i], dkv[i], sems.at[1, i]) for i in range(units)]
    for i in range(units):
        copies[i].start()
        copies[units + i].start()
    half = give.shape[3]
    width = 2 * half
    each = width // pieces
    copies[0].wait()
    for block in range(3):
        if block == 1:
            for copy in copies[1:]:
                copy.wait()
        for out, c in ((give, 1 - me), (keep, me)):
            if block == 0:
                cols = pl.ds(pl.multiple_of(c * half, 128), half)
                acc = dotf(normed[0][...], gq_ref[:, cols], TN)
            else:
                cols = pl.ds(pl.multiple_of((block - 1) * width + c * half, 128), half)
                acc = None
                for i in range(units):
                    term = dotf(normed[i][...], dkv[i][:, cols], TN)
                    acc = term if acc is None else acc + term
            pair = halves_of_x(acc, pieces, half)
            for side in range(2):
                out[side, :, pl.ds(block * each, each), :] = pair[side]
    for out, c in ((give, 1 - me), (keep, me)):
        mine = sums_ref[:, pl.ds(pl.multiple_of(c * half, 128), half)]
        mine = jnp.concatenate([mine, jnp.zeros_like(mine)], axis=0).astype(LOW)
        for side in range(2):
            out[side, :, pl.ds(3 * each, 16), :] = jnp.broadcast_to(mine[None], (out.shape[1],) + mine.shape)


def second_call(pieces, half, grad_query, sums, normed, dkv):
    units = len(normed)
    each = 2 * half // pieces
    outs = [struct((2, pieces // 2, 3 * each + 16, half), LOW)] * 2
    args = [grad_query, sums, *normed, *dkv]
    return call(
        partial(second_kernel, pieces, units),
        "weights",
        outs,
        args,
        sum(v.shape[0] for v in normed) * 2 * half * 8 * half,
        scratch=[pltpu.VMEM(v.shape, LOW) for v in (*normed, *dkv)] + [pltpu.SemaphoreType.DMA((2, units))],
        far=tuple(range(2, len(args))),
        vmem=20,
    )


def weight_kernel(spec, sums_at, pieces, far, count, *refs):
    me = lax.axis_index("dp") % 2
    ins = list(refs[:count])
    outs = refs[count : len(refs) - len(far) - (1 if far else 0)]
    waits = {}
    if far:
        sems = refs[-1]
        for i, number in enumerate(far):
            held = refs[len(refs) - 1 - len(far) + i]
            waits[number] = pltpu.make_async_copy(ins[number], held, sems.at[i])
            waits[number].start()
            ins[number] = held
    parts = len(outs) // 2
    for part, row, lefts, rights, starts in spec:
        for number in (*lefts, *rights):
            if number in waits:
                waits.pop(number).wait()
        for given in (True, False):
            c = 1 - me if given else me
            out = outs[part + (0 if given else parts)]
            half = out.shape[2]
            total = ins[lefts[0]].shape[1]
            each = total // pieces
            step = min(total, 768)
            cols = pl.ds(pl.multiple_of(jnp.where(c == 0, starts[0], starts[1]), 128), half)
            for begin in range(0, total, step):
                acc = None
                for left, right in zip(lefts, rights):
                    term = dotf(ins[left][:, pl.ds(begin, step)], ins[right][:, cols], TN)
                    acc = term if acc is None else acc + term
                acc = acc.reshape(step // each, each, half)
                out[pl.ds(begin // each, step // each), pl.ds(row, each), :] = acc.astype(LOW)
    if sums_at is not None:
        part, row, number = sums_at
        for given in (True, False):
            c = 1 - me if given else me
            out = outs[part + (0 if given else parts)]
            half = out.shape[2]
            mine = ins[number][:, pl.ds(pl.multiple_of(c * half, 128), half)]
            mine = jnp.concatenate([mine, jnp.zeros_like(mine)], axis=0).astype(LOW)
            out[:, pl.ds(row, 16), :] = jnp.broadcast_to(mine[None], (pieces,) + mine.shape)


def weight_call(pieces, heights, half, jobs, sums=None, sums_at=None, far=()):
    spec, args, flops = [], [], 0

    def index(array):
        for i, known in enumerate(args):
            if known is array:
                return i
        args.append(array)
        return len(args) - 1

    for part, row, lefts, rights, starts in jobs:
        spec.append((part, row, [index(v) for v in lefts], [index(v) for v in rights], starts))
        flops += sum(a.shape[0] for a in lefts) * lefts[0].shape[1] * half * 4
    if sums is not None:
        sums_at = (*sums_at, index(sums))
    far = tuple(i for i, a in enumerate(args) if any(a is v for v in far))
    scratch = [pltpu.VMEM(args[i].shape, args[i].dtype) for i in far]
    if far:
        scratch.append(pltpu.SemaphoreType.DMA((len(far),)))
    outs = [struct((pieces, h, half), LOW) for h in heights] * 2
    return call(
        partial(weight_kernel, spec, sums_at, pieces, far, len(args)),
        "weights",
        outs,
        args,
        flops,
        scratch=scratch,
        far=far,
        vmem=8 + sum(args[i].size * 2 for i in far) // MIB,
    )


def end_kernel(x_ref, gain_ref, mid_ref, *refs):
    out = refs[-1]
    grad = refs[0][...].astype(F32)
    for ref in refs[1:-1]:
        grad = grad + ref[...].astype(F32)
    hat, inv = norm_hat(x_ref[...].astype(F32))
    out[...] = mid_ref[...] + norm_back(hat, inv, line(gain_ref), grad)


class Grid:
    def __init__(self, mesh):
        ndp, nblk = mesh.shape["dp"], mesh.shape["blk"]
        self.n = {"c": 2, "x": ndp // 2, "y": 2, "z": nblk // 2}
        self.nblk, self.ndp = nblk, ndp

    def locate(self):
        dp, blk = lax.axis_index("dp"), lax.axis_index("blk")
        self.at = {"x": dp // 2, "c": dp % 2, "z": blk // 2, "y": blk % 2}

    def swap(self, value, axis, k=1):
        pairs = []
        n = self.n
        for x in range(n["x"]):
            for c in range(2):
                for z in range(n["z"]):
                    for y in range(2):
                        here = {"x": x, "c": c, "z": z, "y": y}
                        there = dict(here)
                        there[axis] ^= k
                        flat = [((p["x"] * 2 + p["c"]) * n["z"] + p["z"]) * 2 + p["y"] for p in (here, there)]
                        pairs.append(tuple(flat))
        return lax.ppermute(value, AXES, pairs)

    def all_sum(self, value, axis):
        step = 1
        while step < self.n[axis]:
            value = value + self.swap(value, axis, step)
            step *= 2
        return value

    def scatter(self, array, axis, dim):
        piece = lambda k: lax.dynamic_index_in_dim(array, self.at[axis] ^ k, dim, keepdims=False)
        got = []
        if self.n[axis] > 1:
            got = yield [self.swap(piece(k), axis, k) for k in range(1, self.n[axis])]
        return [piece(0), *got]

    def gather(self, value, axis):
        n = self.n[axis]
        if n == 1:
            return [value]
        got = yield [self.swap(value, axis, k) for k in range(1, n)]
        slots = [value, *got]
        at = self.at[axis]
        out = []
        for p in range(n):
            piece = slots[p]
            for i in range(1, n):
                piece = jnp.where(at == i, slots[p ^ i], piece)
            out.append(piece)
        return out


class Flow:
    def __init__(self, steps):
        self.steps, self.result = steps, None
        self.advance(None, True)

    def advance(self, value, first=False):
        try:
            self.pending = next(self.steps) if first else self.steps.send(value)
        except StopIteration as stop:
            self.pending, self.result = None, stop.value


def tie(flows, *values):
    flows = [f for f in flows if f.pending is not None]
    pending, values = lax.optimization_barrier(([f.pending for f in flows], values))
    for flow, value in zip(flows, pending):
        flow.advance(value)
    return values


def total_of(terms):
    return functools.reduce(lambda a, b: a + b, [t.astype(F32) for t in terms])


def reduce_plain(grid, loop, parts_of, w_qkv, left, right, sums, normed, patches, gain, grad_mid, blocks, each, hidden_each):
    places, units, where_, queries, grad_attn, log_total, delta, kv, tokens = parts_of
    nz, nx = grid.n["z"], grid.n["x"]
    rows, width = patches.shape
    half, hidden, pieces = width // 2, blocks * width, grid.nblk * nx
    act_low, normed_two, attn_low = left[:, :hidden], left[:, hidden : hidden + width], left[:, hidden + width :]
    grad_pre, grad_branch, dy = (
        jnp.concatenate([right[c, :, a:b] for c in range(2)], axis=1)
        for a, b in ((0, hidden // 2), (hidden // 2, hidden // 2 + half), (hidden // 2 + half, hidden // 2 + width))
    )

    def reduce_rows(given, kept):
        got = yield grid.swap(given, "c")
        part = (kept.astype(F32) + got.astype(F32)).astype(LOW).reshape(nz, 2, nx, -1, kept.shape[-1])
        for axis, dim in (("x", 2), ("y", 1), ("z", 0)):
            terms = yield from grid.scatter(part, axis, dim)
            part = total_of(terms).astype(LOW)
        over_x = yield from grid.gather(part, "x")
        over_c = yield from grid.gather(jnp.stack(over_x), "c")
        return over_c

    def reduce_small(part):
        for axis in "cxyz":
            part = grid.all_sum(part, axis)
        return part

    def reduce_all(heights, jobs, far=()):
        made = weight_call(pieces, heights, half, jobs, far=far)
        count = len(heights)
        flows = [Flow(reduce_rows(*v)) for v in zip(made[:count], made[count:])]
        while any(f.pending is not None for f in flows):
            for f in flows:
                if f.pending is not None:
                    f.advance(f.pending)
        return [[v.reshape(-1, half) for v in f.result] for f in flows]

    def join(blocks_):
        return jnp.concatenate([b[c] for c in range(2) for b in blocks_], axis=1).astype(F32)

    jobs = [(0, 0, [act_low], [dy], (0, half)), (1, 0, [attn_low], [grad_branch], (0, half))]
    jobs += [(2 + j, 0, [normed_two], [grad_pre], (j * half, (j + blocks) * half)) for j in range(blocks)]
    first = reduce_all([hidden_each] + [each] * (1 + blocks), jobs)
    total_down, total_out, total_up = join(first[:1]), join(first[1:2]), join(first[2:])
    sums = reduce_small(sums)

    carried = ()
    dkv = [None] * (nz + 1)
    dn, home = {}, []
    for u in reversed(range(nz + 1)):
        outs = bwd_call(
            places[u], [LOW] * len(units[u]), u == nz, u == 0, loop, where_, w_qkv, queries, grad_attn, log_total, delta,
            kv[u], tokens[u], carried,
        )
        dkv[u], carried = outs[2], outs[:2]
        for i, part in enumerate(units[u]):
            dn[part] = outs[3 + i]
        grad_query = outs[-1]
        if u < nz:
            got = grid.swap(dn[u, 1], "y")
            home.append(grid.swap((dn[u, 0].astype(F32) + got.astype(F32)).astype(LOW), "z", u) if u else got)
    (grad_patches,) = call(
        end_kernel, "finish", [struct((rows, width), F32)], [patches, gain, grad_mid, dn[0, 0], *home], rows * width, vmem=40
    )
    jobs = [(0, 0, normed[:1], [grad_query], (0, half)), (1, 0, normed, dkv, (0, half)), (2, 0, normed, dkv, (width, width + half))]
    second = reduce_all([each] * 3, jobs, far=(*normed, *dkv))
    total_qkv = jnp.concatenate([t[c] for t in second for c in range(2)], axis=1).astype(F32)
    return grad_patches, reduce_small(carried[1]), total_qkv, total_out, sums, total_up, total_down


def reduce_packed(
    grid, near, parts_of, w_qkv, left, right, right_given, sums, normed, patches, gain, grad_mid, blocks, each, hidden_each
):
    places, units, where_, queries, grad_attn, log_total, delta, kv, tokens = parts_of
    nz, nblk = grid.n["z"], grid.nblk
    rows, width = patches.shape
    half, hidden, pieces = width // 2, blocks * width, nblk * 2
    ends = lax.optimization_barrier
    z, y, x, c = (grid.at[k] for k in "zyxc")
    f32 = lambda *terms: total_of(terms)

    def pick(array, index):
        return lax.dynamic_index_in_dim(array, index, 0, keepdims=False)

    def send_y(terms):
        cut = [t.reshape(nz, 2, *t.shape[1:]) for t in terms]
        part = lambda i: f32(*(lax.dynamic_index_in_dim(t, i, 1, keepdims=False) for t in cut))
        return grid.swap(part(1 - y).astype(LOW), "y"), part(y)

    def send_z(stays, got):
        total = stays + got.astype(F32)
        return [grid.swap(pick(total, z ^ k).astype(LOW), "z", k) for k in range(1, nz)], pick(total, z)

    def send_x(stays, got):
        mine = f32(stays, *got).astype(LOW)
        return grid.swap(mine, "x"), mine

    def both(mine, got, at):
        return jnp.where(at == 0, jnp.stack([mine, got]), jnp.stack([got, mine]))

    tall = hidden_each
    heights = [2 * each, 2 * each, 2 * each + 16, tall - each]
    jobs = [(hidden, width, j * half, ((j // 2, 0, each, j % 2 * each),)) for j in range(blocks)]
    jobs.append((hidden + width, width, blocks * half, ((2, 0, each, 0),)))
    jobs.append((0, hidden, (blocks + 1) * half, ((2, 0, each, each + 16), (3, each, tall, 0))))
    sums_to = (2, each)

    passed = [grid.swap(v, "c") for v in (left, right_given, sums)]
    carried = ()
    dkv = [None] * (nz + 1)
    dn, over_y, home = {}, {}, {}
    over_x = [None] * 4

    def unit(u):
        nonlocal carried
        outs = bwd_call(
            places[u], [LOW] * len(units[u]), u == nz, u == 0, False, where_, w_qkv, queries, grad_attn, log_total, delta,
            kv[u], tokens[u], carried,
        )
        return outs

    def take(u, outs):
        nonlocal carried
        dkv[u], carried = outs[2], outs[:2]
        for i, part in enumerate(units[u]):
            dn[part] = outs[3 + i]
        if u > 0:
            over_y[u - 1] = grid.swap(dn[u - 1, 1], "y")
        if 0 < u < nz:
            home[u] = grid.swap(f32(dn[u, 0], over_y[u]).astype(LOW), "z", u)
        return outs[-1]

    outs, passed = ends((unit(4), passed))
    take(4, outs)
    made = first_call(near, jobs, sums_to, heights, pieces, half, left, right, passed[0], passed[1], sums, passed[2])
    made, carried = ends((made, carried))
    sent, stay = made[:4], made[4:]
    over_x[0] = grid.swap(sent[0], "x")

    outs, over_y[3], over_x[0] = ends((unit(3), over_y[3], over_x[0]))
    take(3, outs)
    over_x[1] = grid.swap(sent[1], "x")

    outs, over_y[2], over_x[1] = ends((unit(2), over_y[2], over_x[1]))
    take(2, outs)
    over_x[2] = grid.swap(sent[2], "x")

    outs, over_y[1], over_x[2], home[3] = ends((unit(1), over_y[1], over_x[2], home[3]))
    take(1, outs)
    over_x[3] = grid.swap(sent[3], "x")
    ab = [jnp.concatenate(pair, axis=1) for pair in ((stay[0], stay[1]), (over_x[0], over_x[1]))]
    ab_got, ab_stay = send_y(ab)

    grad_query = take(0, unit(0))
    late = carried[1]
    give, keep = second_call(pieces, half, grad_query, late, normed, dkv)
    give, keep, over_y[0], home, ab_got, over_x[3] = ends((give, keep, over_y[0], home, ab_got, over_x[3]))

    w_got = grid.swap(give, "c")
    ab_zs, ab_stay = send_z(ab_stay, ab_got)
    cd = [jnp.concatenate(pair, axis=1) for pair in ((stay[2], stay[3]), (over_x[2], over_x[3]))]
    cd_got, cd_stay = send_y(cd)
    w_x = grid.swap(f32(keep[0], w_got[0]).astype(LOW), "x")
    w_terms = [keep[1], w_got[1]]

    w_x, ab_zs, cd_got = ends((w_x, ab_zs, cd_got))
    w_y, w_stay = send_y([*w_terms, w_x])
    ab_x, ab_mine = send_x(ab_stay, ab_zs)
    cd_zs, cd_stay = send_z(cd_stay, cd_got)

    w_y, ab_x, cd_zs = ends((w_y, ab_x, cd_zs))
    w_zs, w_stay = send_z(w_stay, w_y)
    ab = both(ab_mine, ab_x, x)
    cd_x, cd_mine = send_x(cd_stay, cd_zs)
    ab_c = grid.swap(ab, "c")
    (grad_patches,) = call(
        end_kernel, "finish", [struct((rows, width), F32)],
        [patches, gain, grad_mid, dn[0, 0], *home.values(), over_y[0]], rows * width,
    )

    w_zs, cd_x, ab_c, grad_patches = ends((w_zs, cd_x, ab_c, grad_patches))
    w_x, w_mine = send_x(w_stay, w_zs)
    cd = both(cd_mine, cd_x, x)
    cd_c = grid.swap(cd, "c")
    ab = both(ab, ab_c, c)

    w_x, cd_c = ends((w_x, cd_c))
    w = both(w_mine, w_x, x)
    w_c = grid.swap(w, "c")
    cd = both(cd, cd_c, c)
    w = both(w, w_c, c)

    def rows_of(array, row, height):
        return [array[i, :, row : row + height, :].reshape(2 * height, half) for i in range(2)]

    def join(blocks_):
        return jnp.concatenate([b[i] for i in range(2) for b in blocks_], axis=1).astype(F32)

    total_up = join([rows_of(ab, j * each, each) for j in range(blocks)])
    total_out = join([rows_of(cd, 0, each)])
    down = [jnp.concatenate([cd[i, :, each + 16 : 2 * each + 16], cd[i, :, 2 * each + 16 :]], axis=1) for i in range(2)]
    total_down = jnp.concatenate([d.reshape(2 * tall, half) for d in down], axis=1).astype(F32)
    sums = join([[cd[i, 0, each : each + 8] for i in range(2)]])
    late = join([[w[i, 0, 3 * each : 3 * each + 8] for i in range(2)]])
    thirds = [rows_of(w, j * each, each) for j in range(3)]
    total_qkv = jnp.concatenate([t[i] for t in thirds for i in range(2)], axis=1).astype(F32)
    return grad_patches, late, total_qkv, total_out, sums, total_up, total_down


def local(
    grid,
    patches,
    segment_ids,
    sensor_tags,
    seq_starts,
    ln1_gain,
    ln1_bias,
    w_qkv,
    w_out,
    b_out,
    ln2_gain,
    ln2_bias,
    w_up,
    b_up,
    w_down,
    b_down,
    cotangent,
):
    grid.locate()
    nblk, nz, nx = grid.nblk, grid.n["z"], grid.n["x"]
    loop = nz > 4
    rows, width = patches.shape
    me = lax.axis_index("blk")
    where_ = (segment_ids.reshape(nblk, rows), sensor_tags.reshape(nblk, rows), seq_starts)
    norm_one = (ln1_gain, ln1_bias)


    def place(k, other):
        def chunk():
            blk = lax.axis_index("blk")
            return blk ^ (k * 2 + other)

        return chunk

    units = []
    for u in range(nz + 1):
        parts = ([(u - 1, 1)] if u > 0 else []) + ([(u, 0)] if u < nz else [])
        units.append(parts)
    places = [[place(*p) for p in parts] for parts in units]

    state, queries = None, None
    normed, kv, tokens = [], [], []
    held = {(0, 0): patches}
    for k in range(1, nz):
        held[k, 0] = grid.swap(patches, "z", k)
    for u in range(nz + 1):
        got = grid.swap(held[u, 0], "y") if u < nz else None
        tokens.append([held[p] for p in units[u]])
        outs = fwd_call(places[u], u == 0, u == nz, loop, where_, norm_one, w_qkv, tokens[u], queries, state)
        if u < nz:
            after = held[u + 1, 0] if u < nz - 1 else ()
            got, after, outs = lax.optimization_barrier((got, after, outs))
            held[u, 1] = got
            if u < nz - 1:
                held[u + 1, 0] = after
        state = outs[:3]
        normed.append(outs[3])
        kv.append(outs[4])
        if u == 0:
            queries = outs[5]
    log_total, _, attn_t = state

    near = (w_qkv, queries, *where_, log_total)
    mixed_out, left, right, right_given, grad_mid, grad_attn, delta, sums = mid_call(
        near, attn_t, patches, cotangent, w_out, b_out, ln2_gain, ln2_bias, w_up, b_up, w_down, b_down
    )
    half = width // 2
    hidden = w_down.shape[0]
    blocks = hidden // width
    pieces = nblk * nx
    each = width // pieces
    hidden_each = hidden // pieces
    parts_of = (places, units, where_, queries, grad_attn, log_total, delta, kv, tokens)
    if nz == 4 and nx == 2 and each % 16 == 0:
        summed = reduce_packed(
            grid, near, parts_of, w_qkv, left, right, right_given, sums, normed, patches, ln1_gain, grad_mid, blocks, each, hidden_each
        )
    else:
        summed = reduce_plain(
            grid, loop, parts_of, w_qkv, left, right, sums, normed, patches, ln1_gain, grad_mid, blocks, each, hidden_each
        )
    grad_patches, late, total_qkv, total_out, sums, total_up, total_down = summed

    def own_part(v):
        size = v.size // nblk
        return lax.dynamic_slice_in_dim(v.reshape(-1), me * size, size)

    return (
        mixed_out,
        grad_patches,
        own_part(late[0]),
        own_part(late[1]),
        total_qkv,
        total_out,
        own_part(sums[0]),
        own_part(sums[1]),
        own_part(sums[2]),
        total_up,
        own_part(sums[4:]),
        total_down,
        own_part(sums[3]),
    )


def solution(mesh):
    in_specs = (
        P(("dp", "blk"), None),
        P("dp"),
        P("dp"),
        P(("dp", "blk")),
        *(P(),) * 11,
        P(("dp", "blk"), None),
    )
    out_specs = (
        P(("dp", "blk"), None),
        P(("dp", "blk"), None),
        P("blk"),
        P("blk"),
        P("blk", None),
        P("blk", None),
        P("blk"),
        P("blk"),
        P("blk"),
        P("blk", None),
        P("blk"),
        P("blk", None),
        P("blk"),
    )
    return jax.shard_map(
        partial(local, Grid(mesh)), mesh=mesh, in_specs=in_specs, out_specs=out_specs, check_vma=False
    )
```

```python
import functools
from functools import partial

import jax
import jax.numpy as jnp
from jax import lax
from jax.experimental import pallas as pl
from jax.experimental.pallas import tpu as pltpu
from jax.sharding import PartitionSpec as P

HEADS = 12
EPSILON = 1e-06
MASKED = -1e30
AXES = ("dp", "blk")
NT = (((1,), (1,)), ((), ()))
TN = (((0,), (0,)), ((), ()))
NN = (((1,), (0,)), ((), ()))
VM = pl.BlockSpec(memory_space=pltpu.VMEM)
FAR = pl.BlockSpec(memory_space=pltpu.HBM)
LOW = jnp.bfloat16
F32 = jnp.float32
MIB = 1 << 20
BWD_MIB = 8
SECOND_MIB = 12


def dotf(a, b, dims=NN):
    return lax.dot_general(a, b, dims, preferred_element_type=F32)


def struct(shape, dtype):
    return jax.ShapeDtypeStruct(shape, dtype)


def norm_hat(x):
    center = x - jnp.mean(x, axis=-1, keepdims=True)
    inv = lax.rsqrt(jnp.mean(center * center, axis=-1, keepdims=True) + EPSILON)
    return center * inv, inv


def norm_back(hat, inv, gain, grad):
    g = grad * gain
    return inv * (g - jnp.mean(g, axis=-1, keepdims=True) - hat * jnp.mean(g * hat, axis=-1, keepdims=True))


def call(kernel, name, outs, args, flops, aliases=None, scratch=(), exps=0, vmem=8, far=(), far_outs=()):
    moved = sum(a.size * a.dtype.itemsize for a in args) + sum(o.size * o.dtype.itemsize for o in outs)
    return pl.pallas_call(
        kernel,
        out_shape=[pltpu.HBM(o.shape, o.dtype) if i in far_outs else o for i, o in enumerate(outs)],
        in_specs=[FAR if i in far else VM for i in range(len(args))],
        out_specs=[FAR if i in far_outs else VM for i in range(len(outs))],
        input_output_aliases=aliases or {},
        scratch_shapes=scratch,
        compiler_params=pltpu.CompilerParams(vmem_limit_bytes=vmem * MIB),
        cost_estimate=pl.CostEstimate(flops=int(flops) // 4, bytes_accessed=int(moved) // 4, transcendentals=0),
        name=name,
    )(*(pltpu.with_memory_space_constraint(a, pltpu.HBM) if i in far else a for i, a in enumerate(args)))


def line(ref):
    return ref[...].reshape(1, -1)


def key_bias(chunk, seg_ref, tag_ref, from_ref):
    keys = seg_ref.shape[1]
    me = lax.axis_index("blk")
    base = lax.axis_index("dp") * (seg_ref.shape[0] * keys)

    def column(ref):
        return jnp.broadcast_to(ref[pl.ds(chunk, 1), :], (8, keys)).T[:, 0:1]

    kseg, ktag = column(seg_ref), column(tag_ref)
    qseg, qtag = seg_ref[pl.ds(me, 1), :], tag_ref[pl.ds(me, 1), :]
    pos = base + chunk * keys + lax.broadcasted_iota(jnp.int32, (keys, keys), 0)
    seen = (kseg == qseg) & (pos >= line(from_ref))
    tags = (ktag == qtag) | (qtag == 0) | (ktag == 0)
    return jnp.where(seen & tags, 0.0, MASKED)


def head_lanes(block, odd):
    lane = lax.broadcasted_iota(jnp.int32, block.shape, 1)
    return jnp.where((lane >= 64) if odd else (lane < 64), block, jnp.zeros_like(block))


def over_pairs(heads, loop, body):
    if loop:
        lax.fori_loop(0, heads // 2, lambda i, c: (body(i), c)[1], 0)
    else:
        for i in range(heads // 2):
            body(i)


def fwd_kernel(places, first, last, loop, *refs):
    n = len(places)
    seg_ref, tag_ref, from_ref, gain_ref, shift_ref, w_ref = refs[:6]
    tokens = refs[6 : 6 + n]
    refs = refs[6 + n :]
    if not first:
        q_ref, top_in, sum_in, acc_in = refs[:4]
        refs = refs[4:]
    top_out, sum_out, acc_out = refs[:3]
    normed_far, kv_far = refs[3 : 3 + n], refs[3 + n : 3 + 2 * n]
    if first:
        q_ref = refs[3 + 2 * n]
    bias, normed_out, kv_out, sems = refs[-4:]
    keys, width = tokens[0].shape
    for i in range(n):
        at = pl.ds(i * keys, keys)
        hat = norm_hat(tokens[i][...].astype(F32))[0]
        normed = (hat * line(gain_ref) + line(shift_ref)).astype(LOW)
        normed_out[at, :] = normed
        bias[i] = key_bias(places[i](), seg_ref, tag_ref, from_ref)
    kept = []
    for i in range(n):
        kept.append(pltpu.make_async_copy(normed_out.at[pl.ds(i * keys, keys), :], normed_far[i], sems.at[0, i]))
        kept[-1].start()
    normed = normed_out[...]
    if first:
        q_ref[...] = (dotf(normed, w_ref[:, :width]).astype(LOW) * jnp.asarray(0.125, LOW)).astype(LOW)
    for j in range(2):
        cols = pl.ds(j * width, width)
        kv_out[:, cols] = dotf(normed, w_ref[:, pl.ds((j + 1) * width, width)]).astype(LOW)
    for i in range(n):
        kept.append(pltpu.make_async_copy(kv_out.at[pl.ds(i * keys, keys), :], kv_far[i], sems.at[1, i]))
        kept[-1].start()

    def pair_body(pair):
        lanes = pl.multiple_of(pair * 128, 128)
        at, vat = pl.ds(lanes, 128), pl.ds(width + lanes, 128)
        q_pair = q_ref[:, at]
        v_t = [kv_out[pl.ds(i * keys, keys), vat].T for i in range(n)]
        for odd in range(2):
            h = pair * 2 + odd
            row = pl.ds(h, 1)
            rows = pl.ds(pl.multiple_of(h * 64, 64), 64)
            q_h = head_lanes(q_pair, odd)
            scores = [dotf(kv_out[pl.ds(i * keys, keys), at], q_h, NT) + bias[i] for i in range(n)]
            top = jnp.max(scores[0], axis=0, keepdims=True)
            for s in scores[1:]:
                top = jnp.maximum(top, jnp.max(s, axis=0, keepdims=True))
            if not first:
                old = top_in[row, :]
                top = jnp.maximum(top, old)
                fade = jnp.exp(old - top)
            total = None
            out = None
            for i in range(n):
                p = jnp.exp(scores[i] - top)
                t = jnp.sum(p, axis=0, keepdims=True)
                o = dotf(v_t[i][odd * 64 : odd * 64 + 64], p.astype(LOW))
                total = t if total is None else total + t
                out = o if out is None else out + o
            if not first:
                total = total + sum_in[row, :] * fade
                out = out + acc_in[rows, :] * fade
            if last:
                out = out / total
                top = top + jnp.log(total)
            acc_out[rows, :] = out
            top_out[row, :] = top
            sum_out[row, :] = total

    over_pairs(HEADS, loop, pair_body)
    for copy in kept:
        copy.wait()


def fwd_call(places, first, last, loop, where_, norm, w_qkv, tokens, queries, state):
    keys, width = tokens[0].shape
    n = len(tokens)
    outs = [
        struct((HEADS, keys), F32),
        struct((HEADS, keys), F32),
        struct((width, keys), F32),
        *(struct((keys, width), LOW) for _ in range(n)),
        *(struct((keys, 2 * width), LOW) for _ in range(n)),
    ]
    args = [*where_, *norm, w_qkv, *tokens]
    if first:
        outs.append(struct((keys, width), LOW))
    else:
        args += [queries, *state]
    return call(
        partial(fwd_kernel, places, first, last, loop),
        "attend",
        outs,
        args,
        n * (HEADS * keys * keys * 256 * 8 + keys * width * width * 4),
        aliases={} if first else {len(args) - 3 + i: i for i in range(3)},
        scratch=[
            pltpu.VMEM((n, keys, keys), F32),
            pltpu.VMEM((n * keys, width), LOW),
            pltpu.VMEM((n * keys, 2 * width), LOW),
            pltpu.SemaphoreType.DMA((2, n)),
        ],
        far_outs=tuple(range(3, 3 + 2 * n)),
        exps=n * HEADS * keys * keys,
    )


def bwd_kernel(places, first, last, loop, *refs):
    n = len(places)
    seg_ref, tag_ref, from_ref, w_ref, q_ref, do_ref, lse_ref, delta_ref = refs[:8]
    kvs, tokens = refs[8 : 8 + 2 * n], refs[8 + 2 * n : 8 + 4 * n]
    refs = refs[8 + 4 * n :]
    if not first:
        dq_in, sums_in = refs[:2]
        refs = refs[2:]
    dq_out, sums_out = refs[:2]
    dkvs, dn = refs[2 : 2 + n], refs[2 + n : 2 + 3 * n]
    if last:
        gq_out = refs[2 + 3 * n]
    bias = refs[-1]
    keys, width = tokens[0].shape
    for i in range(n):
        for j in range(2):
            bias[j] = key_bias(places[i][j](), seg_ref, tag_ref, from_ref)
        kv, dkv = kvs[2 * i : 2 * i + 2], dkvs[i]

        def pair_body(pair, fresh=first and i == 0, dq_from=dq_in if not first and i == 0 else dq_out):
            lanes = pl.multiple_of(pair * 128, 128)
            at, vat = pl.ds(lanes, 128), pl.ds(width + lanes, 128)
            q_pair = q_ref[:, at]
            do_pair = do_ref[:, at]
            chunk = [pl.ds(j * keys, keys) for j in range(2)]
            k_t = [kv[j][:, at].T for j in range(2)]
            dk = [None] * 2
            dv = [None] * 2
            for odd in range(2):
                h = pair * 2 + odd
                row = pl.ds(h, 1)
                rows = pl.ds(pl.multiple_of(h * 64, 64), 64)
                q_h = head_lanes(q_pair, odd)
                do_h = head_lanes(do_pair, odd)
                lse = lse_ref[row, :]
                delta = delta_ref[row, :]
                dq = None
                for j in range(2):
                    p = jnp.exp(dotf(kv[j][:, at], q_h, NT) + bias[j] - lse)
                    dp = dotf(kv[j][:, vat], do_h, NT)
                    ds = (p * (dp - delta)).astype(LOW)
                    v_part = dotf(p.astype(LOW), do_h)
                    k_part = dotf(ds, q_h)
                    q_part = dotf(k_t[j][odd * 64 : odd * 64 + 64], ds)
                    dv[j] = v_part if odd == 0 else dv[j] + v_part
                    dk[j] = k_part if odd == 0 else dk[j] + k_part
                    dq = q_part if dq is None else dq + q_part
                if not fresh:
                    dq = dq + dq_from[rows, :]
                dq_out[rows, :] = dq
            for j in range(2):
                dkv[chunk[j], at] = dk[j].astype(LOW)
                dkv[chunk[j], vat] = dv[j].astype(LOW)

        over_pairs(HEADS, loop, pair_body)
        gain_sum = bias_sum = 0.0
        ending = last and i == n - 1
        if ending:
            grad_query = (dq_out[...].T * 0.125).astype(LOW)
            gq_out[...] = grad_query
        for j in range(2):
            part = dotf(dkv[pl.ds(j * keys, keys), :], w_ref[:, width:], NT)
            if ending and j == 1:
                part = part + dotf(grad_query, w_ref[:, :width], NT)
            dn[2 * i + j][...] = part.astype(LOW)
            hat = norm_hat(tokens[2 * i + j][...].astype(F32))[0]
            gain_sum = gain_sum + jnp.sum(part * hat, axis=0, keepdims=True)
            bias_sum = bias_sum + jnp.sum(part, axis=0, keepdims=True)
        if i == 0:
            sums_out[...] = jnp.zeros_like(sums_out) if first else sums_in[...]
        sums_out[0:1, :] += gain_sum
        sums_out[1:2, :] += bias_sum


def bwd_call(slots, first, last, loop, chunks, where_, w_qkv, queries, grad_attn, log_total, delta, carried):
    rows, width = queries.shape
    n = len(slots)
    each = [[chunks[k, other] for other in (1, 0)] for k in slots]
    outs = [struct((width, rows), F32), struct((8, width), F32)]
    outs += [struct((2 * rows, 2 * width), LOW) for _ in slots]
    outs += [struct((rows, width), LOW) for _ in range(2 * n)]
    if last:
        outs.append(struct((rows, width), LOW))
    args = [*where_, w_qkv, queries, grad_attn, log_total, delta]
    args += [c[1] for pair in each for c in pair] + [c[2] for pair in each for c in pair] + list(carried)
    return call(
        partial(bwd_kernel, [[c[0] for c in pair] for pair in each], first, last, loop),
        "attend_back",
        outs,
        args,
        n * 2 * (HEADS * rows * rows * 256 * 14 + rows * width * width * 4),
        aliases={} if first else {len(args) - 2: 0, len(args) - 1: 1},
        scratch=[pltpu.VMEM((2, rows, rows), F32)],
        vmem=BWD_MIB,
    )


def mid_kernel(
    attn_ref, x_ref, dy_ref, wo_ref, bo_ref, g2_ref, s2_ref, wu_ref, bu_ref, wd_ref, bd_ref, *refs
):
    mixed_ref, left_ref, right_ref, given_ref, mid_ref, do_ref, delta_ref, sums_ref = refs[-8:]
    rows, width = x_ref.shape
    hidden = wu_ref.shape[1]
    half, blocks = width // 2, hidden // width
    attn_low = attn_ref[...].T.astype(LOW)
    left_ref[:, pl.ds(hidden + width, width)] = attn_low
    x_mid = x_ref[...].astype(F32) + dotf(attn_low, wo_ref[...]) + line(bo_ref)
    hat, inv = norm_hat(x_mid)
    gain = line(g2_ref)
    normed = (hat * gain + line(s2_ref)).astype(LOW)
    left_ref[:, pl.ds(hidden, width)] = normed
    dy = dy_ref[...]
    dy_full = dy.astype(F32)
    down = None
    grad_normed = None
    for j in range(blocks):
        cols = pl.ds(j * width, width)
        pre = dotf(normed, wu_ref[:, cols]) + bu_ref[cols].reshape(1, -1)
        cdf = 0.5 + 0.5 * lax.erf(pre * (0.5**0.5))
        slope = cdf + pre * (jnp.exp(-0.5 * pre * pre) * 0.3989422804014327)
        act = (pre * cdf).astype(LOW)
        left_ref[:, cols] = act
        part = dotf(act, wd_ref[cols, :])
        down = part if down is None else down + part
        grad_pre = (dotf(dy, wd_ref[cols, :], NT) * slope).astype(LOW)
        right_ref[j * 2 // blocks, :, pl.ds(j % (blocks // 2) * width, width)] = grad_pre
        part = dotf(grad_pre, wu_ref[:, cols], NT)
        grad_normed = part if grad_normed is None else grad_normed + part
        sums_ref[4 + j : 5 + j, :] = jnp.sum(grad_pre.astype(F32), axis=0, keepdims=True)
    mixed_ref[...] = (x_mid + down + line(bd_ref)).astype(LOW)
    grad_mid = dy_full + norm_back(hat, inv, gain, grad_normed)
    mid_ref[...] = grad_mid
    branch = grad_mid.astype(LOW)
    for c in range(2):
        right_ref[c, :, pl.ds(hidden // 2, half)] = branch[:, c * half : (c + 1) * half]
        right_ref[c, :, pl.ds(hidden // 2 + half, half)] = dy[:, c * half : (c + 1) * half]
    given_ref[...] = right_ref[1 - lax.axis_index("dp") % 2]
    grad_attn = dotf(branch, wo_ref[...], NT).astype(LOW)
    do_ref[...] = grad_attn
    product = grad_attn.astype(F32).T * attn_ref[...]
    size = width // HEADS
    for h in range(HEADS):
        delta_ref[h : h + 1, :] = jnp.sum(product[h * size : (h + 1) * size, :], axis=0, keepdims=True)
    sums_ref[0:1, :] = jnp.sum(branch.astype(F32), axis=0, keepdims=True)
    sums_ref[1:2, :] = jnp.sum(grad_normed * hat, axis=0, keepdims=True)
    sums_ref[2:3, :] = jnp.sum(grad_normed, axis=0, keepdims=True)
    sums_ref[3:4, :] = jnp.sum(dy_full, axis=0, keepdims=True)


def mid_call(near, attn_t, patches, cotangent, w_out, b_out, g2, s2, w_up, b_up, w_down, b_down):
    rows, width = patches.shape
    hidden = w_up.shape[1]
    outs = [
        struct((rows, width), LOW),
        struct((rows, hidden + 2 * width), LOW),
        struct((2, rows, hidden // 2 + width), LOW),
        struct((rows, hidden // 2 + width), LOW),
        struct((rows, width), F32),
        struct((rows, width), LOW),
        struct((HEADS, rows), F32),
        struct((4 + hidden // width, width), F32),
    ]
    args = [attn_t, patches, cotangent, w_out, b_out, g2, s2, w_up, b_up, w_down, b_down, *near]
    return call(mid_kernel, "middle", outs, args, rows * width * (hidden * 8 + width * 4), exps=rows * hidden * 4, vmem=16)


def halves_of_x(acc, pieces, half):
    acc = acc.reshape(pieces // 2, 2, -1, half)
    first = lax.axis_index("dp") // 2 == 0
    own = jnp.where(first, acc[:, 0], acc[:, 1]).astype(LOW)
    other = jnp.where(first, acc[:, 1], acc[:, 0]).astype(LOW)
    return other, own


def first_kernel(jobs, sums_to, pieces, left_ref, right_ref, left_got, right_got, sums_ref, sums_got, *refs):
    c = lax.axis_index("dp") % 2
    parts = 1 + max(job[-1][-1][0] for job in jobs)
    outs = refs[-2 * parts :]
    half = outs[0].shape[2]
    width = 2 * half
    for left, total, right, targets in jobs:
        cols = pl.ds(right, half)
        each = total * 2 // (2 * pieces)
        for begin in range(0, total, width):
            rows = pl.ds(left + begin, width)
            acc = dotf(left_ref[:, rows], right_ref[c, :, cols], TN) + dotf(left_got[:, rows], right_got[:, cols], TN)
            pair = halves_of_x(acc, width // each, half)
            blks = width // each // 2
            at = pl.ds(begin // each // 2, blks)
            for part, low, high, row in targets:
                for side in range(2):
                    outs[part + side * parts][at, pl.ds(row, high - low), :] = pair[side][:, low:high, :]
    mine = sums_ref[:, pl.ds(pl.multiple_of(c * half, 128), half)] + sums_got[:, pl.ds(pl.multiple_of(c * half, 128), half)]
    mine = jnp.concatenate([mine, jnp.zeros_like(mine)], axis=0).astype(LOW)
    part, row = sums_to
    for side in range(2):
        out = outs[part + side * parts]
        out[:, pl.ds(row, 16), :] = jnp.broadcast_to(mine[None], (out.shape[0],) + mine.shape)


def first_call(near, jobs, sums_to, heights, pieces, half, left, right, left_got, right_got, sums, sums_got):
    outs = [struct((pieces // 2, h, half), LOW) for h in heights] * 2
    args = [left, right, left_got, right_got, sums, sums_got, *near]
    return call(
        partial(first_kernel, jobs, sums_to, pieces), "weights", outs, args, sum(h for h in heights) * pieces * half * 1024, vmem=12
    )


def second_kernel(pieces, units, *refs):
    me = lax.axis_index("dp") % 2
    gq_ref, sums_ref = refs[:2]
    normed, dkv = refs[2 : 2 + 2 * units], refs[2 + 2 * units : 2 + 3 * units]
    outs = ((refs[-2], 1 - me), (refs[-1], me))
    keys, width = normed[0].shape
    half = width // 2
    each = width // pieces
    for out, c in outs:
        for block in range(3):
            if block == 0:
                cols = pl.ds(pl.multiple_of(c * half, 128), half)
                acc = dotf(normed[1][...], gq_ref[:, cols], TN)
            else:
                cols = pl.ds(pl.multiple_of((block - 1) * width + c * half, 128), half)
                acc = None
                for i in range(2 * units):
                    term = dotf(normed[i][...], dkv[i // 2][pl.ds(i % 2 * keys, keys), cols], TN)
                    acc = term if acc is None else acc + term
            pair = halves_of_x(acc, pieces, half)
            for side in range(2):
                out[side, :, pl.ds(block * each, each), :] = pair[side]
        mine = sums_ref[:, pl.ds(pl.multiple_of(c * half, 128), half)]
        mine = jnp.concatenate([mine, jnp.zeros_like(mine)], axis=0).astype(LOW)
        for side in range(2):
            out[side, :, pl.ds(3 * each, 16), :] = jnp.broadcast_to(mine[None], (out.shape[1],) + mine.shape)


def second_call(pieces, half, grad_query, sums, normed, dkv):
    units = len(dkv)
    each = 2 * half // pieces
    args = [grad_query, sums, *normed, *dkv]
    return call(
        partial(second_kernel, pieces, units),
        "weights",
        [struct((2, pieces // 2, 3 * each + 16, half), LOW)] * 2,
        args,
        sum(v.shape[0] for v in normed) * 2 * half * 4 * half,
        vmem=SECOND_MIB,
    )


def weight_kernel(spec, sums_at, pieces, far, count, *refs):
    me = lax.axis_index("dp") % 2
    ins = list(refs[:count])
    outs = refs[count : len(refs) - len(far) - (1 if far else 0)]
    waits = {}
    if far:
        sems = refs[-1]
        for i, number in enumerate(far):
            held = refs[len(refs) - 1 - len(far) + i]
            waits[number] = pltpu.make_async_copy(ins[number], held, sems.at[i])
            waits[number].start()
            ins[number] = held
    parts = len(outs) // 2
    for part, row, lefts, rights, starts in spec:
        for number in (*lefts, *rights):
            if number in waits:
                waits.pop(number).wait()
        for given in (True, False):
            c = 1 - me if given else me
            out = outs[part + (0 if given else parts)]
            half = out.shape[2]
            total = ins[lefts[0]].shape[1]
            each = total // pieces
            step = min(total, 768)
            cols = pl.ds(pl.multiple_of(jnp.where(c == 0, starts[0], starts[1]), 128), half)
            for begin in range(0, total, step):
                acc = None
                for left, right in zip(lefts, rights):
                    term = dotf(ins[left][:, pl.ds(begin, step)], ins[right][:, cols], TN)
                    acc = term if acc is None else acc + term
                acc = acc.reshape(step // each, each, half)
                out[pl.ds(begin // each, step // each), pl.ds(row, each), :] = acc.astype(LOW)
    if sums_at is not None:
        part, row, number = sums_at
        for given in (True, False):
            c = 1 - me if given else me
            out = outs[part + (0 if given else parts)]
            half = out.shape[2]
            mine = ins[number][:, pl.ds(pl.multiple_of(c * half, 128), half)]
            mine = jnp.concatenate([mine, jnp.zeros_like(mine)], axis=0).astype(LOW)
            out[:, pl.ds(row, 16), :] = jnp.broadcast_to(mine[None], (pieces,) + mine.shape)


def weight_call(pieces, heights, half, jobs, sums=None, sums_at=None, far=()):
    spec, args, flops = [], [], 0

    def index(array):
        for i, known in enumerate(args):
            if known is array:
                return i
        args.append(array)
        return len(args) - 1

    for part, row, lefts, rights, starts in jobs:
        spec.append((part, row, [index(v) for v in lefts], [index(v) for v in rights], starts))
        flops += sum(a.shape[0] for a in lefts) * lefts[0].shape[1] * half * 4
    if sums is not None:
        sums_at = (*sums_at, index(sums))
    far = tuple(i for i, a in enumerate(args) if any(a is v for v in far))
    scratch = [pltpu.VMEM(args[i].shape, args[i].dtype) for i in far]
    if far:
        scratch.append(pltpu.SemaphoreType.DMA((len(far),)))
    outs = [struct((pieces, h, half), LOW) for h in heights] * 2
    return call(
        partial(weight_kernel, spec, sums_at, pieces, far, len(args)),
        "weights",
        outs,
        args,
        flops,
        scratch=scratch,
        far=far,
        vmem=8 + sum(args[i].size * 2 for i in far) // MIB,
    )


def mix_kernel(ops, *refs):
    dp, blk = lax.axis_index("dp"), lax.axis_index("blk")
    at = {"x": dp // 2, "c": dp % 2, "z": blk // 2, "y": blk % 2}
    for kind, ins, outs, more in ops:
        terms = [refs[i] if lead is None else refs[i].at[lead] for i, lead in ins]
        outs = [refs[i] for i in outs]
        if kind == "add":
            outs[0][...] = total_of([t[...] for t in terms]).astype(LOW)
        elif kind == "y":
            size, row = len(terms) // (more or 1), 0
            for begin in range(0, len(terms), size):
                group = terms[begin : begin + size]
                some = pl.ds(row, group[0].shape[1])
                row += group[0].shape[1]
                for q in range(outs[0].shape[0]):
                    outs[0][q, some, :] = total_of([t[2 * q + 1 - at["y"]] for t in group]).astype(LOW)
                    outs[1][q, some, :] = total_of([t[2 * q + at["y"]] for t in group])
        elif kind == "z":
            for k in range(1, terms[0].shape[0]):
                outs[k - 1][...] = total_of([t[at["z"] ^ k] for t in terms]).astype(LOW)
            outs[-1][...] = total_of([t[at["z"]] for t in terms])
        elif kind == "pair":
            outs[0][at[more]] = terms[0][...]
            outs[0][1 - at[more]] = terms[1][...]
        else:
            for row, height, number, starts in more[0]:
                some = pl.ds(row, height)
                for x in range(terms[0].shape[0]):
                    mine, other = terms[0][x, some, :].astype(F32), terms[1][x, some, :].astype(F32)
                    first = at["c"] == 0
                    to = pl.ds(x * height, height)
                    width = mine.shape[1]
                    outs[number][to, pl.ds(starts[0], width)] = jnp.where(first, mine, other)
                    outs[number][to, pl.ds(starts[1], width)] = jnp.where(first, other, mine)
            for number, row, source in more[2] if len(more) > 2 else ():
                size = outs[number].shape[0]
                if size % 128:
                    values = pltpu.roll(outs[source][row : row + 1, :], outs[source].shape[1] - blk * size, 1)
                    outs[number][...] = values[:, :size].reshape(size)
                else:
                    each = outs[source].shape[1] // size
                    values = outs[source][pl.ds(row + blk // each, 1), pl.ds(pl.multiple_of(blk % each * size, 128), size)]
                    outs[number][...] = values.reshape(size)


def mix(*ops):
    args, outs, spec, counts = [], [], [], []

    def index(array):
        for i, known in enumerate(args):
            if known is array:
                return i
        args.append(array)
        return len(args) - 1

    for kind, terms, *more in ops:
        ins = [(index(t[0]), t[1]) if isinstance(t, tuple) else (index(t), None) for t in terms]
        shape = args[ins[0][0]].shape
        shape = shape if ins[0][1] is None else shape[1:]
        if kind == "add":
            new = [struct(shape, LOW)]
        elif kind == "y":
            groups = more[0] if more else 1
            firsts = [ins[i * (len(ins) // groups)] for i in range(groups)]
            height = sum(args[i].shape[-2] for i, _ in firsts)
            shape = (shape[0] // 2, height, shape[2])
            new = [struct(shape, LOW), struct(shape, F32)]
        elif kind == "z":
            new = [struct(shape[1:], LOW)] * (shape[0] - 1) + [struct(shape[1:], F32)]
        elif kind == "pair":
            new = [struct((2, *shape), LOW)]
        else:
            new = [struct(v, F32) for v in more[0][1]]
        spec.append((kind, ins, range(len(outs), len(outs) + len(new)), more[0] if more else None))
        counts.append(len(new))
        outs += new
    spec = [(kind, ins, [len(args) + i for i in out], more) for kind, ins, out, more in spec]
    made = call(partial(mix_kernel, spec), "mix", outs, args, sum(o.size for o in outs), vmem=8)
    split = []
    for n in counts:
        split.append(made[0] if n == 1 else tuple(made[:n]))
        made = made[n:]
    return split


def end_kernel(x_ref, gain_ref, mid_ref, *refs):
    out = refs[-1]
    grad = refs[0][...].astype(F32)
    for ref in refs[1:-1]:
        grad = grad + ref[...].astype(F32)
    hat, inv = norm_hat(x_ref[...].astype(F32))
    out[...] = mid_ref[...] + norm_back(hat, inv, line(gain_ref), grad)


class Grid:
    def __init__(self, mesh):
        ndp, nblk = mesh.shape["dp"], mesh.shape["blk"]
        self.n = {"c": 2, "x": ndp // 2, "y": 2, "z": nblk // 2}
        self.nblk, self.ndp = nblk, ndp

    def locate(self):
        dp, blk = lax.axis_index("dp"), lax.axis_index("blk")
        self.at = {"x": dp // 2, "c": dp % 2, "z": blk // 2, "y": blk % 2}

    def swap(self, value, axis, k=1):
        pairs = []
        n = self.n
        for x in range(n["x"]):
            for c in range(2):
                for z in range(n["z"]):
                    for y in range(2):
                        here = {"x": x, "c": c, "z": z, "y": y}
                        there = dict(here)
                        there[axis] ^= k
                        flat = [((p["x"] * 2 + p["c"]) * n["z"] + p["z"]) * 2 + p["y"] for p in (here, there)]
                        pairs.append(tuple(flat))
        return lax.ppermute(value, AXES, pairs)

    def all_sum(self, value, axis):
        step = 1
        while step < self.n[axis]:
            value = value + self.swap(value, axis, step)
            step *= 2
        return value

    def scatter(self, array, axis, dim):
        piece = lambda k: lax.dynamic_index_in_dim(array, self.at[axis] ^ k, dim, keepdims=False)
        got = []
        if self.n[axis] > 1:
            got = yield [self.swap(piece(k), axis, k) for k in range(1, self.n[axis])]
        return [piece(0), *got]

    def gather(self, value, axis):
        n = self.n[axis]
        if n == 1:
            return [value]
        got = yield [self.swap(value, axis, k) for k in range(1, n)]
        slots = [value, *got]
        at = self.at[axis]
        out = []
        for p in range(n):
            piece = slots[p]
            for i in range(1, n):
                piece = jnp.where(at == i, slots[p ^ i], piece)
            out.append(piece)
        return out


class Flow:
    def __init__(self, steps):
        self.steps, self.result = steps, None
        self.advance(None, True)

    def advance(self, value, first=False):
        try:
            self.pending = next(self.steps) if first else self.steps.send(value)
        except StopIteration as stop:
            self.pending, self.result = None, stop.value


def tie(flows, *values):
    flows = [f for f in flows if f.pending is not None]
    pending, values = lax.optimization_barrier(([f.pending for f in flows], values))
    for flow, value in zip(flows, pending):
        flow.advance(value)
    return values


def total_of(terms):
    return functools.reduce(lambda a, b: a + b, [t.astype(F32) for t in terms])


def reduce_plain(grid, loop, parts_of, w_qkv, left, right, sums, normed, patches, gain, grad_mid, blocks, each, hidden_each):
    chunks, where_, queries, grad_attn, log_total, delta = parts_of
    nz, nx = grid.n["z"], grid.n["x"]
    rows, width = patches.shape
    half, hidden, pieces = width // 2, blocks * width, grid.nblk * nx
    act_low, normed_two, attn_low = left[:, :hidden], left[:, hidden : hidden + width], left[:, hidden + width :]
    grad_pre, grad_branch, dy = (
        jnp.concatenate([right[c, :, a:b] for c in range(2)], axis=1)
        for a, b in ((0, hidden // 2), (hidden // 2, hidden // 2 + half), (hidden // 2 + half, hidden // 2 + width))
    )

    def reduce_rows(given, kept):
        got = yield grid.swap(given, "c")
        part = (kept.astype(F32) + got.astype(F32)).astype(LOW).reshape(nz, 2, nx, -1, kept.shape[-1])
        for axis, dim in (("x", 2), ("y", 1), ("z", 0)):
            terms = yield from grid.scatter(part, axis, dim)
            part = total_of(terms).astype(LOW)
        over_x = yield from grid.gather(part, "x")
        over_c = yield from grid.gather(jnp.stack(over_x), "c")
        return over_c

    def reduce_small(part):
        for axis in "cxyz":
            part = grid.all_sum(part, axis)
        return part

    def reduce_all(heights, jobs, far=()):
        made = weight_call(pieces, heights, half, jobs, far=far)
        count = len(heights)
        flows = [Flow(reduce_rows(*v)) for v in zip(made[:count], made[count:])]
        while any(f.pending is not None for f in flows):
            for f in flows:
                if f.pending is not None:
                    f.advance(f.pending)
        return [[v.reshape(-1, half) for v in f.result] for f in flows]

    def join(blocks_):
        return jnp.concatenate([b[c] for c in range(2) for b in blocks_], axis=1).astype(F32)

    jobs = [(0, 0, [act_low], [dy], (0, half)), (1, 0, [attn_low], [grad_branch], (0, half))]
    jobs += [(2 + j, 0, [normed_two], [grad_pre], (j * half, (j + blocks) * half)) for j in range(blocks)]
    first = reduce_all([hidden_each] + [each] * (1 + blocks), jobs)
    total_down, total_out, total_up = join(first[:1]), join(first[1:2]), join(first[2:])
    sums = reduce_small(sums)

    carried = ()
    dkv, home = [None] * nz, []
    for k in reversed(range(nz)):
        outs = bwd_call([k], k == nz - 1, k == 0, loop, chunks, where_, w_qkv, queries, grad_attn, log_total, delta, carried)
        carried, dkv[k] = outs[:2], outs[2]
        other, own, grad_query = outs[3], outs[4], outs[-1]
        got = grid.swap(other, "y")
        home.append(grid.swap((own.astype(F32) + got.astype(F32)).astype(LOW), "z", k) if k else got)
    (grad_patches,) = call(
        end_kernel, "finish", [struct((rows, width), F32)], [patches, gain, grad_mid, own, *home], rows * width, vmem=40
    )
    own_first = normed[1]
    lefts = [jnp.concatenate(normed[2 * k : 2 * k + 2], axis=0) for k in range(nz)]
    jobs = [(0, 0, [own_first], [grad_query], (0, half)), (1, 0, lefts, dkv, (0, half)), (2, 0, lefts, dkv, (width, width + half))]
    second = reduce_all([each] * 3, jobs, far=(own_first, *lefts, *dkv))
    total_qkv = jnp.concatenate([t[c] for t in second for c in range(2)], axis=1).astype(F32)
    late, me = reduce_small(carried[1]), lax.axis_index("blk")

    def own_part(v):
        size = v.size // grid.nblk
        return lax.dynamic_slice_in_dim(v.reshape(-1), me * size, size)

    small = [own_part(v) for v in (late[0], late[1], sums[0], sums[1], sums[2], sums[3], sums[4:])]
    return grad_patches, total_qkv, total_out, total_up, total_down, small


def reduce_packed(
    grid, near, parts_of, w_qkv, left, right, right_given, sums, normed, patches, gain, grad_mid, blocks, each, hidden_each
):
    chunks, where_, queries, grad_attn, log_total, delta = parts_of
    nz, nblk = grid.n["z"], grid.nblk
    rows, width = patches.shape
    half, hidden, pieces = width // 2, blocks * width, nblk * 2
    ends = lax.optimization_barrier
    over_z = lambda sends: [grid.swap(v, "z", k + 1) for k, v in enumerate(sends)]
    tall = hidden_each
    low = tall // 3
    heights = [blocks * each, each + 16 + low, tall - low]
    jobs = [(hidden, width, j * half, ((0, 0, each, j * each),)) for j in range(blocks)]
    jobs.append((hidden + width, width, blocks * half, ((1, 0, each, 0),)))
    jobs.append((0, hidden, (blocks + 1) * half, ((1, 0, low, each + 16), (2, low, tall, 0))))
    sums_to = (1, each)

    def unit(slots, carried):
        return bwd_call(
            slots, not carried, 0 in slots, False, chunks, where_, w_qkv, queries, grad_attn, log_total, delta, carried
        )

    passed = [grid.swap(v, "c") for v in (left, right_given, sums)]
    dkv = [None] * nz
    outs, passed = ends((unit([3], ()), passed))
    carried, dkv[3], other3, own3 = outs[:2], *outs[2:]
    y3 = grid.swap(other3, "y")
    made = first_call(near, jobs, sums_to, heights, pieces, half, left, right, passed[0], passed[1], sums, passed[2])
    made, carried = ends((made, carried))
    a_x = grid.swap(made[0], "x")

    outs, y3, a_x, *sent = ends((unit([2, 1], carried), y3, a_x, made[1], made[2]))
    carried, dkv[2], dkv[1], other2, own2, other1, own1 = outs[:2], *outs[2:]
    (z3,) = mix(("add", [own3, y3]))
    c_x, z3, y2, y1 = grid.swap(sent[0], "x"), grid.swap(z3, "z", 3), grid.swap(other2, "y"), grid.swap(other1, "y")

    outs, y2, y1, c_x, z3, sent = ends((unit([0], carried), y2, y1, c_x, z3, sent[1]))
    carried, dkv[0], other0, own0, grad_query = outs[:2], *outs[2:]
    z2, z1, (a_y, a_stay) = mix(("add", [own2, y2]), ("add", [own1, y1]), ("y", [made[3], a_x]))
    d_x, z2, z1, a_y, y0 = (
        grid.swap(sent, "x"), grid.swap(z2, "z", 2), grid.swap(z1, "z", 1), grid.swap(a_y, "y"), grid.swap(other0, "y")
    )
    give, keep = second_call(pieces, half, grad_query, carried[1], normed, dkv)
    give, keep, d_x, a_y, z2, z1, y0 = ends((give, keep, d_x, a_y, z2, z1, y0))

    w_got = grid.swap(give, "c")
    (*a_zs, a_stay), (c_y, c_stay) = mix(("z", [a_stay, a_y]), ("y", [made[4], c_x, made[5], d_x], 2))
    c_y, a_zs = grid.swap(c_y, "y"), over_z(a_zs)
    (w_x,) = mix(("add", [(keep, 0), (w_got, 0)]))
    w_x = grid.swap(w_x, "x")
    w_x, c_y, a_zs = ends((w_x, c_y, a_zs))

    (w_y, w_stay), (*c_zs, c_stay), a = mix(
        ("y", [(keep, 1), (w_got, 1), w_x]), ("z", [c_stay, c_y]), ("add", [a_stay, *a_zs])
    )
    w_y, c_zs, a_x = grid.swap(w_y, "y"), over_z(c_zs), grid.swap(a, "x")
    (grad_patches,) = call(
        end_kernel, "finish", [struct((rows, width), F32)], [patches, gain, grad_mid, own0, z3, z2, z1, y0], rows * width,
    )
    w_y, a_x, grad_patches = ends((w_y, a_x, grad_patches))
    (*w_zs, w_stay), a = mix(("z", [w_stay, w_y]), ("pair", [a, a_x], "x"))
    w_zs, c_zs, a_c = ends((over_z(w_zs), c_zs, grid.swap(a, "c")))

    each2, tall2 = 2 * each, 2 * tall
    up_out = [(j * each, each, 0, (j * half, (j + blocks) * half)) for j in range(blocks)]
    w, rest, total_up = mix(
        ("add", [w_stay, *w_zs]), ("add", [c_stay, *c_zs]), ("out", [a, a_c], (up_out, [(each2, hidden)]))
    )
    w_x, rest_x = ends((grid.swap(w, "x"), grid.swap(rest, "x")))

    w, rest = mix(("pair", [w, w_x], "x"), ("pair", [rest, rest_x], "x"))
    w_c, rest_c = grid.swap(w, "c"), grid.swap(rest, "c")
    own, own_hidden = (width // nblk,), (hidden // nblk,)
    ends_out = [(0, each, 0, (0, half)), (each + 16, tall, 1, (0, half)), (each, 16, 2, (0, half))]
    small = [(3, 0, 2), (4, 1, 2), (5, 2, 2), (6, 3, 2), (7, 4, 2)]
    last_out = [(j * each, each, 0, (j * width, j * width + half)) for j in range(3)] + [(3 * each, 16, 1, (0, half))]
    (total_out, total_down, _, b_out, gain_two, bias_two, b_down, b_up), (total_qkv, _, gain_one, bias_one) = mix(
        ("out", [rest, rest_c], (ends_out, [(each2, width), (tall2, width), (32, width), own, own, own, own, own_hidden], small)),
        ("out", [w, w_c], (last_out, [(each2, 3 * width), (32, width), own, own], [(2, 0, 1), (3, 1, 1)])),
    )
    small = (gain_one, bias_one, b_out, gain_two, bias_two, b_down, b_up)
    return grad_patches, total_qkv, total_out, total_up, total_down, small


def local(
    grid,
    patches,
    segment_ids,
    sensor_tags,
    seq_starts,
    ln1_gain,
    ln1_bias,
    w_qkv,
    w_out,
    b_out,
    ln2_gain,
    ln2_bias,
    w_up,
    b_up,
    w_down,
    b_down,
    cotangent,
):
    grid.locate()
    nblk, nz, nx = grid.nblk, grid.n["z"], grid.n["x"]
    loop = nz > 4
    rows, width = patches.shape
    me = lax.axis_index("blk")
    where_ = (segment_ids.reshape(nblk, rows), sensor_tags.reshape(nblk, rows), seq_starts)
    norm_one = (ln1_gain, ln1_bias)


    def place(k, other):
        def chunk():
            blk = lax.axis_index("blk")
            return blk ^ (k * 2 + other)

        return chunk

    units = []
    for u in range(nz + 1):
        parts = ([(u - 1, 1)] if u > 0 else []) + ([(u, 0)] if u < nz else [])
        units.append(parts)
    places = [[place(*p) for p in parts] for parts in units]

    state, queries = None, None
    normed, chunks, tokens = {}, {}, []
    held = {(0, 0): patches}
    for k in range(1, nz):
        held[k, 0] = grid.swap(patches, "z", k)
    for u in range(nz + 1):
        got = grid.swap(held[u, 0], "y") if u < nz else None
        tokens.append([held[p] for p in units[u]])
        outs = fwd_call(places[u], u == 0, u == nz, loop, where_, norm_one, w_qkv, tokens[u], queries, state)
        if u < nz:
            after = held[u + 1, 0] if u < nz - 1 else ()
            got, after, outs = lax.optimization_barrier((got, after, outs))
            held[u, 1] = got
            if u < nz - 1:
                held[u + 1, 0] = after
        state = outs[:3]
        n = len(units[u])
        for i, part in enumerate(units[u]):
            normed[part] = outs[3 + i]
            chunks[part] = (places[u][i], outs[3 + n + i], tokens[u][i])
        if u == 0:
            queries = outs[-1]
    log_total, _, attn_t = state

    near = (w_qkv, queries, *where_, log_total)
    mixed_out, left, right, right_given, grad_mid, grad_attn, delta, sums = mid_call(
        near, attn_t, patches, cotangent, w_out, b_out, ln2_gain, ln2_bias, w_up, b_up, w_down, b_down
    )
    half = width // 2
    hidden = w_down.shape[0]
    blocks = hidden // width
    pieces = nblk * nx
    each = width // pieces
    hidden_each = hidden // pieces
    normed = [normed[k, other] for k in range(nz) for other in (1, 0)]
    parts_of = (chunks, where_, queries, grad_attn, log_total, delta)
    if nz == 4 and nx == 2 and each % 16 == 0:
        summed = reduce_packed(
            grid, near, parts_of, w_qkv, left, right, right_given, sums, normed, patches, ln1_gain, grad_mid, blocks, each, hidden_each
        )
    else:
        summed = reduce_plain(
            grid, loop, parts_of, w_qkv, left, right, sums, normed, patches, ln1_gain, grad_mid, blocks, each, hidden_each
        )
    grad_patches, total_qkv, total_out, total_up, total_down, small = summed
    gain_one, bias_one, total_bout, gain_two, bias_two, total_bdown, total_bup = small
    return (
        mixed_out,
        grad_patches,
        gain_one,
        bias_one,
        total_qkv,
        total_out,
        total_bout,
        gain_two,
        bias_two,
        total_up,
        total_bup,
        total_down,
        total_bdown,
    )


def solution(mesh):
    in_specs = (
        P(("dp", "blk"), None),
        P("dp"),
        P("dp"),
        P(("dp", "blk")),
        *(P(),) * 11,
        P(("dp", "blk"), None),
    )
    out_specs = (
        P(("dp", "blk"), None),
        P(("dp", "blk"), None),
        P("blk"),
        P("blk"),
        P("blk", None),
        P("blk", None),
        P("blk"),
        P("blk"),
        P("blk"),
        P("blk", None),
        P("blk"),
        P("blk", None),
        P("blk"),
    )
    return jax.shard_map(
        partial(local, Grid(mesh)), mesh=mesh, in_specs=in_specs, out_specs=out_specs, check_vma=False
    )
```

```python
import functools
from functools import partial

import jax
import jax.numpy as jnp
from jax import lax
from jax.experimental import pallas as pl
from jax.experimental.pallas import tpu as pltpu
from jax.sharding import PartitionSpec as P

HEADS = 12
EPSILON = 1e-06
MASKED = -1e30
AXES = ("dp", "blk")
NT = (((1,), (1,)), ((), ()))
TN = (((0,), (0,)), ((), ()))
NN = (((1,), (0,)), ((), ()))
VM = pl.BlockSpec(memory_space=pltpu.VMEM)
FAR = pl.BlockSpec(memory_space=pltpu.HBM)
LOW = jnp.bfloat16
F32 = jnp.float32
MIB = 1 << 20
BWD_MIB = 8
SECOND_MIB = 12


def dotf(a, b, dims=NN):
    return lax.dot_general(a, b, dims, preferred_element_type=F32)


def struct(shape, dtype):
    return jax.ShapeDtypeStruct(shape, dtype)


def norm_hat(x):
    center = x - jnp.mean(x, axis=-1, keepdims=True)
    inv = lax.rsqrt(jnp.mean(center * center, axis=-1, keepdims=True) + EPSILON)
    return center * inv, inv


def norm_back(hat, inv, gain, grad):
    g = grad * gain
    return inv * (g - jnp.mean(g, axis=-1, keepdims=True) - hat * jnp.mean(g * hat, axis=-1, keepdims=True))


def call(kernel, name, outs, args, flops, aliases=None, scratch=(), exps=0, vmem=8, far=(), far_outs=()):
    moved = sum(a.size * a.dtype.itemsize for a in args) + sum(o.size * o.dtype.itemsize for o in outs)
    return pl.pallas_call(
        kernel,
        out_shape=[pltpu.HBM(o.shape, o.dtype) if i in far_outs else o for i, o in enumerate(outs)],
        in_specs=[FAR if i in far else VM for i in range(len(args))],
        out_specs=[FAR if i in far_outs else VM for i in range(len(outs))],
        input_output_aliases=aliases or {},
        scratch_shapes=scratch,
        compiler_params=pltpu.CompilerParams(vmem_limit_bytes=vmem * MIB),
        cost_estimate=pl.CostEstimate(flops=int(flops) // 4, bytes_accessed=int(moved) // 4, transcendentals=0),
        name=name,
    )(*(pltpu.with_memory_space_constraint(a, pltpu.HBM) if i in far else a for i, a in enumerate(args)))


def line(ref):
    return ref[...].reshape(1, -1)


def key_bias(chunk, seg_ref, tag_ref, from_ref):
    keys = seg_ref.shape[1]
    me = lax.axis_index("blk")
    base = lax.axis_index("dp") * (seg_ref.shape[0] * keys)

    def column(ref):
        return jnp.broadcast_to(ref[pl.ds(chunk, 1), :], (8, keys)).T[:, 0:1]

    kseg, ktag = column(seg_ref), column(tag_ref)
    qseg, qtag = seg_ref[pl.ds(me, 1), :], tag_ref[pl.ds(me, 1), :]
    pos = base + chunk * keys + lax.broadcasted_iota(jnp.int32, (keys, keys), 0)
    seen = (kseg == qseg) & (pos >= line(from_ref))
    tags = (ktag == qtag) | (qtag == 0) | (ktag == 0)
    return jnp.where(seen & tags, 0.0, MASKED)


def head_lanes(block, odd):
    lane = lax.broadcasted_iota(jnp.int32, block.shape, 1)
    return jnp.where((lane >= 64) if odd else (lane < 64), block, jnp.zeros_like(block))


def over_pairs(heads, loop, body):
    if loop:
        lax.fori_loop(0, heads // 2, lambda i, c: (body(i), c)[1], 0)
    else:
        for i in range(heads // 2):
            body(i)


def fwd_kernel(places, first, last, loop, *refs):
    n = len(places)
    seg_ref, tag_ref, from_ref, gain_ref, shift_ref, w_ref = refs[:6]
    tokens = refs[6 : 6 + n]
    refs = refs[6 + n :]
    if not first:
        q_ref, top_in, sum_in, acc_in = refs[:4]
        refs = refs[4:]
    top_out, sum_out, acc_out = refs[:3]
    normed_far, kv_far = refs[3 : 3 + n], refs[3 + n : 3 + 2 * n]
    if first:
        q_ref = refs[3 + 2 * n]
    bias, normed_out, kv_out, sems = refs[-4:]
    keys, width = tokens[0].shape
    for i in range(n):
        at = pl.ds(i * keys, keys)
        hat = norm_hat(tokens[i][...].astype(F32))[0]
        normed = (hat * line(gain_ref) + line(shift_ref)).astype(LOW)
        normed_out[at, :] = normed
        bias[i] = key_bias(places[i](), seg_ref, tag_ref, from_ref)
    kept = []
    for i in range(n):
        kept.append(pltpu.make_async_copy(normed_out.at[pl.ds(i * keys, keys), :], normed_far[i], sems.at[0, i]))
        kept[-1].start()
    normed = normed_out[...]
    if first:
        q_ref[...] = (dotf(normed, w_ref[:, :width]).astype(LOW) * jnp.asarray(0.125, LOW)).astype(LOW)
    for j in range(2):
        cols = pl.ds(j * width, width)
        kv_out[:, cols] = dotf(normed, w_ref[:, pl.ds((j + 1) * width, width)]).astype(LOW)
    for i in range(n):
        kept.append(pltpu.make_async_copy(kv_out.at[pl.ds(i * keys, keys), :], kv_far[i], sems.at[1, i]))
        kept[-1].start()

    def pair_body(pair):
        lanes = pl.multiple_of(pair * 128, 128)
        at, vat = pl.ds(lanes, 128), pl.ds(width + lanes, 128)
        q_pair = q_ref[:, at]
        v_t = [kv_out[pl.ds(i * keys, keys), vat].T for i in range(n)]
        for odd in range(2):
            h = pair * 2 + odd
            row = pl.ds(h, 1)
            rows = pl.ds(pl.multiple_of(h * 64, 64), 64)
            q_h = head_lanes(q_pair, odd)
            scores = [dotf(kv_out[pl.ds(i * keys, keys), at], q_h, NT) + bias[i] for i in range(n)]
            top = jnp.max(scores[0], axis=0, keepdims=True)
            for s in scores[1:]:
                top = jnp.maximum(top, jnp.max(s, axis=0, keepdims=True))
            if not first:
                old = top_in[row, :]
                top = jnp.maximum(top, old)
                fade = jnp.exp(old - top)
            total = None
            out = None
            for i in range(n):
                p = jnp.exp(scores[i] - top)
                t = jnp.sum(p, axis=0, keepdims=True)
                o = dotf(v_t[i][odd * 64 : odd * 64 + 64], p.astype(LOW))
                total = t if total is None else total + t
                out = o if out is None else out + o
            if not first:
                total = total + sum_in[row, :] * fade
                out = out + acc_in[rows, :] * fade
            if last:
                out = out / total
                top = top + jnp.log(total)
            acc_out[rows, :] = out
            top_out[row, :] = top
            sum_out[row, :] = total

    over_pairs(HEADS, loop, pair_body)
    for copy in kept:
        copy.wait()


def fwd_call(places, first, last, loop, where_, norm, w_qkv, tokens, queries, state):
    keys, width = tokens[0].shape
    n = len(tokens)
    outs = [
        struct((HEADS, keys), F32),
        struct((HEADS, keys), F32),
        struct((width, keys), F32),
        *(struct((keys, width), LOW) for _ in range(n)),
        *(struct((keys, 2 * width), LOW) for _ in range(n)),
    ]
    args = [*where_, *norm, w_qkv, *tokens]
    if first:
        outs.append(struct((keys, width), LOW))
    else:
        args += [queries, *state]
    return call(
        partial(fwd_kernel, places, first, last, loop),
        "attend",
        outs,
        args,
        n * (HEADS * keys * keys * 256 * 8 + keys * width * width * 4),
        aliases={} if first else {len(args) - 3 + i: i for i in range(3)},
        scratch=[
            pltpu.VMEM((n, keys, keys), F32),
            pltpu.VMEM((n * keys, width), LOW),
            pltpu.VMEM((n * keys, 2 * width), LOW),
            pltpu.SemaphoreType.DMA((2, n)),
        ],
        far_outs=tuple(range(3, 3 + 2 * n)),
        exps=n * HEADS * keys * keys,
    )


def bwd_kernel(places, first, last, loop, *refs):
    n = len(places)
    seg_ref, tag_ref, from_ref, w_ref, q_ref, do_ref, lse_ref, delta_ref = refs[:8]
    kvs, tokens = refs[8 : 8 + 2 * n], refs[8 + 2 * n : 8 + 4 * n]
    refs = refs[8 + 4 * n :]
    if not first:
        dq_in, sums_in = refs[:2]
        refs = refs[2:]
    dq_out, sums_out = refs[:2]
    dkvs, dn = refs[2 : 2 + n], refs[2 + n : 2 + 3 * n]
    if last:
        gq_out = refs[2 + 3 * n]
    bias = refs[-1]
    keys, width = tokens[0].shape
    for i in range(n):
        for j in range(2):
            bias[j] = key_bias(places[i][j](), seg_ref, tag_ref, from_ref)
        kv, dkv = kvs[2 * i : 2 * i + 2], dkvs[i]

        def pair_body(pair, fresh=first and i == 0, dq_from=dq_in if not first and i == 0 else dq_out):
            lanes = pl.multiple_of(pair * 128, 128)
            at, vat = pl.ds(lanes, 128), pl.ds(width + lanes, 128)
            q_pair = q_ref[:, at]
            do_pair = do_ref[:, at]
            chunk = [pl.ds(j * keys, keys) for j in range(2)]
            k_t = [kv[j][:, at].T for j in range(2)]
            dk = [None] * 2
            dv = [None] * 2
            for odd in range(2):
                h = pair * 2 + odd
                row = pl.ds(h, 1)
                rows = pl.ds(pl.multiple_of(h * 64, 64), 64)
                q_h = head_lanes(q_pair, odd)
                do_h = head_lanes(do_pair, odd)
                lse = lse_ref[row, :]
                delta = delta_ref[row, :]
                dq = None
                for j in range(2):
                    p = jnp.exp(dotf(kv[j][:, at], q_h, NT) + bias[j] - lse)
                    dp = dotf(kv[j][:, vat], do_h, NT)
                    ds = (p * (dp - delta)).astype(LOW)
                    v_part = dotf(p.astype(LOW), do_h)
                    k_part = dotf(ds, q_h)
                    q_part = dotf(k_t[j][odd * 64 : odd * 64 + 64], ds)
                    dv[j] = v_part if odd == 0 else dv[j] + v_part
                    dk[j] = k_part if odd == 0 else dk[j] + k_part
                    dq = q_part if dq is None else dq + q_part
                if not fresh:
                    dq = dq + dq_from[rows, :]
                dq_out[rows, :] = dq
            for j in range(2):
                dkv[chunk[j], at] = dk[j].astype(LOW)
                dkv[chunk[j], vat] = dv[j].astype(LOW)

        over_pairs(HEADS, loop, pair_body)
        gain_sum = bias_sum = 0.0
        ending = last and i == n - 1
        if ending:
            grad_query = (dq_out[...].T * 0.125).astype(LOW)
            gq_out[...] = grad_query
        for j in range(2):
            part = dotf(dkv[pl.ds(j * keys, keys), :], w_ref[:, width:], NT)
            if ending and j == 1:
                part = part + dotf(grad_query, w_ref[:, :width], NT)
            dn[2 * i + j][...] = part.astype(LOW)
            hat = norm_hat(tokens[2 * i + j][...].astype(F32))[0]
            gain_sum = gain_sum + jnp.sum(part * hat, axis=0, keepdims=True)
            bias_sum = bias_sum + jnp.sum(part, axis=0, keepdims=True)
        if i == 0:
            sums_out[...] = jnp.zeros_like(sums_out) if first else sums_in[...]
        sums_out[0:1, :] += gain_sum
        sums_out[1:2, :] += bias_sum


def bwd_call(slots, first, last, loop, chunks, where_, w_qkv, queries, grad_attn, log_total, delta, carried):
    rows, width = queries.shape
    n = len(slots)
    each = [[chunks[k, other] for other in (1, 0)] for k in slots]
    outs = [struct((width, rows), F32), struct((8, width), F32)]
    outs += [struct((2 * rows, 2 * width), LOW) for _ in slots]
    outs += [struct((rows, width), LOW) for _ in range(2 * n)]
    if last:
        outs.append(struct((rows, width), LOW))
    args = [*where_, w_qkv, queries, grad_attn, log_total, delta]
    args += [c[1] for pair in each for c in pair] + [c[2] for pair in each for c in pair] + list(carried)
    return call(
        partial(bwd_kernel, [[c[0] for c in pair] for pair in each], first, last, loop),
        "attend_back",
        outs,
        args,
        n * 2 * (HEADS * rows * rows * 256 * 14 + rows * width * width * 4),
        aliases={} if first else {len(args) - 2: 0, len(args) - 1: 1},
        scratch=[pltpu.VMEM((2, rows, rows), F32)],
        vmem=BWD_MIB,
    )


def mid_kernel(
    attn_ref, x_ref, dy_ref, wo_ref, bo_ref, g2_ref, s2_ref, wu_ref, bu_ref, wd_ref, bd_ref, *refs
):
    mixed_ref, left_ref, right_ref, given_ref, mid_ref, do_ref, delta_ref, sums_ref = refs[-8:]
    rows, width = x_ref.shape
    hidden = wu_ref.shape[1]
    half, blocks = width // 2, hidden // width
    attn_low = attn_ref[...].T.astype(LOW)
    left_ref[:, pl.ds(hidden + width, width)] = attn_low
    x_mid = x_ref[...].astype(F32) + dotf(attn_low, wo_ref[...]) + line(bo_ref)
    hat, inv = norm_hat(x_mid)
    gain = line(g2_ref)
    normed = (hat * gain + line(s2_ref)).astype(LOW)
    left_ref[:, pl.ds(hidden, width)] = normed
    dy = dy_ref[...]
    dy_full = dy.astype(F32)
    down = None
    grad_normed = None
    for j in range(blocks):
        cols = pl.ds(j * width, width)
        pre = dotf(normed, wu_ref[:, cols]) + bu_ref[cols].reshape(1, -1)
        cdf = 0.5 + 0.5 * lax.erf(pre * (0.5**0.5))
        slope = cdf + pre * (jnp.exp(-0.5 * pre * pre) * 0.3989422804014327)
        act = (pre * cdf).astype(LOW)
        left_ref[:, cols] = act
        part = dotf(act, wd_ref[cols, :])
        down = part if down is None else down + part
        grad_pre = (dotf(dy, wd_ref[cols, :], NT) * slope).astype(LOW)
        right_ref[j * 2 // blocks, :, pl.ds(j % (blocks // 2) * width, width)] = grad_pre
        part = dotf(grad_pre, wu_ref[:, cols], NT)
        grad_normed = part if grad_normed is None else grad_normed + part
        sums_ref[4 + j : 5 + j, :] = jnp.sum(grad_pre.astype(F32), axis=0, keepdims=True)
    mixed_ref[...] = (x_mid + down + line(bd_ref)).astype(LOW)
    grad_mid = dy_full + norm_back(hat, inv, gain, grad_normed)
    mid_ref[...] = grad_mid
    branch = grad_mid.astype(LOW)
    for c in range(2):
        right_ref[c, :, pl.ds(hidden // 2, half)] = branch[:, c * half : (c + 1) * half]
        right_ref[c, :, pl.ds(hidden // 2 + half, half)] = dy[:, c * half : (c + 1) * half]
    given_ref[...] = right_ref[1 - lax.axis_index("dp") % 2]
    grad_attn = dotf(branch, wo_ref[...], NT).astype(LOW)
    do_ref[...] = grad_attn
    product = grad_attn.astype(F32).T * attn_ref[...]
    size = width // HEADS
    for h in range(HEADS):
        delta_ref[h : h + 1, :] = jnp.sum(product[h * size : (h + 1) * size, :], axis=0, keepdims=True)
    sums_ref[0:1, :] = jnp.sum(branch.astype(F32), axis=0, keepdims=True)
    sums_ref[1:2, :] = jnp.sum(grad_normed * hat, axis=0, keepdims=True)
    sums_ref[2:3, :] = jnp.sum(grad_normed, axis=0, keepdims=True)
    sums_ref[3:4, :] = jnp.sum(dy_full, axis=0, keepdims=True)


def mid_call(near, attn_t, patches, cotangent, w_out, b_out, g2, s2, w_up, b_up, w_down, b_down):
    rows, width = patches.shape
    hidden = w_up.shape[1]
    outs = [
        struct((rows, width), LOW),
        struct((rows, hidden + 2 * width), LOW),
        struct((2, rows, hidden // 2 + width), LOW),
        struct((rows, hidden // 2 + width), LOW),
        struct((rows, width), F32),
        struct((rows, width), LOW),
        struct((HEADS, rows), F32),
        struct((4 + hidden // width, width), F32),
    ]
    args = [attn_t, patches, cotangent, w_out, b_out, g2, s2, w_up, b_up, w_down, b_down, *near]
    return call(mid_kernel, "middle", outs, args, rows * width * (hidden * 8 + width * 4), exps=rows * hidden * 4, vmem=16)


def halves_of_x(acc, pieces, half):
    acc = acc.reshape(pieces // 2, 2, -1, half)
    first = lax.axis_index("dp") // 2 == 0
    own = jnp.where(first, acc[:, 0], acc[:, 1]).astype(LOW)
    other = jnp.where(first, acc[:, 1], acc[:, 0]).astype(LOW)
    return other, own


def first_kernel(jobs, sums_to, pieces, left_ref, right_ref, left_got, right_got, sums_ref, sums_got, *refs):
    c = lax.axis_index("dp") % 2
    parts = 1 + max(target[0] for job in jobs for target in job[-1])
    outs = refs[-2 * parts :]
    half = outs[0].shape[2]
    width = 2 * half
    for left, total, right, targets in jobs:
        cols = pl.ds(right, half)
        each = total * 2 // (2 * pieces)
        for begin in range(0, total, width):
            rows = pl.ds(left + begin, width)
            acc = dotf(left_ref[:, rows], right_ref[c, :, cols], TN) + dotf(left_got[:, rows], right_got[:, cols], TN)
            pair = halves_of_x(acc, width // each, half)
            blks = width // each // 2
            at = pl.ds(begin // each // 2, blks)
            for part, low, high, row in targets:
                for side in range(2):
                    outs[part + side * parts][at, pl.ds(row, high - low), :] = pair[side][:, low:high, :]
    mine = sums_ref[:, pl.ds(pl.multiple_of(c * half, 128), half)] + sums_got[:, pl.ds(pl.multiple_of(c * half, 128), half)]
    mine = jnp.concatenate([mine, jnp.zeros_like(mine)], axis=0).astype(LOW)
    part, row = sums_to
    for side in range(2):
        out = outs[part + side * parts]
        out[:, pl.ds(row, 16), :] = jnp.broadcast_to(mine[None], (out.shape[0],) + mine.shape)


def first_call(near, jobs, sums_to, heights, pieces, half, left, right, left_got, right_got, sums, sums_got):
    outs = [struct((pieces // 2, h, half), LOW) for h in heights] * 2
    args = [left, right, left_got, right_got, sums, sums_got, *near]
    return call(
        partial(first_kernel, jobs, sums_to, pieces), "weights", outs, args, sum(h for h in heights) * pieces * half * 1024, vmem=12
    )


def second_kernel(pieces, units, *refs):
    me = lax.axis_index("dp") % 2
    gq_ref, sums_ref = refs[:2]
    normed, dkv = refs[2 : 2 + 2 * units], refs[2 + 2 * units : 2 + 3 * units]
    outs = ((refs[-2], 1 - me), (refs[-1], me))
    keys, width = normed[0].shape
    half = width // 2
    each = width // pieces
    for out, c in outs:
        for block in range(3):
            if block == 0:
                cols = pl.ds(pl.multiple_of(c * half, 128), half)
                acc = dotf(normed[1][...], gq_ref[:, cols], TN)
            else:
                cols = pl.ds(pl.multiple_of((block - 1) * width + c * half, 128), half)
                acc = None
                for i in range(2 * units):
                    term = dotf(normed[i][...], dkv[i // 2][pl.ds(i % 2 * keys, keys), cols], TN)
                    acc = term if acc is None else acc + term
            pair = halves_of_x(acc, pieces, half)
            for side in range(2):
                out[side, :, pl.ds(block * each, each), :] = pair[side]
        mine = sums_ref[:, pl.ds(pl.multiple_of(c * half, 128), half)]
        mine = jnp.concatenate([mine, jnp.zeros_like(mine)], axis=0).astype(LOW)
        for side in range(2):
            out[side, :, pl.ds(3 * each, 16), :] = jnp.broadcast_to(mine[None], (out.shape[1],) + mine.shape)


def second_call(pieces, half, grad_query, sums, normed, dkv):
    units = len(dkv)
    each = 2 * half // pieces
    args = [grad_query, sums, *normed, *dkv]
    return call(
        partial(second_kernel, pieces, units),
        "weights",
        [struct((2, pieces // 2, 3 * each + 16, half), LOW)] * 2,
        args,
        sum(v.shape[0] for v in normed) * 2 * half * 4 * half,
        vmem=SECOND_MIB,
    )


def weight_kernel(spec, sums_at, pieces, far, count, *refs):
    me = lax.axis_index("dp") % 2
    ins = list(refs[:count])
    outs = refs[count : len(refs) - len(far) - (1 if far else 0)]
    waits = {}
    if far:
        sems = refs[-1]
        for i, number in enumerate(far):
            held = refs[len(refs) - 1 - len(far) + i]
            waits[number] = pltpu.make_async_copy(ins[number], held, sems.at[i])
            waits[number].start()
            ins[number] = held
    parts = len(outs) // 2
    for part, row, lefts, rights, starts in spec:
        for number in (*lefts, *rights):
            if number in waits:
                waits.pop(number).wait()
        for given in (True, False):
            c = 1 - me if given else me
            out = outs[part + (0 if given else parts)]
            half = out.shape[2]
            total = ins[lefts[0]].shape[1]
            each = total // pieces
            step = min(total, 768)
            cols = pl.ds(pl.multiple_of(jnp.where(c == 0, starts[0], starts[1]), 128), half)
            for begin in range(0, total, step):
                acc = None
                for left, right in zip(lefts, rights):
                    term = dotf(ins[left][:, pl.ds(begin, step)], ins[right][:, cols], TN)
                    acc = term if acc is None else acc + term
                acc = acc.reshape(step // each, each, half)
                out[pl.ds(begin // each, step // each), pl.ds(row, each), :] = acc.astype(LOW)
    if sums_at is not None:
        part, row, number = sums_at
        for given in (True, False):
            c = 1 - me if given else me
            out = outs[part + (0 if given else parts)]
            half = out.shape[2]
            mine = ins[number][:, pl.ds(pl.multiple_of(c * half, 128), half)]
            mine = jnp.concatenate([mine, jnp.zeros_like(mine)], axis=0).astype(LOW)
            out[:, pl.ds(row, 16), :] = jnp.broadcast_to(mine[None], (pieces,) + mine.shape)


def weight_call(pieces, heights, half, jobs, sums=None, sums_at=None, far=()):
    spec, args, flops = [], [], 0

    def index(array):
        for i, known in enumerate(args):
            if known is array:
                return i
        args.append(array)
        return len(args) - 1

    for part, row, lefts, rights, starts in jobs:
        spec.append((part, row, [index(v) for v in lefts], [index(v) for v in rights], starts))
        flops += sum(a.shape[0] for a in lefts) * lefts[0].shape[1] * half * 4
    if sums is not None:
        sums_at = (*sums_at, index(sums))
    far = tuple(i for i, a in enumerate(args) if any(a is v for v in far))
    scratch = [pltpu.VMEM(args[i].shape, args[i].dtype) for i in far]
    if far:
        scratch.append(pltpu.SemaphoreType.DMA((len(far),)))
    outs = [struct((pieces, h, half), LOW) for h in heights] * 2
    return call(
        partial(weight_kernel, spec, sums_at, pieces, far, len(args)),
        "weights",
        outs,
        args,
        flops,
        scratch=scratch,
        far=far,
        vmem=8 + sum(args[i].size * 2 for i in far) // MIB,
    )


def mix_kernel(ops, *refs):
    dp, blk = lax.axis_index("dp"), lax.axis_index("blk")
    at = {"x": dp // 2, "c": dp % 2, "z": blk // 2, "y": blk % 2}
    for kind, ins, outs, more in ops:
        terms = [refs[i] if lead is None else refs[i].at[lead] for i, lead in ins]
        if kind == "cut":
            whole = total_of([t[...] for t in terms])
            outs_here = [refs[i] for i in outs]
            outs_here[0][...] = whole[:, :more, :].astype(LOW)
            outs_here[1][...] = whole[:, more:, :]
            continue
        outs = [refs[i] for i in outs]
        if kind == "add":
            outs[0][...] = total_of([t[...] for t in terms]).astype(LOW)
        elif kind == "y":
            size, row = len(terms) // (more or 1), 0
            for begin in range(0, len(terms), size):
                group = terms[begin : begin + size]
                some = pl.ds(row, group[0].shape[1])
                row += group[0].shape[1]
                for q in range(outs[0].shape[0]):
                    outs[0][q, some, :] = total_of([t[2 * q + 1 - at["y"]] for t in group]).astype(LOW)
                    outs[1][q, some, :] = total_of([t[2 * q + at["y"]] for t in group])
        elif kind == "z":
            size, row = len(terms) // (more or 1), 0
            for begin in range(0, len(terms), size):
                group = terms[begin : begin + size]
                some = pl.ds(row, group[0].shape[1])
                row += group[0].shape[1]
                for k in range(1, group[0].shape[0]):
                    outs[k - 1][some, :] = total_of([t[at["z"] ^ k] for t in group]).astype(LOW)
                outs[-1][some, :] = total_of([t[at["z"]] for t in group])
        elif kind == "pair":
            outs[0][at[more]] = terms[0][...]
            outs[0][1 - at[more]] = terms[1][...]
        else:
            for source, row, height, number, starts, offset, stride in more[0]:
                some = pl.ds(row, height)
                own, got = terms[2 * source : 2 * source + 2]
                for x in range(own.shape[0]):
                    mine, other = own[x, some, :].astype(F32), got[x, some, :].astype(F32)
                    first = at["c"] == 0
                    to = pl.ds(x * stride + offset, height)
                    width = mine.shape[1]
                    outs[number][to, pl.ds(starts[0], width)] = jnp.where(first, mine, other)
                    outs[number][to, pl.ds(starts[1], width)] = jnp.where(first, other, mine)
            for number, row, source in more[2] if len(more) > 2 else ():
                size = outs[number].shape[0]
                if size % 128:
                    values = pltpu.roll(outs[source][row : row + 1, :], outs[source].shape[1] - blk * size, 1)
                    outs[number][...] = values[:, :size].reshape(size)
                else:
                    each = outs[source].shape[1] // size
                    values = outs[source][pl.ds(row + blk // each, 1), pl.ds(pl.multiple_of(blk % each * size, 128), size)]
                    outs[number][...] = values.reshape(size)


def mix(*ops):
    args, outs, spec, counts = [], [], [], []

    def index(array):
        for i, known in enumerate(args):
            if known is array:
                return i
        args.append(array)
        return len(args) - 1

    for kind, terms, *more in ops:
        ins = [(index(t[0]), t[1]) if isinstance(t, tuple) else (index(t), None) for t in terms]
        shape = args[ins[0][0]].shape
        shape = shape if ins[0][1] is None else shape[1:]
        if kind == "add":
            new = [struct(shape, LOW)]
        elif kind == "y":
            groups = more[0] if more else 1
            firsts = [ins[i * (len(ins) // groups)] for i in range(groups)]
            height = sum(args[i].shape[-2] for i, _ in firsts)
            shape = (shape[0] // 2, height, shape[2])
            new = [struct(shape, LOW), struct(shape, F32)]
        elif kind == "z":
            groups = more[0] if more else 1
            height = sum(args[ins[i * (len(ins) // groups)][0]].shape[-2] for i in range(groups))
            new = [struct((height, shape[2]), LOW)] * (shape[0] - 1) + [struct((height, shape[2]), F32)]
        elif kind == "cut":
            new = [struct((shape[0], more[0], shape[2]), LOW), struct((shape[0], shape[1] - more[0], shape[2]), F32)]
        elif kind == "pair":
            new = [struct((2, *shape), LOW)]
        else:
            new = [struct(v, F32) for v in more[0][1]]
        spec.append((kind, ins, range(len(outs), len(outs) + len(new)), more[0] if more else None))
        counts.append(len(new))
        outs += new
    spec = [(kind, ins, [len(args) + i for i in out], more) for kind, ins, out, more in spec]
    made = call(partial(mix_kernel, spec), "mix", outs, args, sum(o.size for o in outs), vmem=8)
    split = []
    for n in counts:
        split.append(made[0] if n == 1 else tuple(made[:n]))
        made = made[n:]
    return split


def end_kernel(x_ref, gain_ref, mid_ref, *refs):
    out = refs[-1]
    grad = refs[0][...].astype(F32)
    for ref in refs[1:-1]:
        grad = grad + ref[...].astype(F32)
    hat, inv = norm_hat(x_ref[...].astype(F32))
    out[...] = mid_ref[...] + norm_back(hat, inv, line(gain_ref), grad)


class Grid:
    def __init__(self, mesh):
        ndp, nblk = mesh.shape["dp"], mesh.shape["blk"]
        self.n = {"c": 2, "x": ndp // 2, "y": 2, "z": nblk // 2}
        self.nblk, self.ndp = nblk, ndp

    def locate(self):
        dp, blk = lax.axis_index("dp"), lax.axis_index("blk")
        self.at = {"x": dp // 2, "c": dp % 2, "z": blk // 2, "y": blk % 2}

    def swap(self, value, axis, k=1):
        pairs = []
        n = self.n
        for x in range(n["x"]):
            for c in range(2):
                for z in range(n["z"]):
                    for y in range(2):
                        here = {"x": x, "c": c, "z": z, "y": y}
                        there = dict(here)
                        there[axis] ^= k
                        flat = [((p["x"] * 2 + p["c"]) * n["z"] + p["z"]) * 2 + p["y"] for p in (here, there)]
                        pairs.append(tuple(flat))
        return lax.ppermute(value, AXES, pairs)

    def all_sum(self, value, axis):
        step = 1
        while step < self.n[axis]:
            value = value + self.swap(value, axis, step)
            step *= 2
        return value

    def scatter(self, array, axis, dim):
        piece = lambda k: lax.dynamic_index_in_dim(array, self.at[axis] ^ k, dim, keepdims=False)
        got = []
        if self.n[axis] > 1:
            got = yield [self.swap(piece(k), axis, k) for k in range(1, self.n[axis])]
        return [piece(0), *got]

    def gather(self, value, axis):
        n = self.n[axis]
        if n == 1:
            return [value]
        got = yield [self.swap(value, axis, k) for k in range(1, n)]
        slots = [value, *got]
        at = self.at[axis]
        out = []
        for p in range(n):
            piece = slots[p]
            for i in range(1, n):
                piece = jnp.where(at == i, slots[p ^ i], piece)
            out.append(piece)
        return out


class Flow:
    def __init__(self, steps):
        self.steps, self.result = steps, None
        self.advance(None, True)

    def advance(self, value, first=False):
        try:
            self.pending = next(self.steps) if first else self.steps.send(value)
        except StopIteration as stop:
            self.pending, self.result = None, stop.value


def tie(flows, *values):
    flows = [f for f in flows if f.pending is not None]
    pending, values = lax.optimization_barrier(([f.pending for f in flows], values))
    for flow, value in zip(flows, pending):
        flow.advance(value)
    return values


def total_of(terms):
    return functools.reduce(lambda a, b: a + b, [t.astype(F32) for t in terms])


def reduce_plain(grid, loop, parts_of, w_qkv, left, right, sums, normed, patches, gain, grad_mid, blocks, each, hidden_each):
    chunks, where_, queries, grad_attn, log_total, delta = parts_of
    nz, nx = grid.n["z"], grid.n["x"]
    rows, width = patches.shape
    half, hidden, pieces = width // 2, blocks * width, grid.nblk * nx
    act_low, normed_two, attn_low = left[:, :hidden], left[:, hidden : hidden + width], left[:, hidden + width :]
    grad_pre, grad_branch, dy = (
        jnp.concatenate([right[c, :, a:b] for c in range(2)], axis=1)
        for a, b in ((0, hidden // 2), (hidden // 2, hidden // 2 + half), (hidden // 2 + half, hidden // 2 + width))
    )

    def reduce_rows(given, kept):
        got = yield grid.swap(given, "c")
        part = (kept.astype(F32) + got.astype(F32)).astype(LOW).reshape(nz, 2, nx, -1, kept.shape[-1])
        for axis, dim in (("x", 2), ("y", 1), ("z", 0)):
            terms = yield from grid.scatter(part, axis, dim)
            part = total_of(terms).astype(LOW)
        over_x = yield from grid.gather(part, "x")
        over_c = yield from grid.gather(jnp.stack(over_x), "c")
        return over_c

    def reduce_small(part):
        for axis in "cxyz":
            part = grid.all_sum(part, axis)
        return part

    def reduce_all(heights, jobs, far=()):
        made = weight_call(pieces, heights, half, jobs, far=far)
        count = len(heights)
        flows = [Flow(reduce_rows(*v)) for v in zip(made[:count], made[count:])]
        while any(f.pending is not None for f in flows):
            for f in flows:
                if f.pending is not None:
                    f.advance(f.pending)
        return [[v.reshape(-1, half) for v in f.result] for f in flows]

    def join(blocks_):
        return jnp.concatenate([b[c] for c in range(2) for b in blocks_], axis=1).astype(F32)

    jobs = [(0, 0, [act_low], [dy], (0, half)), (1, 0, [attn_low], [grad_branch], (0, half))]
    jobs += [(2 + j, 0, [normed_two], [grad_pre], (j * half, (j + blocks) * half)) for j in range(blocks)]
    first = reduce_all([hidden_each] + [each] * (1 + blocks), jobs)
    total_down, total_out, total_up = join(first[:1]), join(first[1:2]), join(first[2:])
    sums = reduce_small(sums)

    carried = ()
    dkv, home = [None] * nz, []
    for k in reversed(range(nz)):
        outs = bwd_call([k], k == nz - 1, k == 0, loop, chunks, where_, w_qkv, queries, grad_attn, log_total, delta, carried)
        carried, dkv[k] = outs[:2], outs[2]
        other, own, grad_query = outs[3], outs[4], outs[-1]
        got = grid.swap(other, "y")
        home.append(grid.swap((own.astype(F32) + got.astype(F32)).astype(LOW), "z", k) if k else got)
    (grad_patches,) = call(
        end_kernel, "finish", [struct((rows, width), F32)], [patches, gain, grad_mid, own, *home], rows * width, vmem=40
    )
    own_first = normed[1]
    lefts = [jnp.concatenate(normed[2 * k : 2 * k + 2], axis=0) for k in range(nz)]
    jobs = [(0, 0, [own_first], [grad_query], (0, half)), (1, 0, lefts, dkv, (0, half)), (2, 0, lefts, dkv, (width, width + half))]
    second = reduce_all([each] * 3, jobs, far=(own_first, *lefts, *dkv))
    total_qkv = jnp.concatenate([t[c] for t in second for c in range(2)], axis=1).astype(F32)
    late, me = reduce_small(carried[1]), lax.axis_index("blk")

    def own_part(v):
        size = v.size // grid.nblk
        return lax.dynamic_slice_in_dim(v.reshape(-1), me * size, size)

    small = [own_part(v) for v in (late[0], late[1], sums[0], sums[1], sums[2], sums[3], sums[4:])]
    return grad_patches, total_qkv, total_out, total_up, total_down, small


def reduce_packed(
    grid, near, parts_of, w_qkv, left, right, right_given, sums, normed, patches, gain, grad_mid, blocks, each, hidden_each
):
    chunks, where_, queries, grad_attn, log_total, delta = parts_of
    nz, nblk = grid.n["z"], grid.nblk
    rows, width = patches.shape
    half, hidden, pieces = width // 2, blocks * width, nblk * 2
    ends = lax.optimization_barrier
    over_z = lambda sends: [grid.swap(v, "z", k + 1) for k, v in enumerate(sends)]
    tall = hidden_each
    low = tall // 3
    heights = [(blocks - 1) * each, each + 16 + low, tall - low, each]
    jobs = [(hidden, width, (blocks - 1) * half, ((3, 0, each, 0),))]
    jobs += [(hidden, width, j * half, ((0, 0, each, j * each),)) for j in range(blocks - 1)]
    jobs.append((hidden + width, width, blocks * half, ((1, 0, each, 0),)))
    jobs.append((0, hidden, (blocks + 1) * half, ((1, 0, low, each + 16), (2, low, tall, 0))))
    sums_to = (1, each)

    def unit(slots, carried):
        return bwd_call(
            slots, not carried, 0 in slots, False, chunks, where_, w_qkv, queries, grad_attn, log_total, delta, carried
        )

    passed = [grid.swap(v, "c") for v in (left, right_given, sums)]
    dkv = [None] * nz
    outs, passed = ends((unit([3], ()), passed))
    carried, dkv[3], other3, own3 = outs[:2], *outs[2:]
    y3 = grid.swap(other3, "y")
    made = first_call(near, jobs, sums_to, heights, pieces, half, left, right, passed[0], passed[1], sums, passed[2])
    made, carried = ends((made, carried))
    ((e_y, e_stay),) = mix(("y", [made[3], made[7]], 2))
    a_x, e_y = grid.swap(made[0], "x"), grid.swap(e_y, "y")

    outs, y3, a_x, e_y, *sent = ends((unit([2, 1], carried), y3, a_x, e_y, made[1], made[2]))
    carried, dkv[2], dkv[1], other2, own2, other1, own1 = outs[:2], *outs[2:]
    z3, (e_x, e_stay) = mix(("add", [own3, y3]), ("cut", [e_stay, e_y], each))
    c_x, z3, y2, y1 = grid.swap(sent[0], "x"), grid.swap(z3, "z", 3), grid.swap(other2, "y"), grid.swap(other1, "y")
    e_x = grid.swap(e_x, "x")

    outs, y2, y1, c_x, z3, e_x, sent = ends((unit([0], carried), y2, y1, c_x, z3, e_x, sent[1]))
    carried, dkv[0], other0, own0, grad_query = outs[:2], *outs[2:]
    z2, z1, (a_y, a_stay) = mix(("add", [own2, y2]), ("add", [own1, y1]), ("y", [made[4], a_x, made[5], c_x], 2))
    d_x, z2, z1, a_y = grid.swap(sent, "x"), grid.swap(z2, "z", 2), grid.swap(z1, "z", 1), grid.swap(a_y, "y")
    give, keep = second_call(pieces, half, grad_query, carried[1], normed, dkv)
    give, keep, d_x, a_y, z2, z1 = ends((give, keep, d_x, a_y, z2, z1))

    w_got = grid.swap(give, "c")
    (*a_zs, a_stay), (d_y, d_stay) = mix(("z", [a_stay, a_y, e_stay, e_x], 2), ("y", [made[6], d_x]))
    d_y, a_zs = grid.swap(d_y, "y"), over_z(a_zs)
    (w_x,) = mix(("add", [(keep, 0), (w_got, 0)]))
    w_x = grid.swap(w_x, "x")
    w_x, d_y, a_zs = ends((w_x, d_y, a_zs))

    (w_y, w_stay), (*d_zs, d_stay), a = mix(
        ("y", [(keep, 1), (w_got, 1), w_x]), ("z", [d_stay, d_y]), ("add", [a_stay, *a_zs])
    )
    w_y, d_zs, a_x = grid.swap(w_y, "y"), over_z(d_zs), grid.swap(a, "x")
    w_y, d_zs, a_x = ends((w_y, d_zs, a_x))

    (*w_zs, w_stay), d, a = mix(("z", [w_stay, w_y]), ("add", [d_stay, *d_zs]), ("pair", [a, a_x], "x"))
    w_zs, d_x, a_c, y0 = over_z(w_zs), grid.swap(d, "x"), grid.swap(a, "c"), grid.swap(other0, "y")
    w_zs, d_x, a_c, y0 = ends((w_zs, d_x, a_c, y0))

    each2, tall2 = 2 * each, 2 * tall
    own, own_hidden = (width // nblk,), (hidden // nblk,)
    places_up = [*range(0, (blocks - 1) * each, each), (blocks - 1) * each + each + 16 + low]
    first_c = (blocks - 1) * each
    a_out = [(0, row, each, 0, (j * half, (j + blocks) * half), 0, each) for j, row in enumerate(places_up)]
    a_out += [(0, first_c, each, 1, (0, half), 0, each), (0, first_c + each, 16, 2, (0, half), 0, 16)]
    a_shapes = [(each2, hidden), (each2, width), (32, width), own, own, own, own, own_hidden]
    a_small = [(3, 0, 2), (4, 1, 2), (5, 2, 2), (6, 3, 2), (7, 4, 2)]
    w, d = mix(("add", [w_stay, *w_zs]), ("pair", [d, d_x], "x"))
    w_x, d_c = grid.swap(w, "x"), grid.swap(d, "c")
    ((total_up, total_out, _, b_out, gain_two, bias_two, b_down, b_up),) = mix(("out", [a, a_c], (a_out, a_shapes, a_small)))
    (grad_patches,) = call(
        end_kernel, "finish", [struct((rows, width), F32)], [patches, gain, grad_mid, own0, z3, z2, z1, y0], rows * width,
    )
    w_x, d_c, grad_patches, total_up = ends((w_x, d_c, grad_patches, total_up))

    (w,) = mix(("pair", [w, w_x], "x"))
    w_c = grid.swap(w, "c")
    d_out = [(0, first_c + each + 16, low, 0, (0, half), 0, tall), (1, 0, tall - low, 0, (0, half), low, tall)]
    last_out = [(0, j * each, each, 0, (j * width, j * width + half), 0, each) for j in range(3)]
    last_out.append((0, 3 * each, 16, 1, (0, half), 0, 16))
    total_down, (total_qkv, _, gain_one, bias_one) = mix(
        ("out", [a, a_c, d, d_c], (d_out, [(tall2, width)])),
        ("out", [w, w_c], (last_out, [(each2, 3 * width), (32, width), own, own], [(2, 0, 1), (3, 1, 1)])),
    )
    small = (gain_one, bias_one, b_out, gain_two, bias_two, b_down, b_up)
    return grad_patches, total_qkv, total_out, total_up, total_down, small


def local(
    grid,
    patches,
    segment_ids,
    sensor_tags,
    seq_starts,
    ln1_gain,
    ln1_bias,
    w_qkv,
    w_out,
    b_out,
    ln2_gain,
    ln2_bias,
    w_up,
    b_up,
    w_down,
    b_down,
    cotangent,
):
    grid.locate()
    nblk, nz, nx = grid.nblk, grid.n["z"], grid.n["x"]
    loop = nz > 4
    rows, width = patches.shape
    me = lax.axis_index("blk")
    where_ = (segment_ids.reshape(nblk, rows), sensor_tags.reshape(nblk, rows), seq_starts)
    norm_one = (ln1_gain, ln1_bias)


    def place(k, other):
        def chunk():
            blk = lax.axis_index("blk")
            return blk ^ (k * 2 + other)

        return chunk

    units = []
    for u in range(nz + 1):
        parts = ([(u - 1, 1)] if u > 0 else []) + ([(u, 0)] if u < nz else [])
        units.append(parts)
    places = [[place(*p) for p in parts] for parts in units]

    state, queries = None, None
    normed, chunks, tokens = {}, {}, []
    held = {(0, 0): patches}
    for k in range(1, nz):
        held[k, 0] = grid.swap(patches, "z", k)
    for u in range(nz + 1):
        got = grid.swap(held[u, 0], "y") if u < nz else None
        tokens.append([held[p] for p in units[u]])
        outs = fwd_call(places[u], u == 0, u == nz, loop, where_, norm_one, w_qkv, tokens[u], queries, state)
        if u < nz:
            after = held[u + 1, 0] if u < nz - 1 else ()
            got, after, outs = lax.optimization_barrier((got, after, outs))
            held[u, 1] = got
            if u < nz - 1:
                held[u + 1, 0] = after
        state = outs[:3]
        n = len(units[u])
        for i, part in enumerate(units[u]):
            normed[part] = outs[3 + i]
            chunks[part] = (places[u][i], outs[3 + n + i], tokens[u][i])
        if u == 0:
            queries = outs[-1]
    log_total, _, attn_t = state

    near = (w_qkv, queries, *where_, log_total)
    mixed_out, left, right, right_given, grad_mid, grad_attn, delta, sums = mid_call(
        near, attn_t, patches, cotangent, w_out, b_out, ln2_gain, ln2_bias, w_up, b_up, w_down, b_down
    )
    half = width // 2
    hidden = w_down.shape[0]
    blocks = hidden // width
    pieces = nblk * nx
    each = width // pieces
    hidden_each = hidden // pieces
    normed = [normed[k, other] for k in range(nz) for other in (1, 0)]
    parts_of = (chunks, where_, queries, grad_attn, log_total, delta)
    if nz == 4 and nx == 2 and each % 16 == 0:
        summed = reduce_packed(
            grid, near, parts_of, w_qkv, left, right, right_given, sums, normed, patches, ln1_gain, grad_mid, blocks, each, hidden_each
        )
    else:
        summed = reduce_plain(
            grid, loop, parts_of, w_qkv, left, right, sums, normed, patches, ln1_gain, grad_mid, blocks, each, hidden_each
        )
    grad_patches, total_qkv, total_out, total_up, total_down, small = summed
    gain_one, bias_one, total_bout, gain_two, bias_two, total_bdown, total_bup = small
    return (
        mixed_out,
        grad_patches,
        gain_one,
        bias_one,
        total_qkv,
        total_out,
        total_bout,
        gain_two,
        bias_two,
        total_up,
        total_bup,
        total_down,
        total_bdown,
    )


def solution(mesh):
    in_specs = (
        P(("dp", "blk"), None),
        P("dp"),
        P("dp"),
        P(("dp", "blk")),
        *(P(),) * 11,
        P(("dp", "blk"), None),
    )
    out_specs = (
        P(("dp", "blk"), None),
        P(("dp", "blk"), None),
        P("blk"),
        P("blk"),
        P("blk", None),
        P("blk", None),
        P("blk"),
        P("blk"),
        P("blk"),
        P("blk", None),
        P("blk"),
        P("blk", None),
        P("blk"),
    )
    return jax.shard_map(
        partial(local, Grid(mesh)), mesh=mesh, in_specs=in_specs, out_specs=out_specs, check_vma=False
    )
```

```python
import functools
from functools import partial

import jax
import jax.numpy as jnp
from jax import lax
from jax.experimental import pallas as pl
from jax.experimental.pallas import tpu as pltpu
from jax.sharding import PartitionSpec as P

HEADS = 12
EPSILON = 1e-06
MASKED = -1e30
AXES = ("dp", "blk")
NT = (((1,), (1,)), ((), ()))
TN = (((0,), (0,)), ((), ()))
NN = (((1,), (0,)), ((), ()))
VM = pl.BlockSpec(memory_space=pltpu.VMEM)
FAR = pl.BlockSpec(memory_space=pltpu.HBM)
LOW = jnp.bfloat16
F32 = jnp.float32
MIB = 1 << 20
BWD_MIB = 8
SECOND_MIB = 12


def dotf(a, b, dims=NN):
    return lax.dot_general(a, b, dims, preferred_element_type=F32)


def struct(shape, dtype):
    return jax.ShapeDtypeStruct(shape, dtype)


def norm_hat(x):
    center = x - jnp.mean(x, axis=-1, keepdims=True)
    inv = lax.rsqrt(jnp.mean(center * center, axis=-1, keepdims=True) + EPSILON)
    return center * inv, inv


def norm_back(hat, inv, gain, grad):
    g = grad * gain
    return inv * (g - jnp.mean(g, axis=-1, keepdims=True) - hat * jnp.mean(g * hat, axis=-1, keepdims=True))


def call(kernel, name, outs, args, flops, aliases=None, scratch=(), exps=0, vmem=8, far=(), far_outs=()):
    moved = sum(a.size * a.dtype.itemsize for a in args) + sum(o.size * o.dtype.itemsize for o in outs)
    return pl.pallas_call(
        kernel,
        out_shape=[pltpu.HBM(o.shape, o.dtype) if i in far_outs else o for i, o in enumerate(outs)],
        in_specs=[FAR if i in far else VM for i in range(len(args))],
        out_specs=[FAR if i in far_outs else VM for i in range(len(outs))],
        input_output_aliases=aliases or {},
        scratch_shapes=scratch,
        compiler_params=pltpu.CompilerParams(vmem_limit_bytes=vmem * MIB),
        cost_estimate=pl.CostEstimate(flops=int(flops) // 4, bytes_accessed=int(moved) // 4, transcendentals=0),
        name=name,
    )(*(pltpu.with_memory_space_constraint(a, pltpu.HBM) if i in far else a for i, a in enumerate(args)))


def line(ref):
    return ref[...].reshape(1, -1)


def key_bias(chunk, seg_ref, tag_ref, from_ref):
    keys = seg_ref.shape[1]
    me = lax.axis_index("blk")
    base = lax.axis_index("dp") * (seg_ref.shape[0] * keys)

    def column(ref):
        return jnp.broadcast_to(ref[pl.ds(chunk, 1), :], (8, keys)).T[:, 0:1]

    kseg, ktag = column(seg_ref), column(tag_ref)
    qseg, qtag = seg_ref[pl.ds(me, 1), :], tag_ref[pl.ds(me, 1), :]
    pos = base + chunk * keys + lax.broadcasted_iota(jnp.int32, (keys, keys), 0)
    seen = (kseg == qseg) & (pos >= line(from_ref))
    tags = (ktag == qtag) | (qtag == 0) | (ktag == 0)
    return jnp.where(seen & tags, 0.0, MASKED)


def head_lanes(block, odd):
    lane = lax.broadcasted_iota(jnp.int32, block.shape, 1)
    return jnp.where((lane >= 64) if odd else (lane < 64), block, jnp.zeros_like(block))


def over_pairs(heads, loop, body):
    if loop:
        lax.fori_loop(0, heads // 2, lambda i, c: (body(i), c)[1], 0)
    else:
        for i in range(heads // 2):
            body(i)


def fwd_kernel(places, first, last, loop, *refs):
    n = len(places)
    seg_ref, tag_ref, from_ref, gain_ref, shift_ref, w_ref = refs[:6]
    tokens = refs[6 : 6 + n]
    refs = refs[6 + n :]
    if first:
        far = (seg_ref, tag_ref, from_ref, gain_ref, shift_ref, w_ref)
        from_ref, gain_ref, shift_ref, w_ref, few_sems, row_sems = refs[-6:]
        seg_ref, tag_ref = refs[-12:-10]
        refs = refs[:-12] + refs[-10:-6]
        here = (from_ref, gain_ref, shift_ref, w_ref)
        few = [pltpu.make_async_copy(far[2 + i], here[i], few_sems.at[i]) for i in range(4)]
        row_count, row_size = seg_ref.shape
        by_rows = []
        for i in range(2):
            for j in range(row_count):
                some = pl.ds(j * row_size, row_size)
                by_rows.append(pltpu.make_async_copy(far[i].at[some], (seg_ref, tag_ref)[i].at[j], row_sems.at[i, j]))
        few[3].start()
        for copy in (*few[:3], *by_rows):
            copy.start()
        for copy in (*few[:3], *by_rows):
            copy.wait()
    if not first:
        q_ref, top_in, sum_in, acc_in = refs[:4]
        refs = refs[4:]
    top_out, sum_out, acc_out = refs[:3]
    normed_far, kv_far = refs[3 : 3 + n], refs[3 + n : 3 + 2 * n]
    if first:
        q_ref = refs[3 + 2 * n]
    bias, normed_out, kv_out, sems = refs[-4:]
    keys, width = tokens[0].shape
    for i in range(n):
        at = pl.ds(i * keys, keys)
        hat = norm_hat(tokens[i][...].astype(F32))[0]
        normed = (hat * line(gain_ref) + line(shift_ref)).astype(LOW)
        normed_out[at, :] = normed
        bias[i] = key_bias(places[i](), seg_ref, tag_ref, from_ref)
    kept = []
    for i in range(n):
        kept.append(pltpu.make_async_copy(normed_out.at[pl.ds(i * keys, keys), :], normed_far[i], sems.at[0, i]))
        kept[-1].start()
    normed = normed_out[...]
    if first:
        few[3].wait()
        q_ref[...] = (dotf(normed, w_ref[:, :width]).astype(LOW) * jnp.asarray(0.125, LOW)).astype(LOW)
    for j in range(2):
        cols = pl.ds(j * width, width)
        kv_out[:, cols] = dotf(normed, w_ref[:, pl.ds((j + 1) * width, width)]).astype(LOW)
    for i in range(n):
        kept.append(pltpu.make_async_copy(kv_out.at[pl.ds(i * keys, keys), :], kv_far[i], sems.at[1, i]))
        kept[-1].start()

    def pair_body(pair):
        lanes = pl.multiple_of(pair * 128, 128)
        at, vat = pl.ds(lanes, 128), pl.ds(width + lanes, 128)
        q_pair = q_ref[:, at]
        v_t = [kv_out[pl.ds(i * keys, keys), vat].T for i in range(n)]
        for odd in range(2):
            h = pair * 2 + odd
            row = pl.ds(h, 1)
            rows = pl.ds(pl.multiple_of(h * 64, 64), 64)
            q_h = head_lanes(q_pair, odd)
            scores = [dotf(kv_out[pl.ds(i * keys, keys), at], q_h, NT) + bias[i] for i in range(n)]
            top = jnp.max(scores[0], axis=0, keepdims=True)
            for s in scores[1:]:
                top = jnp.maximum(top, jnp.max(s, axis=0, keepdims=True))
            if not first:
                old = top_in[row, :]
                top = jnp.maximum(top, old)
                fade = jnp.exp(old - top)
            total = None
            out = None
            for i in range(n):
                p = jnp.exp(scores[i] - top)
                t = jnp.sum(p, axis=0, keepdims=True)
                o = dotf(v_t[i][odd * 64 : odd * 64 + 64], p.astype(LOW))
                total = t if total is None else total + t
                out = o if out is None else out + o
            if not first:
                total = total + sum_in[row, :] * fade
                out = out + acc_in[rows, :] * fade
            if last:
                out = out / total
                top = top + jnp.log(total)
            acc_out[rows, :] = out
            top_out[row, :] = top
            sum_out[row, :] = total

    over_pairs(HEADS, loop, pair_body)
    for copy in kept:
        copy.wait()


def fwd_call(places, first, last, loop, where_, norm, w_qkv, tokens, queries, state):
    keys, width = tokens[0].shape
    n = len(tokens)
    outs = [
        struct((HEADS, keys), F32),
        struct((HEADS, keys), F32),
        struct((width, keys), F32),
        *(struct((keys, width), LOW) for _ in range(n)),
        *(struct((keys, 2 * width), LOW) for _ in range(n)),
    ]
    args = [*where_, *norm, w_qkv, *tokens]
    scratch = [
        pltpu.VMEM((n, keys, keys), F32),
        pltpu.VMEM((n * keys, width), LOW),
        pltpu.VMEM((n * keys, 2 * width), LOW),
        pltpu.SemaphoreType.DMA((2, n)),
    ]
    if first:
        count = where_[0].shape[0] // keys
        outs += [struct((keys, width), LOW)] + [struct((count, keys), jnp.int32)] * 2
        scratch += [pltpu.VMEM(v.shape, v.dtype) for v in (where_[2], *norm, w_qkv)]
        scratch += [pltpu.SemaphoreType.DMA((4,)), pltpu.SemaphoreType.DMA((2, count))]
    else:
        args += [queries, *state]
    return call(
        partial(fwd_kernel, places, first, last, loop),
        "attend",
        outs,
        args,
        n * (HEADS * keys * keys * 256 * 8 + keys * width * width * 4),
        aliases={} if first else {len(args) - 3 + i: i for i in range(3)},
        scratch=scratch,
        far=range(6) if first else (),
        vmem=16 if first else 8,
        far_outs=tuple(range(3, 3 + 2 * n)),
        exps=n * HEADS * keys * keys,
    )


def bwd_kernel(places, first, last, loop, *refs):
    n = len(places)
    seg_ref, tag_ref, from_ref, w_ref, q_ref, do_ref, lse_ref, delta_ref = refs[:8]
    kvs, tokens = refs[8 : 8 + 2 * n], refs[8 + 2 * n : 8 + 4 * n]
    refs = refs[8 + 4 * n :]
    if not first:
        dq_in, sums_in = refs[:2]
        refs = refs[2:]
    dq_out, sums_out = refs[:2]
    dkvs, dn = refs[2 : 2 + n], refs[2 + n : 2 + 3 * n]
    if last:
        gq_out = refs[2 + 3 * n]
    bias = refs[-1]
    keys, width = tokens[0].shape
    for i in range(n):
        for j in range(2):
            bias[j] = key_bias(places[i][j](), seg_ref, tag_ref, from_ref)
        kv, dkv = kvs[2 * i : 2 * i + 2], dkvs[i]

        def pair_body(pair, fresh=first and i == 0, dq_from=dq_in if not first and i == 0 else dq_out):
            lanes = pl.multiple_of(pair * 128, 128)
            at, vat = pl.ds(lanes, 128), pl.ds(width + lanes, 128)
            q_pair = q_ref[:, at]
            do_pair = do_ref[:, at]
            chunk = [pl.ds(j * keys, keys) for j in range(2)]
            k_t = [kv[j][:, at].T for j in range(2)]
            dk = [None] * 2
            dv = [None] * 2
            for odd in range(2):
                h = pair * 2 + odd
                row = pl.ds(h, 1)
                rows = pl.ds(pl.multiple_of(h * 64, 64), 64)
                q_h = head_lanes(q_pair, odd)
                do_h = head_lanes(do_pair, odd)
                lse = lse_ref[row, :]
                delta = delta_ref[row, :]
                dq = None
                for j in range(2):
                    p = jnp.exp(dotf(kv[j][:, at], q_h, NT) + bias[j] - lse)
                    dp = dotf(kv[j][:, vat], do_h, NT)
                    ds = (p * (dp - delta)).astype(LOW)
                    v_part = dotf(p.astype(LOW), do_h)
                    k_part = dotf(ds, q_h)
                    q_part = dotf(k_t[j][odd * 64 : odd * 64 + 64], ds)
                    dv[j] = v_part if odd == 0 else dv[j] + v_part
                    dk[j] = k_part if odd == 0 else dk[j] + k_part
                    dq = q_part if dq is None else dq + q_part
                if not fresh:
                    dq = dq + dq_from[rows, :]
                dq_out[rows, :] = dq
            for j in range(2):
                dkv[chunk[j], at] = dk[j].astype(LOW)
                dkv[chunk[j], vat] = dv[j].astype(LOW)

        over_pairs(HEADS, loop, pair_body)
        gain_sum = bias_sum = 0.0
        ending = last and i == n - 1
        if ending:
            grad_query = (dq_out[...].T * 0.125).astype(LOW)
            gq_out[...] = grad_query
        for j in range(2):
            part = dotf(dkv[pl.ds(j * keys, keys), :], w_ref[:, width:], NT)
            if ending and j == 1:
                part = part + dotf(grad_query, w_ref[:, :width], NT)
            dn[2 * i + j][...] = part.astype(LOW)
            hat = norm_hat(tokens[2 * i + j][...].astype(F32))[0]
            gain_sum = gain_sum + jnp.sum(part * hat, axis=0, keepdims=True)
            bias_sum = bias_sum + jnp.sum(part, axis=0, keepdims=True)
        if i == 0:
            sums_out[...] = jnp.zeros_like(sums_out) if first else sums_in[...]
        sums_out[0:1, :] += gain_sum
        sums_out[1:2, :] += bias_sum


def bwd_give_kernel(places, pieces, count, left_count, more, *refs):
    outs = refs[count + more : -2]
    bwd_kernel(places, False, True, False, *refs[:count], *outs, refs[-1])
    normed, dkv = refs[count : count + left_count], refs[count + left_count : count + more]
    second_part(pieces, 1 - lax.axis_index("dp") % 2, normed, (outs[2], *dkv), outs[-1], outs[1], refs[-2])


def bwd_call(slots, first, last, loop, chunks, where_, w_qkv, queries, grad_attn, log_total, delta, carried, give=None):
    rows, width = queries.shape
    n = len(slots)
    each = [[chunks[k, other] for other in (1, 0)] for k in slots]
    outs = [struct((width, rows), F32), struct((8, width), F32)]
    outs += [struct((2 * rows, 2 * width), LOW) for _ in slots]
    outs += [struct((rows, width), LOW) for _ in range(2 * n)]
    if last:
        outs.append(struct((rows, width), LOW))
    args = [*where_, w_qkv, queries, grad_attn, log_total, delta]
    args += [c[1] for pair in each for c in pair] + [c[2] for pair in each for c in pair] + list(carried)
    places = [[c[0] for c in pair] for pair in each]
    aliases = {} if first else {len(args) - 2: 0, len(args) - 1: 1}
    kernel = partial(bwd_kernel, places, first, last, loop)
    if give:
        pieces, normed, dkv = give
        kernel = partial(bwd_give_kernel, places, pieces, len(args), len(normed), len(normed) + len(dkv))
        args += [*normed, *dkv]
        outs.append(struct((2, pieces // 2, 3 * width // pieces + 16, width // 2), LOW))
    return call(
        kernel,
        "attend_back",
        outs,
        args,
        n * 2 * (HEADS * rows * rows * 256 * 14 + rows * width * width * 4),
        aliases=aliases,
        scratch=[pltpu.VMEM((2, rows, rows), F32)],
        vmem=SECOND_MIB if give else BWD_MIB,
    )


def mid_kernel(
    attn_ref, x_ref, dy_ref, wo_ref, bo_ref, g2_ref, s2_ref, wu_ref, bu_ref, wd_ref, bd_ref, *refs
):
    mixed_ref, left_ref, right_ref, given_ref, mid_ref, do_ref, delta_ref, sums_ref = refs[-8:]
    rows, width = x_ref.shape
    hidden = wu_ref.shape[1]
    half, blocks = width // 2, hidden // width
    attn_low = attn_ref[...].T.astype(LOW)
    left_ref[:, pl.ds(hidden + width, width)] = attn_low
    x_mid = x_ref[...].astype(F32) + dotf(attn_low, wo_ref[...]) + line(bo_ref)
    hat, inv = norm_hat(x_mid)
    gain = line(g2_ref)
    normed = (hat * gain + line(s2_ref)).astype(LOW)
    left_ref[:, pl.ds(hidden, width)] = normed
    dy = dy_ref[...]
    dy_full = dy.astype(F32)
    down = None
    grad_normed = None
    for j in range(blocks):
        cols = pl.ds(j * width, width)
        pre = dotf(normed, wu_ref[:, cols]) + bu_ref[cols].reshape(1, -1)
        cdf = 0.5 + 0.5 * lax.erf(pre * (0.5**0.5))
        slope = cdf + pre * (jnp.exp(-0.5 * pre * pre) * 0.3989422804014327)
        act = (pre * cdf).astype(LOW)
        left_ref[:, cols] = act
        part = dotf(act, wd_ref[cols, :])
        down = part if down is None else down + part
        grad_pre = (dotf(dy, wd_ref[cols, :], NT) * slope).astype(LOW)
        right_ref[j * 2 // blocks, :, pl.ds(j % (blocks // 2) * width, width)] = grad_pre
        part = dotf(grad_pre, wu_ref[:, cols], NT)
        grad_normed = part if grad_normed is None else grad_normed + part
        sums_ref[4 + j : 5 + j, :] = jnp.sum(grad_pre.astype(F32), axis=0, keepdims=True)
    mixed_ref[...] = (x_mid + down + line(bd_ref)).astype(LOW)
    grad_mid = dy_full + norm_back(hat, inv, gain, grad_normed)
    mid_ref[...] = grad_mid
    branch = grad_mid.astype(LOW)
    for c in range(2):
        right_ref[c, :, pl.ds(hidden // 2, half)] = branch[:, c * half : (c + 1) * half]
        right_ref[c, :, pl.ds(hidden // 2 + half, half)] = dy[:, c * half : (c + 1) * half]
    given_ref[...] = right_ref[1 - lax.axis_index("dp") % 2]
    grad_attn = dotf(branch, wo_ref[...], NT).astype(LOW)
    do_ref[...] = grad_attn
    product = grad_attn.astype(F32).T * attn_ref[...]
    size = width // HEADS
    for h in range(HEADS):
        delta_ref[h : h + 1, :] = jnp.sum(product[h * size : (h + 1) * size, :], axis=0, keepdims=True)
    sums_ref[0:1, :] = jnp.sum(branch.astype(F32), axis=0, keepdims=True)
    sums_ref[1:2, :] = jnp.sum(grad_normed * hat, axis=0, keepdims=True)
    sums_ref[2:3, :] = jnp.sum(grad_normed, axis=0, keepdims=True)
    sums_ref[3:4, :] = jnp.sum(dy_full, axis=0, keepdims=True)


def mid_call(near, attn_t, patches, cotangent, w_out, b_out, g2, s2, w_up, b_up, w_down, b_down):
    rows, width = patches.shape
    hidden = w_up.shape[1]
    outs = [
        struct((rows, width), LOW),
        struct((rows, hidden + 2 * width), LOW),
        struct((2, rows, hidden // 2 + width), LOW),
        struct((rows, hidden // 2 + width), LOW),
        struct((rows, width), F32),
        struct((rows, width), LOW),
        struct((HEADS, rows), F32),
        struct((4 + hidden // width, width), F32),
    ]
    args = [attn_t, patches, cotangent, w_out, b_out, g2, s2, w_up, b_up, w_down, b_down, *near]
    return call(mid_kernel, "middle", outs, args, rows * width * (hidden * 8 + width * 4), exps=rows * hidden * 4, vmem=16)


def halves_of_x(acc, pieces, half):
    acc = acc.reshape(pieces // 2, 2, -1, half)
    first = lax.axis_index("dp") // 2 == 0
    own = jnp.where(first, acc[:, 0], acc[:, 1]).astype(LOW)
    other = jnp.where(first, acc[:, 1], acc[:, 0]).astype(LOW)
    return other, own


def first_kernel(jobs, sums_to, pieces, left_ref, right_ref, left_got, right_got, sums_ref, sums_got, *refs):
    c = lax.axis_index("dp") % 2
    parts = 1 + max(target[0] for job in jobs for target in job[-1])
    outs = refs[-2 * parts :]
    half = outs[0].shape[2]
    width = 2 * half
    for left, total, right, targets in jobs:
        cols = pl.ds(right, half)
        each = total * 2 // (2 * pieces)
        for begin in range(0, total, width):
            rows = pl.ds(left + begin, width)
            acc = dotf(left_ref[:, rows], right_ref[c, :, cols], TN) + dotf(left_got[:, rows], right_got[:, cols], TN)
            pair = halves_of_x(acc, width // each, half)
            blks = width // each // 2
            at = pl.ds(begin // each // 2, blks)
            for part, low, high, row in targets:
                for side in range(2):
                    outs[part + side * parts][at, pl.ds(row, high - low), :] = pair[side][:, low:high, :]
    mine = sums_ref[:, pl.ds(pl.multiple_of(c * half, 128), half)] + sums_got[:, pl.ds(pl.multiple_of(c * half, 128), half)]
    mine = jnp.concatenate([mine, jnp.zeros_like(mine)], axis=0).astype(LOW)
    part, row = sums_to
    for side in range(2):
        out = outs[part + side * parts]
        out[:, pl.ds(row, 16), :] = jnp.broadcast_to(mine[None], (out.shape[0],) + mine.shape)


def first_call(near, jobs, sums_to, heights, pieces, half, left, right, left_got, right_got, sums, sums_got):
    outs = [struct((pieces // 2, h, half), LOW) for h in heights] * 2
    args = [left, right, left_got, right_got, sums, sums_got, *near]
    return call(
        partial(first_kernel, jobs, sums_to, pieces), "weights", outs, args, sum(h for h in heights) * pieces * half * 1024, vmem=12
    )


def second_part(pieces, c, normed, dkv, gq_ref, sums_ref, out):
    keys, width = normed[0].shape
    half = width // 2
    each = width // pieces
    for block in range(3):
        if block == 0:
            cols = pl.ds(pl.multiple_of(c * half, 128), half)
            acc = dotf(normed[1][...], gq_ref[:, cols], TN)
        else:
            cols = pl.ds(pl.multiple_of((block - 1) * width + c * half, 128), half)
            acc = None
            for i in range(len(normed)):
                term = dotf(normed[i][...], dkv[i // 2][pl.ds(i % 2 * keys, keys), cols], TN)
                acc = term if acc is None else acc + term
        pair = halves_of_x(acc, pieces, half)
        for side in range(2):
            out[side, :, pl.ds(block * each, each), :] = pair[side]
    mine = sums_ref[:, pl.ds(pl.multiple_of(c * half, 128), half)]
    mine = jnp.concatenate([mine, jnp.zeros_like(mine)], axis=0).astype(LOW)
    for side in range(2):
        out[side, :, pl.ds(3 * each, 16), :] = jnp.broadcast_to(mine[None], (out.shape[1],) + mine.shape)


def keep_kernel(pieces, units, *refs):
    normed, dkv = refs[2 : 2 + 2 * units], refs[2 + 2 * units : 2 + 3 * units]
    second_part(pieces, lax.axis_index("dp") % 2, normed, dkv, *refs[:2], refs[-1])


def keep_call(pieces, half, grad_query, sums, normed, dkv):
    each = 2 * half // pieces
    args = [grad_query, sums, *normed, *dkv]
    (out,) = call(
        partial(keep_kernel, pieces, len(dkv)),
        "weights",
        [struct((2, pieces // 2, 3 * each + 16, half), LOW)],
        args,
        sum(v.shape[0] for v in normed) * 2 * half * 4 * half,
        vmem=SECOND_MIB,
    )
    return out


def weight_kernel(spec, sums_at, pieces, far, count, *refs):
    me = lax.axis_index("dp") % 2
    ins = list(refs[:count])
    outs = refs[count : len(refs) - len(far) - (1 if far else 0)]
    waits = {}
    if far:
        sems = refs[-1]
        for i, number in enumerate(far):
            held = refs[len(refs) - 1 - len(far) + i]
            waits[number] = pltpu.make_async_copy(ins[number], held, sems.at[i])
            waits[number].start()
            ins[number] = held
    parts = len(outs) // 2
    for part, row, lefts, rights, starts in spec:
        for number in (*lefts, *rights):
            if number in waits:
                waits.pop(number).wait()
        for given in (True, False):
            c = 1 - me if given else me
            out = outs[part + (0 if given else parts)]
            half = out.shape[2]
            total = ins[lefts[0]].shape[1]
            each = total // pieces
            step = min(total, 768)
            cols = pl.ds(pl.multiple_of(jnp.where(c == 0, starts[0], starts[1]), 128), half)
            for begin in range(0, total, step):
                acc = None
                for left, right in zip(lefts, rights):
                    term = dotf(ins[left][:, pl.ds(begin, step)], ins[right][:, cols], TN)
                    acc = term if acc is None else acc + term
                acc = acc.reshape(step // each, each, half)
                out[pl.ds(begin // each, step // each), pl.ds(row, each), :] = acc.astype(LOW)
    if sums_at is not None:
        part, row, number = sums_at
        for given in (True, False):
            c = 1 - me if given else me
            out = outs[part + (0 if given else parts)]
            half = out.shape[2]
            mine = ins[number][:, pl.ds(pl.multiple_of(c * half, 128), half)]
            mine = jnp.concatenate([mine, jnp.zeros_like(mine)], axis=0).astype(LOW)
            out[:, pl.ds(row, 16), :] = jnp.broadcast_to(mine[None], (pieces,) + mine.shape)


def weight_call(pieces, heights, half, jobs, sums=None, sums_at=None, far=()):
    spec, args, flops = [], [], 0

    def index(array):
        for i, known in enumerate(args):
            if known is array:
                return i
        args.append(array)
        return len(args) - 1

    for part, row, lefts, rights, starts in jobs:
        spec.append((part, row, [index(v) for v in lefts], [index(v) for v in rights], starts))
        flops += sum(a.shape[0] for a in lefts) * lefts[0].shape[1] * half * 4
    if sums is not None:
        sums_at = (*sums_at, index(sums))
    far = tuple(i for i, a in enumerate(args) if any(a is v for v in far))
    scratch = [pltpu.VMEM(args[i].shape, args[i].dtype) for i in far]
    if far:
        scratch.append(pltpu.SemaphoreType.DMA((len(far),)))
    outs = [struct((pieces, h, half), LOW) for h in heights] * 2
    return call(
        partial(weight_kernel, spec, sums_at, pieces, far, len(args)),
        "weights",
        outs,
        args,
        flops,
        scratch=scratch,
        far=far,
        vmem=8 + sum(args[i].size * 2 for i in far) // MIB,
    )


def mix_kernel(ops, *refs):
    dp, blk = lax.axis_index("dp"), lax.axis_index("blk")
    at = {"x": dp // 2, "c": dp % 2, "z": blk // 2, "y": blk % 2}
    for kind, ins, outs, more in ops:
        terms = [refs[i] if lead is None else refs[i].at[lead] for i, lead in ins]
        if kind == "cut":
            whole = total_of([t[...] for t in terms])
            outs_here = [refs[i] for i in outs]
            outs_here[0][...] = whole[:, :more, :].astype(LOW)
            outs_here[1][...] = whole[:, more:, :]
            continue
        outs = [refs[i] for i in outs]
        if kind == "add":
            outs[0][...] = total_of([t[...] for t in terms]).astype(LOW)
        elif kind == "y":
            size, row = len(terms) // (more or 1), 0
            for begin in range(0, len(terms), size):
                group = terms[begin : begin + size]
                some = pl.ds(row, group[0].shape[1])
                row += group[0].shape[1]
                for q in range(outs[0].shape[0]):
                    outs[0][q, some, :] = total_of([t[2 * q + 1 - at["y"]] for t in group]).astype(LOW)
                    outs[1][q, some, :] = total_of([t[2 * q + at["y"]] for t in group])
        elif kind == "z":
            size, row = len(terms) // (more or 1), 0
            for begin in range(0, len(terms), size):
                group = terms[begin : begin + size]
                some = pl.ds(row, group[0].shape[1])
                row += group[0].shape[1]
                for k in range(1, group[0].shape[0]):
                    outs[k - 1][some, :] = total_of([t[at["z"] ^ k] for t in group]).astype(LOW)
                outs[-1][some, :] = total_of([t[at["z"]] for t in group])
        elif kind == "pair":
            outs[0][at[more]] = terms[0][...]
            outs[0][1 - at[more]] = terms[1][...]
        else:
            for source, row, height, number, starts, offset, stride in more[0]:
                some = pl.ds(row, height)
                own, got = terms[2 * source : 2 * source + 2]
                for x in range(own.shape[0]):
                    mine, other = own[x, some, :].astype(F32), got[x, some, :].astype(F32)
                    first = at["c"] == 0
                    to = pl.ds(x * stride + offset, height)
                    width = mine.shape[1]
                    outs[number][to, pl.ds(starts[0], width)] = jnp.where(first, mine, other)
                    outs[number][to, pl.ds(starts[1], width)] = jnp.where(first, other, mine)
            for number, row, source in more[2] if len(more) > 2 else ():
                size = outs[number].shape[0]
                if size % 128:
                    values = pltpu.roll(outs[source][row : row + 1, :], outs[source].shape[1] - blk * size, 1)
                    outs[number][...] = values[:, :size].reshape(size)
                else:
                    each = outs[source].shape[1] // size
                    values = outs[source][pl.ds(row + blk // each, 1), pl.ds(pl.multiple_of(blk % each * size, 128), size)]
                    outs[number][...] = values.reshape(size)


def mix(*ops):
    args, outs, spec, counts = [], [], [], []

    def index(array):
        for i, known in enumerate(args):
            if known is array:
                return i
        args.append(array)
        return len(args) - 1

    for kind, terms, *more in ops:
        ins = [(index(t[0]), t[1]) if isinstance(t, tuple) else (index(t), None) for t in terms]
        shape = args[ins[0][0]].shape
        shape = shape if ins[0][1] is None else shape[1:]
        if kind == "add":
            new = [struct(shape, LOW)]
        elif kind == "y":
            groups = more[0] if more else 1
            firsts = [ins[i * (len(ins) // groups)] for i in range(groups)]
            height = sum(args[i].shape[-2] for i, _ in firsts)
            shape = (shape[0] // 2, height, shape[2])
            new = [struct(shape, LOW), struct(shape, F32)]
        elif kind == "z":
            groups = more[0] if more else 1
            height = sum(args[ins[i * (len(ins) // groups)][0]].shape[-2] for i in range(groups))
            new = [struct((height, shape[2]), LOW)] * (shape[0] - 1) + [struct((height, shape[2]), F32)]
        elif kind == "cut":
            new = [struct((shape[0], more[0], shape[2]), LOW), struct((shape[0], shape[1] - more[0], shape[2]), F32)]
        elif kind == "pair":
            new = [struct((2, *shape), LOW)]
        else:
            new = [struct(v, F32) for v in more[0][1]]
        spec.append((kind, ins, range(len(outs), len(outs) + len(new)), more[0] if more else None))
        counts.append(len(new))
        outs += new
    spec = [(kind, ins, [len(args) + i for i in out], more) for kind, ins, out, more in spec]
    made = call(partial(mix_kernel, spec), "mix", outs, args, sum(o.size for o in outs), vmem=8)
    split = []
    for n in counts:
        split.append(made[0] if n == 1 else tuple(made[:n]))
        made = made[n:]
    return split


def end_kernel(x_ref, gain_ref, mid_ref, *refs):
    out = refs[-1]
    grad = refs[0][...].astype(F32)
    for ref in refs[1:-1]:
        grad = grad + ref[...].astype(F32)
    hat, inv = norm_hat(x_ref[...].astype(F32))
    out[...] = mid_ref[...] + norm_back(hat, inv, line(gain_ref), grad)


class Grid:
    def __init__(self, mesh):
        ndp, nblk = mesh.shape["dp"], mesh.shape["blk"]
        self.n = {"c": 2, "x": ndp // 2, "y": 2, "z": nblk // 2}
        self.nblk, self.ndp = nblk, ndp

    def locate(self):
        dp, blk = lax.axis_index("dp"), lax.axis_index("blk")
        self.at = {"x": dp // 2, "c": dp % 2, "z": blk // 2, "y": blk % 2}

    def swap(self, value, axis, k=1):
        pairs = []
        n = self.n
        for x in range(n["x"]):
            for c in range(2):
                for z in range(n["z"]):
                    for y in range(2):
                        here = {"x": x, "c": c, "z": z, "y": y}
                        there = dict(here)
                        there[axis] ^= k
                        flat = [((p["x"] * 2 + p["c"]) * n["z"] + p["z"]) * 2 + p["y"] for p in (here, there)]
                        pairs.append(tuple(flat))
        return lax.ppermute(value, AXES, pairs)

    def all_sum(self, value, axis):
        step = 1
        while step < self.n[axis]:
            value = value + self.swap(value, axis, step)
            step *= 2
        return value

    def scatter(self, array, axis, dim):
        piece = lambda k: lax.dynamic_index_in_dim(array, self.at[axis] ^ k, dim, keepdims=False)
        got = []
        if self.n[axis] > 1:
            got = yield [self.swap(piece(k), axis, k) for k in range(1, self.n[axis])]
        return [piece(0), *got]

    def gather(self, value, axis):
        n = self.n[axis]
        if n == 1:
            return [value]
        got = yield [self.swap(value, axis, k) for k in range(1, n)]
        slots = [value, *got]
        at = self.at[axis]
        out = []
        for p in range(n):
            piece = slots[p]
            for i in range(1, n):
                piece = jnp.where(at == i, slots[p ^ i], piece)
            out.append(piece)
        return out


class Flow:
    def __init__(self, steps):
        self.steps, self.result = steps, None
        self.advance(None, True)

    def advance(self, value, first=False):
        try:
            self.pending = next(self.steps) if first else self.steps.send(value)
        except StopIteration as stop:
            self.pending, self.result = None, stop.value


def tie(flows, *values):
    flows = [f for f in flows if f.pending is not None]
    pending, values = lax.optimization_barrier(([f.pending for f in flows], values))
    for flow, value in zip(flows, pending):
        flow.advance(value)
    return values


def total_of(terms):
    return functools.reduce(lambda a, b: a + b, [t.astype(F32) for t in terms])


def reduce_plain(grid, loop, parts_of, w_qkv, left, right, sums, normed, patches, gain, grad_mid, blocks, each, hidden_each):
    chunks, where_, queries, grad_attn, log_total, delta = parts_of
    nz, nx = grid.n["z"], grid.n["x"]
    rows, width = patches.shape
    half, hidden, pieces = width // 2, blocks * width, grid.nblk * nx
    act_low, normed_two, attn_low = left[:, :hidden], left[:, hidden : hidden + width], left[:, hidden + width :]
    grad_pre, grad_branch, dy = (
        jnp.concatenate([right[c, :, a:b] for c in range(2)], axis=1)
        for a, b in ((0, hidden // 2), (hidden // 2, hidden // 2 + half), (hidden // 2 + half, hidden // 2 + width))
    )

    def reduce_rows(given, kept):
        got = yield grid.swap(given, "c")
        part = (kept.astype(F32) + got.astype(F32)).astype(LOW).reshape(nz, 2, nx, -1, kept.shape[-1])
        for axis, dim in (("x", 2), ("y", 1), ("z", 0)):
            terms = yield from grid.scatter(part, axis, dim)
            part = total_of(terms).astype(LOW)
        over_x = yield from grid.gather(part, "x")
        over_c = yield from grid.gather(jnp.stack(over_x), "c")
        return over_c

    def reduce_small(part):
        for axis in "cxyz":
            part = grid.all_sum(part, axis)
        return part

    def reduce_all(heights, jobs, far=()):
        made = weight_call(pieces, heights, half, jobs, far=far)
        count = len(heights)
        flows = [Flow(reduce_rows(*v)) for v in zip(made[:count], made[count:])]
        while any(f.pending is not None for f in flows):
            for f in flows:
                if f.pending is not None:
                    f.advance(f.pending)
        return [[v.reshape(-1, half) for v in f.result] for f in flows]

    def join(blocks_):
        return jnp.concatenate([b[c] for c in range(2) for b in blocks_], axis=1).astype(F32)

    jobs = [(0, 0, [act_low], [dy], (0, half)), (1, 0, [attn_low], [grad_branch], (0, half))]
    jobs += [(2 + j, 0, [normed_two], [grad_pre], (j * half, (j + blocks) * half)) for j in range(blocks)]
    first = reduce_all([hidden_each] + [each] * (1 + blocks), jobs)
    total_down, total_out, total_up = join(first[:1]), join(first[1:2]), join(first[2:])
    sums = reduce_small(sums)

    carried = ()
    dkv, home = [None] * nz, []
    for k in reversed(range(nz)):
        outs = bwd_call([k], k == nz - 1, k == 0, loop, chunks, where_, w_qkv, queries, grad_attn, log_total, delta, carried)
        carried, dkv[k] = outs[:2], outs[2]
        other, own, grad_query = outs[3], outs[4], outs[-1]
        got = grid.swap(other, "y")
        home.append(grid.swap((own.astype(F32) + got.astype(F32)).astype(LOW), "z", k) if k else got)
    (grad_patches,) = call(
        end_kernel, "finish", [struct((rows, width), F32)], [patches, gain, grad_mid, own, *home], rows * width, vmem=40
    )
    own_first = normed[1]
    lefts = [jnp.concatenate(normed[2 * k : 2 * k + 2], axis=0) for k in range(nz)]
    jobs = [(0, 0, [own_first], [grad_query], (0, half)), (1, 0, lefts, dkv, (0, half)), (2, 0, lefts, dkv, (width, width + half))]
    second = reduce_all([each] * 3, jobs, far=(own_first, *lefts, *dkv))
    total_qkv = jnp.concatenate([t[c] for t in second for c in range(2)], axis=1).astype(F32)
    late, me = reduce_small(carried[1]), lax.axis_index("blk")

    def own_part(v):
        size = v.size // grid.nblk
        return lax.dynamic_slice_in_dim(v.reshape(-1), me * size, size)

    small = [own_part(v) for v in (late[0], late[1], sums[0], sums[1], sums[2], sums[3], sums[4:])]
    return grad_patches, total_qkv, total_out, total_up, total_down, small


def reduce_packed(
    grid, near, parts_of, w_qkv, left, right, right_given, sums, normed, patches, gain, grad_mid, blocks, each, hidden_each
):
    chunks, where_, queries, grad_attn, log_total, delta = parts_of
    nz, nblk = grid.n["z"], grid.nblk
    rows, width = patches.shape
    half, hidden, pieces = width // 2, blocks * width, nblk * 2
    ends = lax.optimization_barrier
    over_z = lambda sends: [grid.swap(v, "z", len(sends) - k) for k, v in enumerate(reversed(sends))][::-1]
    tall = hidden_each
    low = tall // 3
    heights = [(blocks - 1) * each, each + 16 + low, tall - low, each]
    jobs = [(hidden, width, (blocks - 1) * half, ((3, 0, each, 0),))]
    jobs += [(hidden, width, j * half, ((0, 0, each, j * each),)) for j in range(blocks - 1)]
    jobs.append((hidden + width, width, blocks * half, ((1, 0, each, 0),)))
    jobs.append((0, hidden, (blocks + 1) * half, ((1, 0, low, each + 16), (2, low, tall, 0))))
    sums_to = (1, each)

    def unit(slots, carried, give=None):
        return bwd_call(
            slots, not carried, 0 in slots, False, chunks, where_, w_qkv, queries, grad_attn, log_total, delta, carried, give
        )

    passed = [grid.swap(v, "c") for v in (left, right_given, sums)]
    dkv = [None] * nz
    outs, passed = ends((unit([3], ()), passed))
    carried, dkv[3], other3, own3 = outs[:2], *outs[2:]
    y3 = grid.swap(other3, "y")
    made = first_call(near, jobs, sums_to, heights, pieces, half, left, right, passed[0], passed[1], sums, passed[2])
    made, carried = ends((made, carried))
    ((e_y, e_stay),) = mix(("y", [made[3], made[7]], 2))
    a_x, e_y = grid.swap(made[0], "x"), grid.swap(e_y, "y")

    outs, y3, a_x, e_y, *sent = ends((unit([2, 1], carried), y3, a_x, e_y, made[1], made[2]))
    carried, dkv[2], dkv[1], other2, own2, other1, own1 = outs[:2], *outs[2:]
    z3, (e_x, e_stay) = mix(("add", [own3, y3]), ("cut", [e_stay, e_y], each))
    c_x, z3, y2, y1 = grid.swap(sent[0], "x"), grid.swap(z3, "z", 3), grid.swap(other2, "y"), grid.swap(other1, "y")
    e_x = grid.swap(e_x, "x")

    outs, y2, y1, c_x, z3, e_x, sent = ends(
        (unit([0], carried, (pieces, normed, dkv[1:])), y2, y1, c_x, z3, e_x, sent[1])
    )
    carried, dkv[0], other0, own0, grad_query, give = outs[:2], *outs[2:]
    z2, z1, (a_y, a_stay) = mix(("add", [own2, y2]), ("add", [own1, y1]), ("y", [made[4], a_x, made[5], c_x], 2))
    d_x, z2, z1, a_y = grid.swap(sent, "x"), grid.swap(z2, "z", 2), grid.swap(z1, "z", 1), grid.swap(a_y, "y")
    w_got = grid.swap(give, "c")
    keep = keep_call(pieces, half, grad_query, carried[1], normed, dkv)
    w_got, keep, d_x, a_y, z2, z1 = ends((w_got, keep, d_x, a_y, z2, z1))

    w_x, (*a_zs, a_stay), (d_y, d_stay) = mix(
        ("add", [(keep, 0), (w_got, 0)]), ("z", [a_stay, a_y, e_stay, e_x], 2), ("y", [made[6], d_x])
    )
    w_x, d_y, a_zs = grid.swap(w_x, "x"), grid.swap(d_y, "y"), over_z(a_zs)
    w_x, d_y, a_zs = ends((w_x, d_y, a_zs))

    (w_y, w_stay), (*d_zs, d_stay), a = mix(
        ("y", [(keep, 1), (w_got, 1), w_x]), ("z", [d_stay, d_y]), ("add", [a_stay, *a_zs])
    )
    w_y, d_zs, a_x = grid.swap(w_y, "y"), over_z(d_zs), grid.swap(a, "x")
    w_y, d_zs, a_x = ends((w_y, d_zs, a_x))

    (*w_zs, w_stay), d, a = mix(("z", [w_stay, w_y]), ("add", [d_stay, *d_zs]), ("pair", [a, a_x], "x"))
    w_zs, d_x, a_c, y0 = over_z(w_zs), grid.swap(d, "x"), grid.swap(a, "c"), grid.swap(other0, "y")
    w_zs, d_x, a_c, y0 = ends((w_zs, d_x, a_c, y0))

    each2, tall2 = 2 * each, 2 * tall
    own, own_hidden = (width // nblk,), (hidden // nblk,)
    places_up = [*range(0, (blocks - 1) * each, each), (blocks - 1) * each + each + 16 + low]
    first_c = (blocks - 1) * each
    a_out = [(0, row, each, 0, (j * half, (j + blocks) * half), 0, each) for j, row in enumerate(places_up)]
    a_out += [(0, first_c, each, 1, (0, half), 0, each), (0, first_c + each, 16, 2, (0, half), 0, 16)]
    a_shapes = [(each2, hidden), (each2, width), (32, width), own, own, own, own, own_hidden]
    a_small = [(3, 0, 2), (4, 1, 2), (5, 2, 2), (6, 3, 2), (7, 4, 2)]
    w, d = mix(("add", [w_stay, *w_zs]), ("pair", [d, d_x], "x"))
    w_x, d_c = grid.swap(w, "x"), grid.swap(d, "c")
    ((total_up, total_out, _, b_out, gain_two, bias_two, b_down, b_up),) = mix(("out", [a, a_c], (a_out, a_shapes, a_small)))
    (grad_patches,) = call(
        end_kernel, "finish", [struct((rows, width), F32)], [patches, gain, grad_mid, own0, z3, z2, z1, y0], rows * width,
    )
    w_x, d_c, grad_patches, total_up = ends((w_x, d_c, grad_patches, total_up))

    (w,) = mix(("pair", [w, w_x], "x"))
    w_c = grid.swap(w, "c")
    d_out = [(0, first_c + each + 16, low, 0, (0, half), 0, tall), (1, 0, tall - low, 0, (0, half), low, tall)]
    last_out = [(0, j * each, each, 0, (j * width, j * width + half), 0, each) for j in range(3)]
    last_out.append((0, 3 * each, 16, 1, (0, half), 0, 16))
    total_down, (total_qkv, _, gain_one, bias_one) = mix(
        ("out", [a, a_c, d, d_c], (d_out, [(tall2, width)])),
        ("out", [w, w_c], (last_out, [(each2, 3 * width), (32, width), own, own], [(2, 0, 1), (3, 1, 1)])),
    )
    small = (gain_one, bias_one, b_out, gain_two, bias_two, b_down, b_up)
    return grad_patches, total_qkv, total_out, total_up, total_down, small


def local(
    grid,
    patches,
    segment_ids,
    sensor_tags,
    seq_starts,
    ln1_gain,
    ln1_bias,
    w_qkv,
    w_out,
    b_out,
    ln2_gain,
    ln2_bias,
    w_up,
    b_up,
    w_down,
    b_down,
    cotangent,
):
    grid.locate()
    nblk, nz, nx = grid.nblk, grid.n["z"], grid.n["x"]
    loop = nz > 4
    rows, width = patches.shape
    me = lax.axis_index("blk")
    where_ = (segment_ids, sensor_tags, seq_starts)
    norm_one = (ln1_gain, ln1_bias)


    def place(k, other):
        def chunk():
            blk = lax.axis_index("blk")
            return blk ^ (k * 2 + other)

        return chunk

    units = []
    for u in range(nz + 1):
        parts = ([(u - 1, 1)] if u > 0 else []) + ([(u, 0)] if u < nz else [])
        units.append(parts)
    places = [[place(*p) for p in parts] for parts in units]

    state, queries = None, None
    normed, chunks, tokens = {}, {}, []
    held = {(0, 0): patches}
    for k in range(1, nz):
        held[k, 0] = grid.swap(patches, "z", k)
    for u in range(nz + 1):
        got = grid.swap(held[u, 0], "y") if u < nz else None
        tokens.append([held[p] for p in units[u]])
        outs = fwd_call(places[u], u == 0, u == nz, loop, where_, norm_one, w_qkv, tokens[u], queries, state)
        if u < nz:
            after = held[u + 1, 0] if u < nz - 1 else ()
            got, after, outs = lax.optimization_barrier((got, after, outs))
            held[u, 1] = got
            if u < nz - 1:
                held[u + 1, 0] = after
        state = outs[:3]
        n = len(units[u])
        for i, part in enumerate(units[u]):
            normed[part] = outs[3 + i]
            chunks[part] = (places[u][i], outs[3 + n + i], tokens[u][i])
        if u == 0:
            queries = outs[-3]
            where_ = (outs[-2], outs[-1], seq_starts)
    log_total, _, attn_t = state

    near = (w_qkv, queries, *where_, log_total)
    mixed_out, left, right, right_given, grad_mid, grad_attn, delta, sums = mid_call(
        near, attn_t, patches, cotangent, w_out, b_out, ln2_gain, ln2_bias, w_up, b_up, w_down, b_down
    )
    half = width // 2
    hidden = w_down.shape[0]
    blocks = hidden // width
    pieces = nblk * nx
    each = width // pieces
    hidden_each = hidden // pieces
    normed = [normed[k, other] for k in range(nz) for other in (1, 0)]
    parts_of = (chunks, where_, queries, grad_attn, log_total, delta)
    if nz == 4 and nx == 2 and each % 16 == 0:
        summed = reduce_packed(
            grid, near, parts_of, w_qkv, left, right, right_given, sums, normed, patches, ln1_gain, grad_mid, blocks, each, hidden_each
        )
    else:
        summed = reduce_plain(
            grid, loop, parts_of, w_qkv, left, right, sums, normed, patches, ln1_gain, grad_mid, blocks, each, hidden_each
        )
    grad_patches, total_qkv, total_out, total_up, total_down, small = summed
    gain_one, bias_one, total_bout, gain_two, bias_two, total_bdown, total_bup = small
    return (
        mixed_out,
        grad_patches,
        gain_one,
        bias_one,
        total_qkv,
        total_out,
        total_bout,
        gain_two,
        bias_two,
        total_up,
        total_bup,
        total_down,
        total_bdown,
    )


def solution(mesh):
    in_specs = (
        P(("dp", "blk"), None),
        P("dp"),
        P("dp"),
        P(("dp", "blk")),
        *(P(),) * 11,
        P(("dp", "blk"), None),
    )
    out_specs = (
        P(("dp", "blk"), None),
        P(("dp", "blk"), None),
        P("blk"),
        P("blk"),
        P("blk", None),
        P("blk", None),
        P("blk"),
        P("blk"),
        P("blk"),
        P("blk", None),
        P("blk"),
        P("blk", None),
        P("blk"),
    )
    return jax.shard_map(
        partial(local, Grid(mesh)), mesh=mesh, in_specs=in_specs, out_specs=out_specs, check_vma=False
    )
```

```python
import functools
from functools import partial

import jax
import jax.numpy as jnp
from jax import lax
from jax.experimental import pallas as pl
from jax.experimental.pallas import tpu as pltpu
from jax.sharding import PartitionSpec as P

HEADS = 12
EPSILON = 1e-06
MASKED = -1e30
AXES = ("dp", "blk")
NT = (((1,), (1,)), ((), ()))
TN = (((0,), (0,)), ((), ()))
NN = (((1,), (0,)), ((), ()))
VM = pl.BlockSpec(memory_space=pltpu.VMEM)
FAR = pl.BlockSpec(memory_space=pltpu.HBM)
LOW = jnp.bfloat16
F32 = jnp.float32
MIB = 1 << 20
BWD_MIB = 8
SECOND_MIB = 12


def dotf(a, b, dims=NN):
    return lax.dot_general(a, b, dims, preferred_element_type=F32)


def struct(shape, dtype):
    return jax.ShapeDtypeStruct(shape, dtype)


def norm_hat(x):
    center = x - jnp.mean(x, axis=-1, keepdims=True)
    inv = lax.rsqrt(jnp.mean(center * center, axis=-1, keepdims=True) + EPSILON)
    return center * inv, inv


def norm_back(hat, inv, gain, grad):
    g = grad * gain
    return inv * (g - jnp.mean(g, axis=-1, keepdims=True) - hat * jnp.mean(g * hat, axis=-1, keepdims=True))


def call(kernel, name, outs, args, flops, aliases=None, scratch=(), exps=0, vmem=8, far=(), far_outs=()):
    moved = sum(a.size * a.dtype.itemsize for a in args) + sum(o.size * o.dtype.itemsize for o in outs)
    return pl.pallas_call(
        kernel,
        out_shape=[pltpu.HBM(o.shape, o.dtype) if i in far_outs else o for i, o in enumerate(outs)],
        in_specs=[FAR if i in far else VM for i in range(len(args))],
        out_specs=[FAR if i in far_outs else VM for i in range(len(outs))],
        input_output_aliases=aliases or {},
        scratch_shapes=scratch,
        compiler_params=pltpu.CompilerParams(vmem_limit_bytes=vmem * MIB),
        cost_estimate=pl.CostEstimate(flops=int(flops) // 4, bytes_accessed=int(moved) // 4, transcendentals=0),
        name=name,
    )(*(pltpu.with_memory_space_constraint(a, pltpu.HBM) if i in far else a for i, a in enumerate(args)))


def line(ref):
    return ref[...].reshape(1, -1)


def key_bias(chunk, seg_ref, tag_ref, from_ref):
    keys = seg_ref.shape[1]
    me = lax.axis_index("blk")
    base = lax.axis_index("dp") * (seg_ref.shape[0] * keys)

    def column(ref):
        return jnp.broadcast_to(ref[pl.ds(chunk, 1), :], (8, keys)).T[:, 0:1]

    kseg, ktag = column(seg_ref), column(tag_ref)
    qseg, qtag = seg_ref[pl.ds(me, 1), :], tag_ref[pl.ds(me, 1), :]
    pos = base + chunk * keys + lax.broadcasted_iota(jnp.int32, (keys, keys), 0)
    seen = (kseg == qseg) & (pos >= line(from_ref))
    tags = (ktag == qtag) | (qtag == 0) | (ktag == 0)
    return jnp.where(seen & tags, 0.0, MASKED)


def head_lanes(block, odd):
    lane = lax.broadcasted_iota(jnp.int32, block.shape, 1)
    return jnp.where((lane >= 64) if odd else (lane < 64), block, jnp.zeros_like(block))


def over_pairs(heads, loop, body):
    if loop:
        lax.fori_loop(0, heads // 2, lambda i, c: (body(i), c)[1], 0)
    else:
        for i in range(heads // 2):
            body(i)


def fwd_kernel(places, first, last, loop, *refs):
    n = len(places)
    seg_ref, tag_ref, from_ref, gain_ref, shift_ref, w_ref = refs[:6]
    tokens = refs[6 : 6 + n]
    refs = refs[6 + n :]
    if first:
        far = (seg_ref, tag_ref, from_ref, gain_ref, shift_ref, w_ref)
        from_ref, gain_ref, shift_ref, w_ref, few_sems, row_sems = refs[-6:]
        seg_ref, tag_ref = refs[-12:-10]
        refs = refs[:-12] + refs[-10:-6]
        here = (from_ref, gain_ref, shift_ref, w_ref)
        few = [pltpu.make_async_copy(far[2 + i], here[i], few_sems.at[i]) for i in range(4)]
        row_count, row_size = seg_ref.shape
        by_rows = []
        for i in range(2):
            for j in range(row_count):
                some = pl.ds(j * row_size, row_size)
                by_rows.append(pltpu.make_async_copy(far[i].at[some], (seg_ref, tag_ref)[i].at[j], row_sems.at[i, j]))
        few[3].start()
        for copy in (*few[:3], *by_rows):
            copy.start()
        for copy in (*few[:3], *by_rows):
            copy.wait()
    if not first:
        q_ref, top_in, sum_in, acc_in = refs[:4]
        refs = refs[4:]
    top_out, sum_out, acc_out = refs[:3]
    normed_far, kv_far = refs[3 : 3 + n], refs[3 + n : 3 + 2 * n]
    if first:
        q_ref = refs[3 + 2 * n]
    bias, normed_out, kv_out, sems = refs[-4:]
    keys, width = tokens[0].shape
    for i in range(n):
        at = pl.ds(i * keys, keys)
        hat = norm_hat(tokens[i][...].astype(F32))[0]
        normed = (hat * line(gain_ref) + line(shift_ref)).astype(LOW)
        normed_out[at, :] = normed
        bias[i] = key_bias(places[i](), seg_ref, tag_ref, from_ref)
    kept = []
    for i in range(n):
        kept.append(pltpu.make_async_copy(normed_out.at[pl.ds(i * keys, keys), :], normed_far[i], sems.at[0, i]))
        kept[-1].start()
    normed = normed_out[...]
    if first:
        few[3].wait()
        q_ref[...] = (dotf(normed, w_ref[:, :width]).astype(LOW) * jnp.asarray(0.125, LOW)).astype(LOW)
    for j in range(2):
        cols = pl.ds(j * width, width)
        kv_out[:, cols] = dotf(normed, w_ref[:, pl.ds((j + 1) * width, width)]).astype(LOW)
    for i in range(n):
        kept.append(pltpu.make_async_copy(kv_out.at[pl.ds(i * keys, keys), :], kv_far[i], sems.at[1, i]))
        kept[-1].start()

    def pair_body(pair):
        lanes = pl.multiple_of(pair * 128, 128)
        at, vat = pl.ds(lanes, 128), pl.ds(width + lanes, 128)
        q_pair = q_ref[:, at]
        v_t = [kv_out[pl.ds(i * keys, keys), vat].T for i in range(n)]
        for odd in range(2):
            h = pair * 2 + odd
            row = pl.ds(h, 1)
            rows = pl.ds(pl.multiple_of(h * 64, 64), 64)
            q_h = head_lanes(q_pair, odd)
            scores = [dotf(kv_out[pl.ds(i * keys, keys), at], q_h, NT) + bias[i] for i in range(n)]
            top = jnp.max(scores[0], axis=0, keepdims=True)
            for s in scores[1:]:
                top = jnp.maximum(top, jnp.max(s, axis=0, keepdims=True))
            if not first:
                old = top_in[row, :]
                top = jnp.maximum(top, old)
                fade = jnp.exp(old - top)
            total = None
            out = None
            for i in range(n):
                p = jnp.exp(scores[i] - top)
                t = jnp.sum(p, axis=0, keepdims=True)
                o = dotf(v_t[i][odd * 64 : odd * 64 + 64], p.astype(LOW))
                total = t if total is None else total + t
                out = o if out is None else out + o
            if not first:
                total = total + sum_in[row, :] * fade
                out = out + acc_in[rows, :] * fade
            if last:
                out = out / total
                top = top + jnp.log(total)
            acc_out[rows, :] = out
            top_out[row, :] = top
            sum_out[row, :] = total

    over_pairs(HEADS, loop, pair_body)
    for copy in kept:
        copy.wait()


def fwd_call(places, first, last, loop, where_, norm, w_qkv, tokens, queries, state):
    keys, width = tokens[0].shape
    n = len(tokens)
    outs = [
        struct((HEADS, keys), F32),
        struct((HEADS, keys), F32),
        struct((width, keys), F32),
        *(struct((keys, width), LOW) for _ in range(n)),
        *(struct((keys, 2 * width), LOW) for _ in range(n)),
    ]
    args = [*where_, *norm, w_qkv, *tokens]
    scratch = [
        pltpu.VMEM((n, keys, keys), F32),
        pltpu.VMEM((n * keys, width), LOW),
        pltpu.VMEM((n * keys, 2 * width), LOW),
        pltpu.SemaphoreType.DMA((2, n)),
    ]
    if first:
        count = where_[0].shape[0] // keys
        outs += [struct((keys, width), LOW)] + [struct((count, keys), jnp.int32)] * 2
        scratch += [pltpu.VMEM(v.shape, v.dtype) for v in (where_[2], *norm, w_qkv)]
        scratch += [pltpu.SemaphoreType.DMA((4,)), pltpu.SemaphoreType.DMA((2, count))]
    else:
        args += [queries, *state]
    return call(
        partial(fwd_kernel, places, first, last, loop),
        "attend",
        outs,
        args,
        n * (HEADS * keys * keys * 256 * 8 + keys * width * width * 4),
        aliases={} if first else {len(args) - 3 + i: i for i in range(3)},
        scratch=scratch,
        far=range(6) if first else (),
        vmem=16 if first else 8,
        far_outs=tuple(range(3, 3 + 2 * n)),
        exps=n * HEADS * keys * keys,
    )


def bwd_kernel(places, first, last, loop, *refs):
    n = len(places)
    seg_ref, tag_ref, from_ref, w_ref, q_ref, do_ref, lse_ref, delta_ref = refs[:8]
    kvs, tokens = refs[8 : 8 + 2 * n], refs[8 + 2 * n : 8 + 4 * n]
    refs = refs[8 + 4 * n :]
    if not first:
        dq_in, sums_in = refs[:2]
        refs = refs[2:]
    dq_out, sums_out = refs[:2]
    dkvs, dn = refs[2 : 2 + n], refs[2 + n : 2 + 3 * n]
    if last:
        gq_out = refs[2 + 3 * n]
    bias = refs[-1]
    keys, width = tokens[0].shape
    for i in range(n):
        for j in range(2):
            bias[j] = key_bias(places[i][j](), seg_ref, tag_ref, from_ref)
        kv, dkv = kvs[2 * i : 2 * i + 2], dkvs[i]

        def pair_body(pair, fresh=first and i == 0, dq_from=dq_in if not first and i == 0 else dq_out):
            lanes = pl.multiple_of(pair * 128, 128)
            at, vat = pl.ds(lanes, 128), pl.ds(width + lanes, 128)
            q_pair = q_ref[:, at]
            do_pair = do_ref[:, at]
            chunk = [pl.ds(j * keys, keys) for j in range(2)]
            k_t = [kv[j][:, at].T for j in range(2)]
            dk = [None] * 2
            dv = [None] * 2
            for odd in range(2):
                h = pair * 2 + odd
                row = pl.ds(h, 1)
                rows = pl.ds(pl.multiple_of(h * 64, 64), 64)
                q_h = head_lanes(q_pair, odd)
                do_h = head_lanes(do_pair, odd)
                lse = lse_ref[row, :]
                delta = delta_ref[row, :]
                dq = None
                for j in range(2):
                    p = jnp.exp(dotf(kv[j][:, at], q_h, NT) + bias[j] - lse)
                    dp = dotf(kv[j][:, vat], do_h, NT)
                    ds = (p * (dp - delta)).astype(LOW)
                    v_part = dotf(p.astype(LOW), do_h)
                    k_part = dotf(ds, q_h)
                    q_part = dotf(k_t[j][odd * 64 : odd * 64 + 64], ds)
                    dv[j] = v_part if odd == 0 else dv[j] + v_part
                    dk[j] = k_part if odd == 0 else dk[j] + k_part
                    dq = q_part if dq is None else dq + q_part
                if not fresh:
                    dq = dq + dq_from[rows, :]
                dq_out[rows, :] = dq
            for j in range(2):
                dkv[chunk[j], at] = dk[j].astype(LOW)
                dkv[chunk[j], vat] = dv[j].astype(LOW)

        over_pairs(HEADS, loop, pair_body)
        gain_sum = bias_sum = 0.0
        ending = last and i == n - 1
        if ending:
            grad_query = (dq_out[...].T * 0.125).astype(LOW)
            gq_out[...] = grad_query
        for j in range(2):
            part = dotf(dkv[pl.ds(j * keys, keys), :], w_ref[:, width:], NT)
            if ending and j == 1:
                part = part + dotf(grad_query, w_ref[:, :width], NT)
            dn[2 * i + j][...] = part.astype(LOW)
            hat = norm_hat(tokens[2 * i + j][...].astype(F32))[0]
            gain_sum = gain_sum + jnp.sum(part * hat, axis=0, keepdims=True)
            bias_sum = bias_sum + jnp.sum(part, axis=0, keepdims=True)
        if i == 0:
            sums_out[...] = jnp.zeros_like(sums_out) if first else sums_in[...]
        sums_out[0:1, :] += gain_sum
        sums_out[1:2, :] += bias_sum


def bwd_give_kernel(places, pieces, count, left_count, more, *refs):
    outs = refs[count + more : -2]
    bwd_kernel(places, False, True, False, *refs[:count], *outs, refs[-1])
    normed, dkv = refs[count : count + left_count], refs[count + left_count : count + more]
    second_part(pieces, 1 - lax.axis_index("dp") % 2, normed, (outs[2], *dkv), outs[-1], outs[1], refs[-2])


def bwd_call(slots, first, last, loop, chunks, where_, w_qkv, queries, grad_attn, log_total, delta, carried, give=None):
    rows, width = queries.shape
    n = len(slots)
    each = [[chunks[k, other] for other in (1, 0)] for k in slots]
    outs = [struct((width, rows), F32), struct((8, width), F32)]
    outs += [struct((2 * rows, 2 * width), LOW) for _ in slots]
    outs += [struct((rows, width), LOW) for _ in range(2 * n)]
    if last:
        outs.append(struct((rows, width), LOW))
    args = [*where_, w_qkv, queries, grad_attn, log_total, delta]
    args += [c[1] for pair in each for c in pair] + [c[2] for pair in each for c in pair] + list(carried)
    places = [[c[0] for c in pair] for pair in each]
    aliases = {} if first else {len(args) - 2: 0, len(args) - 1: 1}
    kernel = partial(bwd_kernel, places, first, last, loop)
    if give:
        pieces, normed, dkv = give
        kernel = partial(bwd_give_kernel, places, pieces, len(args), len(normed), len(normed) + len(dkv))
        args += [*normed, *dkv]
        outs.append(struct((2, pieces // 2, 3 * width // pieces + 16, width // 2), LOW))
    return call(
        kernel,
        "attend_back",
        outs,
        args,
        n * 2 * (HEADS * rows * rows * 256 * 14 + rows * width * width * 4),
        aliases=aliases,
        scratch=[pltpu.VMEM((2, rows, rows), F32)],
        vmem=SECOND_MIB if give else BWD_MIB,
    )


def mid_kernel(
    attn_ref, x_ref, dy_ref, wo_ref, bo_ref, g2_ref, s2_ref, wu_ref, bu_ref, wd_ref, bd_ref, *refs
):
    mixed_ref, left_ref, right_ref, given_ref, mid_ref, do_ref, delta_ref, sums_ref = refs[-8:]
    rows, width = x_ref.shape
    hidden = wu_ref.shape[1]
    half, blocks = width // 2, hidden // width
    attn_low = attn_ref[...].T.astype(LOW)
    left_ref[:, pl.ds(hidden + width, width)] = attn_low
    x_mid = x_ref[...].astype(F32) + dotf(attn_low, wo_ref[...]) + line(bo_ref)
    hat, inv = norm_hat(x_mid)
    gain = line(g2_ref)
    normed = (hat * gain + line(s2_ref)).astype(LOW)
    left_ref[:, pl.ds(hidden, width)] = normed
    dy = dy_ref[...]
    dy_full = dy.astype(F32)
    down = None
    grad_normed = None
    for j in range(blocks):
        cols = pl.ds(j * width, width)
        pre = dotf(normed, wu_ref[:, cols]) + bu_ref[cols].reshape(1, -1)
        cdf = 0.5 + 0.5 * lax.erf(pre * (0.5**0.5))
        slope = cdf + pre * (jnp.exp(-0.5 * pre * pre) * 0.3989422804014327)
        act = (pre * cdf).astype(LOW)
        left_ref[:, cols] = act
        part = dotf(act, wd_ref[cols, :])
        down = part if down is None else down + part
        grad_pre = (dotf(dy, wd_ref[cols, :], NT) * slope).astype(LOW)
        right_ref[j * 2 // blocks, :, pl.ds(j % (blocks // 2) * width, width)] = grad_pre
        part = dotf(grad_pre, wu_ref[:, cols], NT)
        grad_normed = part if grad_normed is None else grad_normed + part
        sums_ref[4 + j : 5 + j, :] = jnp.sum(grad_pre.astype(F32), axis=0, keepdims=True)
    mixed_ref[...] = (x_mid + down + line(bd_ref)).astype(LOW)
    grad_mid = dy_full + norm_back(hat, inv, gain, grad_normed)
    mid_ref[...] = grad_mid
    branch = grad_mid.astype(LOW)
    for c in range(2):
        right_ref[c, :, pl.ds(hidden // 2, half)] = branch[:, c * half : (c + 1) * half]
        right_ref[c, :, pl.ds(hidden // 2 + half, half)] = dy[:, c * half : (c + 1) * half]
    given_ref[...] = right_ref[1 - lax.axis_index("dp") % 2]
    grad_attn = dotf(branch, wo_ref[...], NT).astype(LOW)
    do_ref[...] = grad_attn
    product = grad_attn.astype(F32).T * attn_ref[...]
    size = width // HEADS
    for h in range(HEADS):
        delta_ref[h : h + 1, :] = jnp.sum(product[h * size : (h + 1) * size, :], axis=0, keepdims=True)
    sums_ref[0:1, :] = jnp.sum(branch.astype(F32), axis=0, keepdims=True)
    sums_ref[1:2, :] = jnp.sum(grad_normed * hat, axis=0, keepdims=True)
    sums_ref[2:3, :] = jnp.sum(grad_normed, axis=0, keepdims=True)
    sums_ref[3:4, :] = jnp.sum(dy_full, axis=0, keepdims=True)


def mid_call(near, attn_t, patches, cotangent, w_out, b_out, g2, s2, w_up, b_up, w_down, b_down):
    rows, width = patches.shape
    hidden = w_up.shape[1]
    outs = [
        struct((rows, width), LOW),
        struct((rows, hidden + 2 * width), LOW),
        struct((2, rows, hidden // 2 + width), LOW),
        struct((rows, hidden // 2 + width), LOW),
        struct((rows, width), F32),
        struct((rows, width), LOW),
        struct((HEADS, rows), F32),
        struct((4 + hidden // width, width), F32),
    ]
    args = [attn_t, patches, cotangent, w_out, b_out, g2, s2, w_up, b_up, w_down, b_down, *near]
    return call(mid_kernel, "middle", outs, args, rows * width * (hidden * 8 + width * 4), exps=rows * hidden * 4, vmem=16)


def halves_of_x(acc, pieces, half):
    acc = acc.reshape(pieces // 2, 2, -1, half)
    first = lax.axis_index("dp") // 2 == 0
    own = jnp.where(first, acc[:, 0], acc[:, 1]).astype(LOW)
    other = jnp.where(first, acc[:, 1], acc[:, 0]).astype(LOW)
    return other, own


def first_kernel(jobs, sums_to, pieces, left_ref, right_ref, left_got, right_got, sums_ref, sums_got, *refs):
    c = lax.axis_index("dp") % 2
    parts = 1 + max(target[0] for job in jobs for target in job[-1])
    outs = refs[-2 * parts :]
    half = outs[0].shape[2]
    width = 2 * half
    for left, total, right, targets in jobs:
        cols = pl.ds(right, half)
        each = total * 2 // (2 * pieces)
        for begin in range(0, total, width):
            rows = pl.ds(left + begin, width)
            acc = dotf(left_ref[:, rows], right_ref[c, :, cols], TN) + dotf(left_got[:, rows], right_got[:, cols], TN)
            pair = halves_of_x(acc, width // each, half)
            blks = width // each // 2
            at = pl.ds(begin // each // 2, blks)
            for part, low, high, row in targets:
                for side in range(2):
                    outs[part + side * parts][at, pl.ds(row, high - low), :] = pair[side][:, low:high, :]
    mine = sums_ref[:, pl.ds(pl.multiple_of(c * half, 128), half)] + sums_got[:, pl.ds(pl.multiple_of(c * half, 128), half)]
    mine = jnp.concatenate([mine, jnp.zeros_like(mine)], axis=0).astype(LOW)
    part, row = sums_to
    for side in range(2):
        out = outs[part + side * parts]
        out[:, pl.ds(row, 16), :] = jnp.broadcast_to(mine[None], (out.shape[0],) + mine.shape)


def first_call(near, jobs, sums_to, heights, pieces, half, left, right, left_got, right_got, sums, sums_got):
    outs = [struct((pieces // 2, h, half), LOW) for h in heights] * 2
    args = [left, right, left_got, right_got, sums, sums_got, *near]
    return call(
        partial(first_kernel, jobs, sums_to, pieces), "weights", outs, args, sum(h for h in heights) * pieces * half * 1024, vmem=12
    )


def second_part(pieces, c, normed, dkv, gq_ref, sums_ref, out):
    keys, width = normed[0].shape
    half = width // 2
    each = width // pieces
    for block in range(3):
        if block == 0:
            cols = pl.ds(pl.multiple_of(c * half, 128), half)
            acc = dotf(normed[1][...], gq_ref[:, cols], TN)
        else:
            cols = pl.ds(pl.multiple_of((block - 1) * width + c * half, 128), half)
            acc = None
            for i in range(len(normed)):
                term = dotf(normed[i][...], dkv[i // 2][pl.ds(i % 2 * keys, keys), cols], TN)
                acc = term if acc is None else acc + term
        pair = halves_of_x(acc, pieces, half)
        for side in range(2):
            out[side, :, pl.ds(block * each, each), :] = pair[side]
    mine = sums_ref[:, pl.ds(pl.multiple_of(c * half, 128), half)]
    mine = jnp.concatenate([mine, jnp.zeros_like(mine)], axis=0).astype(LOW)
    for side in range(2):
        out[side, :, pl.ds(3 * each, 16), :] = jnp.broadcast_to(mine[None], (out.shape[1],) + mine.shape)


def keep_kernel(pieces, units, *refs):
    normed, dkv = refs[2 : 2 + 2 * units], refs[2 + 2 * units : 2 + 3 * units]
    second_part(pieces, lax.axis_index("dp") % 2, normed, dkv, *refs[:2], refs[-1])


def keep_call(pieces, half, grad_query, sums, normed, dkv):
    each = 2 * half // pieces
    args = [grad_query, sums, *normed, *dkv]
    (out,) = call(
        partial(keep_kernel, pieces, len(dkv)),
        "weights",
        [struct((2, pieces // 2, 3 * each + 16, half), LOW)],
        args,
        sum(v.shape[0] for v in normed) * 2 * half * 4 * half,
        vmem=SECOND_MIB,
    )
    return out


def weight_kernel(spec, sums_at, pieces, far, count, *refs):
    me = lax.axis_index("dp") % 2
    ins = list(refs[:count])
    outs = refs[count : len(refs) - len(far) - (1 if far else 0)]
    waits = {}
    if far:
        sems = refs[-1]
        for i, number in enumerate(far):
            held = refs[len(refs) - 1 - len(far) + i]
            waits[number] = pltpu.make_async_copy(ins[number], held, sems.at[i])
            waits[number].start()
            ins[number] = held
    parts = len(outs) // 2
    for part, row, lefts, rights, starts in spec:
        for number in (*lefts, *rights):
            if number in waits:
                waits.pop(number).wait()
        for given in (True, False):
            c = 1 - me if given else me
            out = outs[part + (0 if given else parts)]
            half = out.shape[2]
            total = ins[lefts[0]].shape[1]
            each = total // pieces
            step = min(total, 768)
            cols = pl.ds(pl.multiple_of(jnp.where(c == 0, starts[0], starts[1]), 128), half)
            for begin in range(0, total, step):
                acc = None
                for left, right in zip(lefts, rights):
                    term = dotf(ins[left][:, pl.ds(begin, step)], ins[right][:, cols], TN)
                    acc = term if acc is None else acc + term
                acc = acc.reshape(step // each, each, half)
                out[pl.ds(begin // each, step // each), pl.ds(row, each), :] = acc.astype(LOW)
    if sums_at is not None:
        part, row, number = sums_at
        for given in (True, False):
            c = 1 - me if given else me
            out = outs[part + (0 if given else parts)]
            half = out.shape[2]
            mine = ins[number][:, pl.ds(pl.multiple_of(c * half, 128), half)]
            mine = jnp.concatenate([mine, jnp.zeros_like(mine)], axis=0).astype(LOW)
            out[:, pl.ds(row, 16), :] = jnp.broadcast_to(mine[None], (pieces,) + mine.shape)


def weight_call(pieces, heights, half, jobs, sums=None, sums_at=None, far=()):
    spec, args, flops = [], [], 0

    def index(array):
        for i, known in enumerate(args):
            if known is array:
                return i
        args.append(array)
        return len(args) - 1

    for part, row, lefts, rights, starts in jobs:
        spec.append((part, row, [index(v) for v in lefts], [index(v) for v in rights], starts))
        flops += sum(a.shape[0] for a in lefts) * lefts[0].shape[1] * half * 4
    if sums is not None:
        sums_at = (*sums_at, index(sums))
    far = tuple(i for i, a in enumerate(args) if any(a is v for v in far))
    scratch = [pltpu.VMEM(args[i].shape, args[i].dtype) for i in far]
    if far:
        scratch.append(pltpu.SemaphoreType.DMA((len(far),)))
    outs = [struct((pieces, h, half), LOW) for h in heights] * 2
    return call(
        partial(weight_kernel, spec, sums_at, pieces, far, len(args)),
        "weights",
        outs,
        args,
        flops,
        scratch=scratch,
        far=far,
        vmem=8 + sum(args[i].size * 2 for i in far) // MIB,
    )


def mix_kernel(ops, *refs):
    dp, blk = lax.axis_index("dp"), lax.axis_index("blk")
    at = {"x": dp // 2, "c": dp % 2, "z": blk // 2, "y": blk % 2}
    for kind, ins, outs, more in ops:
        terms = [refs[i] if lead is None else refs[i].at[lead] for i, lead in ins]
        if kind == "cut":
            whole = total_of([t[...] for t in terms])
            outs_here = [refs[i] for i in outs]
            outs_here[0][...] = whole[:, :more, :].astype(LOW)
            outs_here[1][...] = whole[:, more:, :]
            continue
        outs = [refs[i] for i in outs]
        if kind == "add":
            outs[0][...] = total_of([t[...] for t in terms]).astype(LOW)
        elif kind == "y":
            size, row = len(terms) // (more or 1), 0
            for begin in range(0, len(terms), size):
                group = terms[begin : begin + size]
                some = pl.ds(row, group[0].shape[1])
                row += group[0].shape[1]
                for q in range(outs[0].shape[0]):
                    outs[0][q, some, :] = total_of([t[2 * q + 1 - at["y"]] for t in group]).astype(LOW)
                    outs[1][q, some, :] = total_of([t[2 * q + at["y"]] for t in group])
        elif kind == "z":
            size, row = len(terms) // (more or 1), 0
            for begin in range(0, len(terms), size):
                group = terms[begin : begin + size]
                some = pl.ds(row, group[0].shape[1])
                row += group[0].shape[1]
                for k in range(1, group[0].shape[0]):
                    outs[k - 1][some, :] = total_of([t[at["z"] ^ k] for t in group]).astype(LOW)
                outs[-1][some, :] = total_of([t[at["z"]] for t in group])
        elif kind == "pair":
            outs[0][at[more]] = terms[0][...]
            outs[0][1 - at[more]] = terms[1][...]
        else:
            for source, row, height, number, starts, offset, stride in more[0]:
                some = pl.ds(row, height)
                own, got = terms[2 * source : 2 * source + 2]
                for x in range(own.shape[0]):
                    mine, other = own[x, some, :].astype(F32), got[x, some, :].astype(F32)
                    first = at["c"] == 0
                    to = pl.ds(x * stride + offset, height)
                    width = mine.shape[1]
                    outs[number][to, pl.ds(starts[0], width)] = jnp.where(first, mine, other)
                    outs[number][to, pl.ds(starts[1], width)] = jnp.where(first, other, mine)
            for number, row, source in more[2] if len(more) > 2 else ():
                size = outs[number].shape[0]
                if size % 128:
                    values = pltpu.roll(outs[source][row : row + 1, :], outs[source].shape[1] - blk * size, 1)
                    outs[number][...] = values[:, :size].reshape(size)
                else:
                    each = outs[source].shape[1] // size
                    values = outs[source][pl.ds(row + blk // each, 1), pl.ds(pl.multiple_of(blk % each * size, 128), size)]
                    outs[number][...] = values.reshape(size)


def mix(*ops):
    args, outs, spec, counts = [], [], [], []

    def index(array):
        for i, known in enumerate(args):
            if known is array:
                return i
        args.append(array)
        return len(args) - 1

    for kind, terms, *more in ops:
        ins = [(index(t[0]), t[1]) if isinstance(t, tuple) else (index(t), None) for t in terms]
        shape = args[ins[0][0]].shape
        shape = shape if ins[0][1] is None else shape[1:]
        if kind == "add":
            new = [struct(shape, LOW)]
        elif kind == "y":
            groups = more[0] if more else 1
            firsts = [ins[i * (len(ins) // groups)] for i in range(groups)]
            height = sum(args[i].shape[-2] for i, _ in firsts)
            shape = (shape[0] // 2, height, shape[2])
            new = [struct(shape, LOW), struct(shape, F32)]
        elif kind == "z":
            groups = more[0] if more else 1
            height = sum(args[ins[i * (len(ins) // groups)][0]].shape[-2] for i in range(groups))
            new = [struct((height, shape[2]), LOW)] * (shape[0] - 1) + [struct((height, shape[2]), F32)]
        elif kind == "cut":
            new = [struct((shape[0], more[0], shape[2]), LOW), struct((shape[0], shape[1] - more[0], shape[2]), F32)]
        elif kind == "pair":
            new = [struct((2, *shape), LOW)]
        else:
            new = [struct(v, F32) for v in more[0][1]]
        spec.append((kind, ins, range(len(outs), len(outs) + len(new)), more[0] if more else None))
        counts.append(len(new))
        outs += new
    spec = [(kind, ins, [len(args) + i for i in out], more) for kind, ins, out, more in spec]
    made = call(partial(mix_kernel, spec), "mix", outs, args, sum(o.size for o in outs), vmem=8)
    split = []
    for n in counts:
        split.append(made[0] if n == 1 else tuple(made[:n]))
        made = made[n:]
    return split


def end_kernel(x_ref, gain_ref, mid_ref, *refs):
    out = refs[-1]
    grad = refs[0][...].astype(F32)
    for ref in refs[1:-1]:
        grad = grad + ref[...].astype(F32)
    hat, inv = norm_hat(x_ref[...].astype(F32))
    out[...] = mid_ref[...] + norm_back(hat, inv, line(gain_ref), grad)


class Grid:
    def __init__(self, mesh):
        ndp, nblk = mesh.shape["dp"], mesh.shape["blk"]
        self.n = {"c": 2, "x": ndp // 2, "y": 2, "z": nblk // 2}
        self.nblk, self.ndp = nblk, ndp

    def locate(self):
        dp, blk = lax.axis_index("dp"), lax.axis_index("blk")
        self.at = {"x": dp // 2, "c": dp % 2, "z": blk // 2, "y": blk % 2}

    def swap(self, value, axis, k=1):
        pairs = []
        n = self.n
        for x in range(n["x"]):
            for c in range(2):
                for z in range(n["z"]):
                    for y in range(2):
                        here = {"x": x, "c": c, "z": z, "y": y}
                        there = dict(here)
                        there[axis] ^= k
                        flat = [((p["x"] * 2 + p["c"]) * n["z"] + p["z"]) * 2 + p["y"] for p in (here, there)]
                        pairs.append(tuple(flat))
        return lax.ppermute(value, AXES, pairs)

    def all_sum(self, value, axis):
        step = 1
        while step < self.n[axis]:
            value = value + self.swap(value, axis, step)
            step *= 2
        return value

    def scatter(self, array, axis, dim):
        piece = lambda k: lax.dynamic_index_in_dim(array, self.at[axis] ^ k, dim, keepdims=False)
        got = []
        if self.n[axis] > 1:
            got = yield [self.swap(piece(k), axis, k) for k in range(1, self.n[axis])]
        return [piece(0), *got]

    def gather(self, value, axis):
        n = self.n[axis]
        if n == 1:
            return [value]
        got = yield [self.swap(value, axis, k) for k in range(1, n)]
        slots = [value, *got]
        at = self.at[axis]
        out = []
        for p in range(n):
            piece = slots[p]
            for i in range(1, n):
                piece = jnp.where(at == i, slots[p ^ i], piece)
            out.append(piece)
        return out


class Flow:
    def __init__(self, steps):
        self.steps, self.result = steps, None
        self.advance(None, True)

    def advance(self, value, first=False):
        try:
            self.pending = next(self.steps) if first else self.steps.send(value)
        except StopIteration as stop:
            self.pending, self.result = None, stop.value


def tie(flows, *values):
    flows = [f for f in flows if f.pending is not None]
    pending, values = lax.optimization_barrier(([f.pending for f in flows], values))
    for flow, value in zip(flows, pending):
        flow.advance(value)
    return values


def total_of(terms):
    return functools.reduce(lambda a, b: a + b, [t.astype(F32) for t in terms])


def reduce_plain(grid, loop, parts_of, w_qkv, left, right, sums, normed, patches, gain, grad_mid, blocks, each, hidden_each):
    chunks, where_, queries, grad_attn, log_total, delta = parts_of
    nz, nx = grid.n["z"], grid.n["x"]
    rows, width = patches.shape
    half, hidden, pieces = width // 2, blocks * width, grid.nblk * nx
    act_low, normed_two, attn_low = left[:, :hidden], left[:, hidden : hidden + width], left[:, hidden + width :]
    grad_pre, grad_branch, dy = (
        jnp.concatenate([right[c, :, a:b] for c in range(2)], axis=1)
        for a, b in ((0, hidden // 2), (hidden // 2, hidden // 2 + half), (hidden // 2 + half, hidden // 2 + width))
    )

    def reduce_rows(given, kept):
        got = yield grid.swap(given, "c")
        part = (kept.astype(F32) + got.astype(F32)).astype(LOW).reshape(nz, 2, nx, -1, kept.shape[-1])
        for axis, dim in (("x", 2), ("y", 1), ("z", 0)):
            terms = yield from grid.scatter(part, axis, dim)
            part = total_of(terms).astype(LOW)
        over_x = yield from grid.gather(part, "x")
        over_c = yield from grid.gather(jnp.stack(over_x), "c")
        return over_c

    def reduce_small(part):
        for axis in "cxyz":
            part = grid.all_sum(part, axis)
        return part

    def reduce_all(heights, jobs, far=()):
        made = weight_call(pieces, heights, half, jobs, far=far)
        count = len(heights)
        flows = [Flow(reduce_rows(*v)) for v in zip(made[:count], made[count:])]
        while any(f.pending is not None for f in flows):
            for f in flows:
                if f.pending is not None:
                    f.advance(f.pending)
        return [[v.reshape(-1, half) for v in f.result] for f in flows]

    def join(blocks_):
        return jnp.concatenate([b[c] for c in range(2) for b in blocks_], axis=1).astype(F32)

    jobs = [(0, 0, [act_low], [dy], (0, half)), (1, 0, [attn_low], [grad_branch], (0, half))]
    jobs += [(2 + j, 0, [normed_two], [grad_pre], (j * half, (j + blocks) * half)) for j in range(blocks)]
    first = reduce_all([hidden_each] + [each] * (1 + blocks), jobs)
    total_down, total_out, total_up = join(first[:1]), join(first[1:2]), join(first[2:])
    sums = reduce_small(sums)

    carried = ()
    dkv, home = [None] * nz, []
    for k in reversed(range(nz)):
        outs = bwd_call([k], k == nz - 1, k == 0, loop, chunks, where_, w_qkv, queries, grad_attn, log_total, delta, carried)
        carried, dkv[k] = outs[:2], outs[2]
        other, own, grad_query = outs[3], outs[4], outs[-1]
        got = grid.swap(other, "y")
        home.append(grid.swap((own.astype(F32) + got.astype(F32)).astype(LOW), "z", k) if k else got)
    (grad_patches,) = call(
        end_kernel, "finish", [struct((rows, width), F32)], [patches, gain, grad_mid, own, *home], rows * width, vmem=40
    )
    own_first = normed[1]
    lefts = [jnp.concatenate(normed[2 * k : 2 * k + 2], axis=0) for k in range(nz)]
    jobs = [(0, 0, [own_first], [grad_query], (0, half)), (1, 0, lefts, dkv, (0, half)), (2, 0, lefts, dkv, (width, width + half))]
    second = reduce_all([each] * 3, jobs, far=(own_first, *lefts, *dkv))
    total_qkv = jnp.concatenate([t[c] for t in second for c in range(2)], axis=1).astype(F32)
    late, me = reduce_small(carried[1]), lax.axis_index("blk")

    def own_part(v):
        size = v.size // grid.nblk
        return lax.dynamic_slice_in_dim(v.reshape(-1), me * size, size)

    small = [own_part(v) for v in (late[0], late[1], sums[0], sums[1], sums[2], sums[3], sums[4:])]
    return grad_patches, total_qkv, total_out, total_up, total_down, small


def reduce_packed(
    grid, near, parts_of, w_qkv, left, right, right_given, sums, normed, patches, gain, grad_mid, blocks, each, hidden_each
):
    chunks, where_, queries, grad_attn, log_total, delta = parts_of
    nz, nblk = grid.n["z"], grid.nblk
    rows, width = patches.shape
    half, hidden, pieces = width // 2, blocks * width, nblk * 2
    ends = lax.optimization_barrier
    over_z = lambda sends: [grid.swap(v, "z", len(sends) - k) for k, v in enumerate(reversed(sends))][::-1]
    tall = hidden_each
    low = tall // 3
    heights = [(blocks - 1) * each, each + 16 + low, tall - low, each]
    jobs = [(hidden, width, (blocks - 1) * half, ((3, 0, each, 0),))]
    jobs += [(hidden, width, j * half, ((0, 0, each, j * each),)) for j in range(blocks - 1)]
    jobs.append((hidden + width, width, blocks * half, ((1, 0, each, 0),)))
    jobs.append((0, hidden, (blocks + 1) * half, ((1, 0, low, each + 16), (2, low, tall, 0))))
    sums_to = (1, each)

    def unit(slots, carried, give=None):
        return bwd_call(
            slots, not carried, 0 in slots, False, chunks, where_, w_qkv, queries, grad_attn, log_total, delta, carried, give
        )

    passed = [grid.swap(v, "c") for v in (left, right_given, sums)]
    dkv = [None] * nz
    outs, passed = ends((unit([3], ()), passed))
    carried, dkv[3], other3, own3 = outs[:2], *outs[2:]
    y3 = grid.swap(other3, "y")
    made = first_call(near, jobs, sums_to, heights, pieces, half, left, right, passed[0], passed[1], sums, passed[2])
    made, carried = ends((made, carried))
    ((e_y, e_stay),) = mix(("y", [made[3], made[7]], 2))
    a_x, e_y = grid.swap(made[0], "x"), grid.swap(e_y, "y")

    outs, y3, a_x, e_y, *sent = ends((unit([2, 1], carried), y3, a_x, e_y, made[1], made[2]))
    carried, dkv[2], dkv[1], other2, own2, other1, own1 = outs[:2], *outs[2:]
    z3, (e_x, e_stay) = mix(("add", [own3, y3]), ("cut", [e_stay, e_y], each))
    c_x, z3, y2, y1 = grid.swap(sent[0], "x"), grid.swap(z3, "z", 3), grid.swap(other2, "y"), grid.swap(other1, "y")
    e_x = grid.swap(e_x, "x")

    outs, y2, y1, c_x, z3, e_x, sent = ends(
        (unit([0], carried, (pieces, normed, dkv[1:])), y2, y1, c_x, z3, e_x, sent[1])
    )
    carried, dkv[0], other0, own0, grad_query, give = outs[:2], *outs[2:]
    z2, z1, (a_y, a_stay) = mix(("add", [own2, y2]), ("add", [own1, y1]), ("y", [made[4], a_x, made[5], c_x], 2))
    d_x, z2, z1, a_y = grid.swap(sent, "x"), grid.swap(z2, "z", 2), grid.swap(z1, "z", 1), grid.swap(a_y, "y")
    w_got = grid.swap(give, "c")
    keep = keep_call(pieces, half, grad_query, carried[1], normed, dkv)
    w_got, keep, d_x, a_y, z2, z1 = ends((w_got, keep, d_x, a_y, z2, z1))

    w_x, (*a_zs, a_stay), (d_y, d_stay) = mix(
        ("add", [(keep, 0), (w_got, 0)]), ("z", [a_stay, a_y, e_stay, e_x], 2), ("y", [made[6], d_x])
    )
    w_x, d_y, a_zs = grid.swap(w_x, "x"), grid.swap(d_y, "y"), over_z(a_zs)
    w_x, d_y, a_zs = ends((w_x, d_y, a_zs))

    (w_y, w_stay), (*d_zs, d_stay), a = mix(
        ("y", [(keep, 1), (w_got, 1), w_x]), ("z", [d_stay, d_y]), ("add", [a_stay, *a_zs])
    )
    w_y, d_zs, a_x = grid.swap(w_y, "y"), over_z(d_zs), grid.swap(a, "x")
    w_y, d_zs, a_x = ends((w_y, d_zs, a_x))

    (*w_zs, w_stay), d, a = mix(("z", [w_stay, w_y]), ("add", [d_stay, *d_zs]), ("pair", [a, a_x], "x"))
    w_zs, d_x, a_c, y0 = over_z(w_zs), grid.swap(d, "x"), grid.swap(a, "c"), grid.swap(other0, "y")
    w_zs, d_x, a_c, y0 = ends((w_zs, d_x, a_c, y0))

    each2, tall2 = 2 * each, 2 * tall
    own, own_hidden = (width // nblk,), (hidden // nblk,)
    places_up = [*range(0, (blocks - 1) * each, each), (blocks - 1) * each + each + 16 + low]
    first_c = (blocks - 1) * each
    a_out = [(0, row, each, 0, (j * half, (j + blocks) * half), 0, each) for j, row in enumerate(places_up)]
    a_out += [(0, first_c, each, 1, (0, half), 0, each), (0, first_c + each, 16, 2, (0, half), 0, 16)]
    a_shapes = [(each2, hidden), (each2, width), (32, width), own, own, own, own, own_hidden]
    a_small = [(3, 0, 2), (4, 1, 2), (5, 2, 2), (6, 3, 2), (7, 4, 2)]
    w, d = mix(("add", [w_stay, *w_zs]), ("pair", [d, d_x], "x"))
    w_x, d_c = grid.swap(w, "x"), grid.swap(d, "c")
    ((total_up, total_out, _, b_out, gain_two, bias_two, b_down, b_up),) = mix(("out", [a, a_c], (a_out, a_shapes, a_small)))
    (grad_patches,) = call(
        end_kernel, "finish", [struct((rows, width), F32)], [patches, gain, grad_mid, own0, z3, z2, z1, y0], rows * width,
    )
    w_x, d_c, grad_patches, total_up = ends((w_x, d_c, grad_patches, total_up))

    (w,) = mix(("pair", [w, w_x], "x"))
    w_c = grid.swap(w, "c")
    d_out = [(0, first_c + each + 16, low, 0, (0, half), 0, tall), (1, 0, tall - low, 0, (0, half), low, tall)]
    last_out = [(0, j * each, each, 0, (j * width, j * width + half), 0, each) for j in range(3)]
    last_out.append((0, 3 * each, 16, 1, (0, half), 0, 16))
    (total_down,) = mix(("out", [a, a_c, d, d_c], (d_out, [(tall2, width)])))
    w_c, total_down = ends((w_c, total_down))
    ((total_qkv, _, gain_one, bias_one),) = mix(
        ("out", [w, w_c], (last_out, [(each2, 3 * width), (32, width), own, own], [(2, 0, 1), (3, 1, 1)]))
    )
    small = (gain_one, bias_one, b_out, gain_two, bias_two, b_down, b_up)
    return grad_patches, total_qkv, total_out, total_up, total_down, small


def local(
    grid,
    patches,
    segment_ids,
    sensor_tags,
    seq_starts,
    ln1_gain,
    ln1_bias,
    w_qkv,
    w_out,
    b_out,
    ln2_gain,
    ln2_bias,
    w_up,
    b_up,
    w_down,
    b_down,
    cotangent,
):
    grid.locate()
    nblk, nz, nx = grid.nblk, grid.n["z"], grid.n["x"]
    loop = nz > 4
    rows, width = patches.shape
    me = lax.axis_index("blk")
    where_ = (segment_ids, sensor_tags, seq_starts)
    norm_one = (ln1_gain, ln1_bias)


    def place(k, other):
        def chunk():
            blk = lax.axis_index("blk")
            return blk ^ (k * 2 + other)

        return chunk

    units = []
    for u in range(nz + 1):
        parts = ([(u - 1, 1)] if u > 0 else []) + ([(u, 0)] if u < nz else [])
        units.append(parts)
    places = [[place(*p) for p in parts] for parts in units]

    state, queries = None, None
    normed, chunks, tokens = {}, {}, []
    held = {(0, 0): patches}
    for k in range(1, nz):
        held[k, 0] = grid.swap(patches, "z", k)
    for u in range(nz + 1):
        got = grid.swap(held[u, 0], "y") if u < nz else None
        tokens.append([held[p] for p in units[u]])
        outs = fwd_call(places[u], u == 0, u == nz, loop, where_, norm_one, w_qkv, tokens[u], queries, state)
        if u < nz:
            after = held[u + 1, 0] if u < nz - 1 else ()
            got, after, outs = lax.optimization_barrier((got, after, outs))
            held[u, 1] = got
            if u < nz - 1:
                held[u + 1, 0] = after
        state = outs[:3]
        n = len(units[u])
        for i, part in enumerate(units[u]):
            normed[part] = outs[3 + i]
            chunks[part] = (places[u][i], outs[3 + n + i], tokens[u][i])
        if u == 0:
            queries = outs[-3]
            where_ = (outs[-2], outs[-1], seq_starts)
    log_total, _, attn_t = state

    near = (w_qkv, queries, *where_, log_total)
    mixed_out, left, right, right_given, grad_mid, grad_attn, delta, sums = mid_call(
        near, attn_t, patches, cotangent, w_out, b_out, ln2_gain, ln2_bias, w_up, b_up, w_down, b_down
    )
    half = width // 2
    hidden = w_down.shape[0]
    blocks = hidden // width
    pieces = nblk * nx
    each = width // pieces
    hidden_each = hidden // pieces
    normed = [normed[k, other] for k in range(nz) for other in (1, 0)]
    parts_of = (chunks, where_, queries, grad_attn, log_total, delta)
    if nz == 4 and nx == 2 and each % 16 == 0:
        summed = reduce_packed(
            grid, near, parts_of, w_qkv, left, right, right_given, sums, normed, patches, ln1_gain, grad_mid, blocks, each, hidden_each
        )
    else:
        summed = reduce_plain(
            grid, loop, parts_of, w_qkv, left, right, sums, normed, patches, ln1_gain, grad_mid, blocks, each, hidden_each
        )
    grad_patches, total_qkv, total_out, total_up, total_down, small = summed
    gain_one, bias_one, total_bout, gain_two, bias_two, total_bdown, total_bup = small
    return (
        mixed_out,
        grad_patches,
        gain_one,
        bias_one,
        total_qkv,
        total_out,
        total_bout,
        gain_two,
        bias_two,
        total_up,
        total_bup,
        total_down,
        total_bdown,
    )


def solution(mesh):
    in_specs = (
        P(("dp", "blk"), None),
        P("dp"),
        P("dp"),
        P(("dp", "blk")),
        *(P(),) * 11,
        P(("dp", "blk"), None),
    )
    out_specs = (
        P(("dp", "blk"), None),
        P(("dp", "blk"), None),
        P("blk"),
        P("blk"),
        P("blk", None),
        P("blk", None),
        P("blk"),
        P("blk"),
        P("blk"),
        P("blk", None),
        P("blk"),
        P("blk", None),
        P("blk"),
    )
    return jax.shard_map(
        partial(local, Grid(mesh)), mesh=mesh, in_specs=in_specs, out_specs=out_specs, check_vma=False
    )
```
